32 devices in a mesh: seq: 8 (over y, x, core), head: 4 (over z).
Axes of the slice: x: 2, y: 2, z: 4, core: 2. Of those that a mesh axis runs over, the one named last changes fastest.
Arguments:
- queries: bfloat16 [4096, 4096], P(('seq', 'head')), may hold values from -80 to 80
- keys: bfloat16 [4096, 512], P(('seq', 'head')), may hold values from -4 to 4
- values: bfloat16 [4096, 512], P(('seq', 'head')), may hold values from -6 to 6
- output_gradient: bfloat16 [4096, 4096], P(('seq', 'head')), may hold values from -0.59765625 to 0.59765625
- inputs: bfloat16 [4096, 8192], P(('seq', 'head')), may hold values from -6 to 6
- adapter_activation: bfloat16 [4096, 16], P(('seq', 'head')), may hold values from -6 to 6
- adapter_up_weight: bfloat16 [8, 16, 4096], P('seq', None, 'head'), may hold values from -0.09375 to 0.09375
- segment_length: int32 [8, 8], P('seq'), may hold values from 1 to 192, 512 in all within a row
- segment_adapter: int32 [8, 8], P('seq'), may hold values from 0 to 7
- owner: int32 [8], replicated, may hold values from 0 to 7, each once
Outputs:
- down_gradient: float32 [8, 8192, 16], P('seq', 'head')
- up_gradient: float32 [8, 16, 4096], P('seq', None, 'head')
The draws below stay inside these ranges and needn't reach their ends.
Inputs may be any that keep to these rules, and one draw needn't show every extreme that they name: `segment_length`: each pack's 8 lengths sum to 512, and its longest segment has exactly 192 tokens. `owner`: each seq index owns exactly one adapter.
All inputs are finite; a program needn't handle non-finite values.
Results may differ from the reference program's by a relative error of at most 0.014.
Values may be sent and summed in bfloat16 or wider, within the bound.
No kernel may reach another device: no remote copies, remote signals or barrier semaphores. Data moves between devices by JAX's collectives and lax.ppermute only.
A program may use at most 64 MiB of HBM per device.

```python
import math
import jax
import jax.numpy as jnp
import numpy as np
from jax import lax

D = 8192
QUERY_HEADS = 32
KEY_VALUE_HEADS = 4
HEAD_SIZE = 128
ADAPTER_RANK = 16
PACK_SEGMENTS = 8
PACK_TOKENS = 512
MOST = 192
ADAPTER_COUNT = 8
TOKEN_TOTAL = 4096
N_SEQ = 8


def key_base(key):
    return jnp.clip(jax.random.normal(key, (TOKEN_TOTAL, KEY_VALUE_HEADS * HEAD_SIZE), jnp.float32), -4.0, 4.0)


def draw_keys(key, part):
    common_rows = key_base(key)
    return common_rows.astype(jnp.bfloat16)


def draw_queries(key, part):
    key = jax.random.fold_in(key, 13)
    fresh_rows = jnp.clip(jax.random.normal(key, (TOKEN_TOTAL, QUERY_HEADS, HEAD_SIZE), jnp.float32), -4.0, 4.0)
    return fresh_rows.reshape(TOKEN_TOTAL, QUERY_HEADS * HEAD_SIZE).astype(jnp.bfloat16)


def with_ends(array, key, least, high):
    spot = [jax.random.randint(jax.random.fold_in(key, axis), (), 0, length) for axis, length in enumerate(array.shape)]
    longest = array.shape.index(max(array.shape))
    neighbour = spot[:longest] + [(spot[longest] + 1) % array.shape[longest]] + spot[longest + 1:]
    return array.at[tuple(spot)].set(least).at[tuple(neighbour)].set(high)


def level_of(stream_key, extent, cuts, smallest, high):
    loudness, own = 1.0, jax.random.fold_in(stream_key, 6)
    for axis_at, shards_of in cuts:
        draws = jnp.exp(jax.random.uniform(jax.random.fold_in(own, axis_at), (shards_of,), jnp.float32, smallest / len(cuts), high / len(cuts)))
        loudness = loudness * jnp.repeat(draws, extent[axis_at] // shards_of).reshape([-1 if axis == axis_at else 1 for axis in range(len(extent))])
    return loudness


def split_up(amount, total, most, skew):
    portions = [(1 << 20) // math.isqrt(rank ** skew) + 1 for rank in range(2, amount + 1)]
    surplus, counts = total - most - (amount - 1), [1] * (amount - 1)
    while surplus > 0:
        free = [i for i in range(amount - 1) if counts[i] < most]
        pool, budget = sum([portions[i] for i in free]), surplus
        for i in free:
            extra = min(most - counts[i], max(1, budget * portions[i] // pool), surplus)
            counts[i] = counts[i] + extra
            surplus = surplus - extra
    return np.array([most] + counts)


def uneven_parts(rng, count, total, bound, skew):
    if count == 2:
        one = jax.random.randint(rng, (), max(1, total - bound), min(bound, total - 1) + 1)
        return jnp.stack([one, total - one])
    lengths = jnp.asarray(split_up(count, total, bound, skew), jnp.int32)
    pairs = (count - 1) // 2
    source_of, taker = lengths[1:1 + 2 * pairs:2], lengths[2:2 + 2 * pairs:2]
    room = jnp.minimum(source_of - 1, bound - taker)
    moved = jax.random.randint(jax.random.fold_in(rng, 1), (pairs,), 0, 1 << 20) % (room + 1)
    lengths = lengths.at[1:1 + 2 * pairs:2].set(source_of - moved).at[2:2 + 2 * pairs:2].set(taker + moved)
    return lengths[jax.random.permutation(jax.random.fold_in(rng, 2), count)]


def bell_draw(stream_key, dims, width, most, cuts=(), held_as=jnp.bfloat16):
    entries = width * jax.random.normal(stream_key, dims, jnp.float32)
    if cuts:
        entries = entries * level_of(stream_key, dims, cuts, -0.22, 0.18)
    return jnp.clip(entries, -most, most).astype(held_as)


def setup_inputs(seed: int = 0) -> dict:
    seeds = jax.random.split(jax.random.key(seed), 11)
    return {
        "queries": draw_queries(jax.random.fold_in(seeds[10], 71), 0),
        "keys": draw_keys(jax.random.fold_in(seeds[10], 71), 0),
        "values": bell_draw(seeds[2], (TOKEN_TOTAL, KEY_VALUE_HEADS * HEAD_SIZE), 1.0, 6.0, ((0, 32),)),
        "output_gradient": bell_draw(seeds[3], (TOKEN_TOTAL, QUERY_HEADS * HEAD_SIZE), 0.1, 0.59765625, ((0, 32),)),
        "inputs": bell_draw(seeds[4], (TOKEN_TOTAL, D), 1.0, 6.0, ((0, 32),)),
        "adapter_activation": bell_draw(seeds[5], (TOKEN_TOTAL, ADAPTER_RANK), 1.0, 6.0, ((0, 32),)),
        "adapter_up_weight": bell_draw(seeds[6], (ADAPTER_COUNT, ADAPTER_RANK, QUERY_HEADS * HEAD_SIZE), (QUERY_HEADS * HEAD_SIZE) ** -0.5, 0.09375, ((0, 8), (2, 4))),
        "segment_length": jax.vmap(lambda own: uneven_parts(own, PACK_SEGMENTS, PACK_TOKENS, MOST, 2))(jax.random.split(seeds[7], N_SEQ)).reshape((N_SEQ, PACK_SEGMENTS)).astype(jnp.int32),
        "segment_adapter": with_ends(jax.random.randint(seeds[8], (N_SEQ, PACK_SEGMENTS), 0, ADAPTER_COUNT), jax.random.fold_in(seeds[8], 1), 0, ADAPTER_COUNT - 1).astype(jnp.int32),
        "owner": jax.random.permutation(seeds[9], ADAPTER_COUNT).astype(jnp.int32),
    }


ADAPTER_SCALE = 2.0
HIGHEST = lax.Precision.HIGHEST


def segment_of(seg_lens, pack_len):
    seg_ends = jnp.cumsum(seg_lens)
    positions = jnp.arange(pack_len, dtype=jnp.int32)
    return jnp.sum((positions[:, None] >= seg_ends[None, :]).astype(jnp.int32), axis=1)


def head_backward(q_head, g_head, k_head, v_head, segment):
    pack_len, head_width = q_head.shape
    score_scale = 1.0 / (head_width ** 0.5)
    positions = jnp.arange(pack_len, dtype=jnp.int32)
    k_wide = k_head.astype(jnp.float32)
    scores = jnp.dot(q_head.astype(jnp.float32), k_wide.T, preferred_element_type=jnp.float32) * score_scale
    allowed = (segment[:, None] == segment[None, :]) & (positions[None, :] <= positions[:, None])
    scores = jnp.where(allowed, scores, -jnp.inf)
    row_max = jnp.max(scores, axis=1, keepdims=True)
    weights = jnp.exp(scores - row_max)
    attn_prob = weights / jnp.sum(weights, axis=1, keepdims=True)
    d_prob = jnp.dot(g_head.astype(jnp.float32), v_head.astype(jnp.float32).T, preferred_element_type=jnp.float32)
    row_delta = jnp.sum(attn_prob * d_prob, axis=1, keepdims=True)
    dscore = (attn_prob * (d_prob - row_delta) * score_scale).astype(jnp.bfloat16)
    return jnp.dot(dscore.astype(jnp.float32), k_wide, preferred_element_type=jnp.float32).astype(jnp.bfloat16)


def reference(queries, keys, values, output_gradient, inputs, adapter_activation, adapter_up_weight, segment_length, segment_adapter, owner):
    query_group_width = QUERY_HEADS // KEY_VALUE_HEADS
    query_width = QUERY_HEADS * HEAD_SIZE

    def one_pack(totals, pack_index):
        down_running_sum, up_running_sum = totals
        starting_row = pack_index * PACK_TOKENS
        q_rows = lax.dynamic_slice_in_dim(queries, starting_row, PACK_TOKENS, 0).reshape(PACK_TOKENS, QUERY_HEADS, HEAD_SIZE).transpose(1, 0, 2)
        g_rows = lax.dynamic_slice_in_dim(output_gradient, starting_row, PACK_TOKENS, 0).reshape(PACK_TOKENS, QUERY_HEADS, HEAD_SIZE).transpose(1, 0, 2)
        key_rows = lax.dynamic_slice_in_dim(keys, starting_row, PACK_TOKENS, 0).reshape(PACK_TOKENS, KEY_VALUE_HEADS, HEAD_SIZE).transpose(1, 0, 2)
        value_rows = lax.dynamic_slice_in_dim(values, starting_row, PACK_TOKENS, 0).reshape(PACK_TOKENS, KEY_VALUE_HEADS, HEAD_SIZE).transpose(1, 0, 2)
        x_rows = lax.dynamic_slice_in_dim(inputs, starting_row, PACK_TOKENS, 0)
        activation_rows = lax.dynamic_slice_in_dim(adapter_activation, starting_row, PACK_TOKENS, 0)
        key_rows = jnp.repeat(key_rows, query_group_width, axis=0)
        value_rows = jnp.repeat(value_rows, query_group_width, axis=0)
        segment = segment_of(segment_length[pack_index], PACK_TOKENS)
        segment_index = segment_adapter[pack_index]
        dq_stack = lax.map(lambda stacked: head_backward(stacked[0], stacked[1], stacked[2], stacked[3], segment),
                           (q_rows, g_rows, key_rows, value_rows))
        dquery = dq_stack.transpose(1, 0, 2).reshape(PACK_TOKENS, query_width)
        up_weight_segment = adapter_up_weight[segment_index].reshape(PACK_SEGMENTS * ADAPTER_RANK, query_width)
        rank_seg = jnp.dot(dquery.astype(jnp.float32), up_weight_segment.astype(jnp.float32).T, preferred_element_type=jnp.float32)
        seg_mask = segment[:, None] == jnp.arange(PACK_SEGMENTS, dtype=jnp.int32)[None, :]
        rank_grad = jnp.sum(rank_seg.reshape(PACK_TOKENS, PACK_SEGMENTS, ADAPTER_RANK) * seg_mask[:, :, None], axis=1)
        rank_low = rank_grad.astype(jnp.bfloat16)
        mask_low = seg_mask.astype(jnp.bfloat16)
        rank_cols = (mask_low[:, :, None] * rank_low[:, None, :]).reshape(PACK_TOKENS, PACK_SEGMENTS * ADAPTER_RANK)
        act_cols = (mask_low[:, :, None] * activation_rows[:, None, :]).reshape(PACK_TOKENS, PACK_SEGMENTS * ADAPTER_RANK)
        part_a = jnp.dot(x_rows.astype(jnp.float32).T, rank_cols.astype(jnp.float32),
                         preferred_element_type=jnp.float32).reshape(D, PACK_SEGMENTS, ADAPTER_RANK)
        part_b = jnp.dot(act_cols.astype(jnp.float32).T, dquery.astype(jnp.float32),
                         preferred_element_type=jnp.float32).reshape(PACK_SEGMENTS, ADAPTER_RANK, query_width)
        onehot = (segment_index[:, None] == jnp.arange(ADAPTER_COUNT, dtype=jnp.int32)[None, :]).astype(jnp.float32)
        down_running_sum = down_running_sum + jnp.einsum("dsr,sa->adr", part_a, onehot, precision=HIGHEST)
        up_running_sum = up_running_sum + jnp.einsum("srf,sa->arf", part_b, onehot, precision=HIGHEST)
        return (down_running_sum, up_running_sum), None

    zeros_init = (jnp.zeros((ADAPTER_COUNT, D, ADAPTER_RANK), jnp.float32), jnp.zeros((ADAPTER_COUNT, ADAPTER_RANK, query_width), jnp.float32))
    (down_running_sum, up_running_sum), unused = lax.scan(one_pack, zeros_init, jnp.arange(N_SEQ, dtype=jnp.int32))
    down_gradient = jnp.zeros_like(down_running_sum).at[owner].set(down_running_sum) * ADAPTER_SCALE
    up_gradient = jnp.zeros_like(up_running_sum).at[owner].set(up_running_sum) * ADAPTER_SCALE
    return down_gradient, up_gradient
```

```python
import functools
import math

import jax
import jax.numpy as jnp
from jax import lax
from jax.experimental import pallas as pl
from jax.experimental.pallas import tpu as pltpu
from jax.sharding import PartitionSpec as P

QUERY_HEADS = 32
KEY_VALUE_HEADS = 4
HEAD_SIZE = 128
GROUP = QUERY_HEADS // KEY_VALUE_HEADS
ADAPTER_SCALE = 2.0
NEVER = -1e30
BF16 = jnp.bfloat16
F32 = jnp.float32
VMEM = pl.BlockSpec(memory_space=pltpu.VMEM)
SMEM = pl.BlockSpec(memory_space=pltpu.SMEM)


def dot(a, b, a_dim, b_dim):
    return lax.dot_general(a, b, (((a_dim,), (b_dim,)), ((), ())), preferred_element_type=F32)


def local_kernel(
    n_halo, by_slot, bits,
    place_ref, length_ref, adapter_ref, owner_ref,
    q_ref, g_ref, k_ref, v_ref, *refs,
):
    halo_refs = refs[:n_halo]
    (w_ref, x_ref, act_ref, *out_refs) = refs[n_halo:-6]
    k_all, v_all, k_turned, bias, dq_turned, rank_all = refs[-6:]
    tok, width = q_ref.shape
    kv_width = k_ref.shape[1]
    n_quarters = w_ref.shape[0]
    rank = act_ref.shape[0]
    n_seg = length_ref.shape[1]
    key_rows = k_all.shape[0]
    seq, head = place_ref[0], place_ref[1]

    start = 0
    for halo_ref in halo_refs:
        rows = halo_ref.shape[0]
        k_all[start : start + rows, :] = halo_ref[:, :kv_width]
        v_all[start : start + rows, :] = halo_ref[:, kv_width:]
        start += rows
    k_all[start:, :] = k_ref[...]
    v_all[start:, :] = v_ref[...]
    k_turned[...] = k_all[...].T

    position = head * tok + lax.broadcasted_iota(jnp.int32, (1, tok), 1)
    seg_start = jnp.zeros((1, tok), jnp.int32)
    adapter = jnp.zeros((1, tok), jnp.int32)
    group = jnp.zeros((1, tok), jnp.int32)
    end = 0
    for s in range(n_seg):
        mine = adapter_ref[0, s]
        goes_to = owner_ref[mine] if by_slot else s
        inside = position >= end
        seg_start = jnp.where(inside, end, seg_start)
        adapter = jnp.where(inside, mine, adapter)
        group = jnp.where(inside, goes_to, group)
        end = end + length_ref[0, s]

    key_position = (
        head * tok - (key_rows - tok) + lax.broadcasted_iota(jnp.int32, (key_rows, tok), 0)
    )
    allowed = (key_position >= seg_start) & (key_position <= position)
    bias[...] = jnp.where(allowed, 0.0, NEVER)

    scale = 1.0 / HEAD_SIZE**0.5
    to_log2 = scale * math.log2(math.e)

    def one_group(kv, carry):
        at_kv = pl.ds(pl.multiple_of(kv * HEAD_SIZE, HEAD_SIZE), HEAD_SIZE)
        k_g = k_all[:, at_kv]
        v_g = v_all[:, at_kv]
        kt_g = k_turned[at_kv, :]
        for i in range(GROUP):
            first = pl.multiple_of((kv * GROUP + i) * HEAD_SIZE, HEAD_SIZE)
            at = pl.ds(first, HEAD_SIZE)
            s = dot(k_g, q_ref[:, at], 1, 1) * to_log2 + bias[...]
            d_prob = dot(v_g, g_ref[:, at], 1, 1)
            weights = jnp.exp2(s - jnp.max(s, axis=0, keepdims=True))
            total = jnp.sum(weights, axis=0, keepdims=True)
            inverse = 1.0 / total
            delta = jnp.sum(weights * d_prob, axis=0, keepdims=True) * inverse
            dscore = (weights * (d_prob - delta) * (inverse * scale)).astype(BF16)
            dq_turned[at, :] = dot(kt_g, dscore, 1, 0).astype(BF16)
        return carry

    lax.fori_loop(0, KEY_VALUE_HEADS, one_group, 0)

    part = width // n_quarters
    rank_all[...] = dot(w_ref[0], dq_turned[0:part, :], 1, 0)
    for i in range(1, n_quarters):
        rank_all[...] += dot(w_ref[i], dq_turned[i * part : (i + 1) * part, :], 1, 0)
    n_adapters = rank_all.shape[0] // rank
    rank_grad = jnp.zeros((rank, tok), F32)
    for a in range(n_adapters):
        rows = rank_all[a * rank : (a + 1) * rank, :]
        rank_grad = rank_grad + jnp.where(adapter == a, rows, 0.0)

    n_groups = 1 << bits
    row = lax.broadcasted_iota(jnp.int32, (n_groups * rank, tok), 0) // rank
    if by_slot:
        turned = jnp.zeros_like(row)
        for b in range(bits):
            turned = turned | (((row >> b) & 1) << (bits - 1 - b))
        row = turned ^ seq
    own = row == group
    rank_low = rank_grad.astype(BF16).astype(F32)
    rank_cols = jnp.where(own, jnp.concatenate([rank_low] * n_groups, axis=0), 0.0).astype(BF16)
    act = act_ref[...].astype(F32)
    act_cols = jnp.where(own, jnp.concatenate([act] * n_groups, axis=0), 0.0).astype(BF16)

    x_part = x_ref.shape[1] // n_quarters
    per = out_refs[0].shape[1]
    for j in range(n_quarters):
        quarter = lax.rem(head + j, n_quarters) if by_slot else j
        at = pl.ds(pl.multiple_of(quarter * x_part, x_part), x_part)
        down = dot(rank_cols, x_ref[:, at], 1, 0).astype(BF16)
        at = pl.ds(pl.multiple_of(quarter * part, part), part)
        up = dot(act_cols, dq_turned[at, :], 1, 1).astype(BF16)
        for o, out_ref in enumerate(out_refs):
            out_ref[j, :, :x_part] = down[o * per : (o + 1) * per, :]
            out_ref[j, :, x_part:] = up[o * per : (o + 1) * per, :]


def on_device(
    queries, keys, values, output_gradient, inputs, adapter_activation,
    adapter_up_weight, segment_length, segment_adapter, owner,
):
    n_head = lax.axis_size("head")
    n_seq = lax.axis_size("seq")
    tok, width = queries.shape
    pack = tok * n_head
    rank = adapter_up_weight.shape[1]
    n_adapters = owner.shape[0]
    n_seg = segment_length.shape[1]
    bits = (n_seg - 1).bit_length()
    by_slot = n_adapters == n_seq == 1 << bits

    need = pack * 3 // 8
    key_values = jnp.concatenate([keys, values], axis=1)
    halos = []
    hop = 1
    while need > 0:
        rows = min(need, tok)
        shift = [(i, i + hop) for i in range(n_head - hop)]
        halos.insert(0, lax.ppermute(key_values[tok - rows :], "head", shift))
        need -= rows
        hop += 1
    key_rows = tok + sum(h.shape[0] for h in halos)

    up_weight = lax.all_gather(adapter_up_weight, ("head", "seq"), axis=0, tiled=True)
    up_weight = up_weight.reshape(n_head, n_adapters * rank, width // n_head)

    place = jnp.stack([lax.axis_index("seq"), lax.axis_index("head")]).astype(jnp.int32)
    out_width = (inputs.shape[1] + width) // n_head
    n_out = 2 if by_slot else 1
    group_rows = (1 << bits) * rank
    outs = pl.pallas_call(
        functools.partial(local_kernel, len(halos), by_slot, bits),
        out_shape=[
            jax.ShapeDtypeStruct((n_head, group_rows // n_out, out_width), BF16)
        ] * n_out,
        in_specs=[SMEM] * 4 + [VMEM] * (7 + len(halos)),
        out_specs=[VMEM] * n_out,
        scratch_shapes=[
            pltpu.VMEM((key_rows, keys.shape[1]), BF16),
            pltpu.VMEM((key_rows, keys.shape[1]), BF16),
            pltpu.VMEM((keys.shape[1], key_rows), BF16),
            pltpu.VMEM((key_rows, tok), F32),
            pltpu.VMEM((width, tok), BF16),
            pltpu.VMEM((n_adapters * rank, tok), F32),
        ],
        compiler_params=pltpu.CompilerParams(vmem_limit_bytes=40 * 2**20),
        cost_estimate=pl.CostEstimate(
            flops=2 * tok * width * key_rows * 3, bytes_accessed=9 * 2**20, transcendentals=tok * key_rows * QUERY_HEADS
        ),
        name="local_gradients",
    )(
        place, segment_length, segment_adapter, owner, queries, output_gradient, keys, values,
        *halos, up_weight, inputs, adapter_activation.T,
    )
    reduce = sum_by_slot if by_slot else sum_by_segment
    total = reduce(outs, bits, segment_adapter, owner, rank) * ADAPTER_SCALE
    down_width = inputs.shape[1] // n_head
    return total[:, :down_width].T[None], total[:, down_width:][None]


def sum_by_slot(outs, bits, segment_adapter, owner, rank):
    n_seq, n_head = lax.axis_size("seq"), lax.axis_size("head")
    keep, send = outs
    for b in range(bits):
        got = lax.ppermute(send, "seq", [(i, i ^ (1 << b)) for i in range(n_seq)])
        both = keep.astype(F32) + got.astype(F32)
        half = both.shape[1] // 2
        if b < bits - 1:
            keep, send = both[:, :half].astype(BF16), both[:, half:].astype(BF16)
    total = both[0]
    for j in range(1, n_head):
        shift = [(i, (i + j) % n_head) for i in range(n_head)]
        total = total + lax.ppermute(both[j].astype(BF16), "head", shift).astype(F32)
    return total


def sum_by_segment(outs, bits, segment_adapter, owner, rank):
    pieces = lax.all_to_all(outs[0], "head", split_axis=0, concat_axis=0, tiled=True)
    part = jnp.sum(pieces.astype(F32), axis=0)
    n_seg, n_seq = segment_adapter.shape[1], lax.axis_size("seq")
    part = part.reshape(-1, rank, part.shape[1])[:n_seg]
    goes_to = owner[segment_adapter[0]]
    slots = (goes_to[:, None] == jnp.arange(n_seq, dtype=jnp.int32)[None, :]).astype(F32)
    spread = jnp.einsum("srw,so->orw", part, slots, precision=lax.Precision.HIGHEST)
    spread = lax.all_to_all(spread.astype(BF16), "seq", split_axis=0, concat_axis=0, tiled=True)
    return jnp.sum(spread.astype(F32), axis=0)


def solution(mesh):
    return jax.shard_map(
        on_device,
        mesh=mesh,
        in_specs=(
            P(("seq", "head"), None),
            P(("seq", "head"), None),
            P(("seq", "head"), None),
            P(("seq", "head"), None),
            P(("seq", "head"), None),
            P(("seq", "head"), None),
            P("seq", None, "head"),
            P("seq", None),
            P("seq", None),
            P(),
        ),
        out_specs=(P("seq", "head", None), P("seq", None, "head")),
        check_vma=False,
    )
```

```python
import functools
import math

import jax
import jax.numpy as jnp
from jax import lax
from jax.experimental import pallas as pl
from jax.experimental.pallas import tpu as pltpu
from jax.sharding import PartitionSpec as P

QUERY_HEADS = 32
KEY_VALUE_HEADS = 4
HEAD_SIZE = 128
GROUP = QUERY_HEADS // KEY_VALUE_HEADS
ADAPTER_SCALE = 2.0
NEVER = -1e30
BF16 = jnp.bfloat16
F32 = jnp.float32
I32 = jnp.int32
VMEM = pl.BlockSpec(memory_space=pltpu.VMEM)
SMEM = pl.BlockSpec(memory_space=pltpu.SMEM)
ANY = pl.BlockSpec(memory_space=pl.ANY)


def dot(a, b, a_dim, b_dim):
    return lax.dot_general(a, b, (((a_dim,), (b_dim,)), ((), ())), preferred_element_type=F32)


def of_tokens(position, length_ref, values_of):
    end = 0
    found = None
    for s in range(length_ref.shape[1]):
        new = values_of(s, end)
        if found is None:
            found = [jnp.zeros_like(position) + value for value in new]
        else:
            inside = position >= end
            found = [jnp.where(inside, value, old) for value, old in zip(new, found)]
        end = end + length_ref[0, s]
    return found


def group_rows(rows_of_group, n_groups, width, seq, by_slot):
    row = lax.broadcasted_iota(I32, (n_groups * rows_of_group, width), 0) // rows_of_group
    if by_slot:
        half = n_groups // 2
        row = jnp.where(row < half, row * 2, (row - half) * 2 + 1) ^ seq
    return row


def attention_kernel(
    n_halo, by_slot,
    place_ref, length_ref, adapter_ref, owner_ref,
    q_hbm, g_hbm, k_ref, v_ref, *refs,
):
    halo_refs = refs[:n_halo]
    act_ref, dq_turned, *out_refs = refs[n_halo:-7]
    q_ref, g_ref, q_sem, g_sem, k_all, v_all, k_turned = refs[-7:]
    tok, width = q_ref.shape
    kv_width = k_ref.shape[1]
    rank = act_ref.shape[0]
    n_seg = length_ref.shape[1]
    key_rows = v_all.shape[0]
    seq, head = place_ref[0], place_ref[1]
    per_kv = GROUP * HEAD_SIZE

    def fetch(kv):
        at = pl.ds(kv * per_kv, per_kv)
        return (
            pltpu.make_async_copy(q_hbm.at[:, at], q_ref.at[:, at], q_sem.at[kv]),
            pltpu.make_async_copy(g_hbm.at[:, at], g_ref.at[:, at], g_sem.at[kv]),
        )

    for kv in range(KEY_VALUE_HEADS):
        for copy in fetch(kv):
            copy.start()

    position = head * tok + lax.broadcasted_iota(I32, (1, tok), 1)
    seg_start, group = of_tokens(
        position,
        length_ref,
        lambda s, start: (start, owner_ref[adapter_ref[0, s]] if by_slot else s),
    )
    key_position = (
        head * tok - (key_rows - tok) + lax.broadcasted_iota(I32, (key_rows, tok), 0)
    )
    allowed = (key_position >= seg_start) & (key_position <= position)
    bias = jnp.where(allowed, 0.0, NEVER).astype(BF16)

    for kv in range(KEY_VALUE_HEADS):
        start = 0
        at = slice(kv * HEAD_SIZE, (kv + 1) * HEAD_SIZE)
        for halo_ref in halo_refs:
            rows = halo_ref.shape[0]
            k_all[kv, start : start + rows, :HEAD_SIZE] = halo_ref[:, at]
            v_all[start : start + rows, at] = halo_ref[:, kv_width + at.start : kv_width + at.stop]
            start += rows
        k_all[kv, start:, :HEAD_SIZE] = k_ref[:, at]
        v_all[start:, at] = v_ref[:, at]
        k_all[kv, :, HEAD_SIZE:] = bias
        k_turned[at, :] = k_all[kv, :, :HEAD_SIZE].T

    one = lax.broadcasted_iota(I32, (2 * tok, tok), 0) % tok
    pick = (one == lax.broadcasted_iota(I32, (2 * tok, tok), 1)).astype(F32).astype(BF16)
    scale = 1.0 / HEAD_SIZE**0.5
    to_log2 = scale * math.log2(math.e)

    def one_group(kv, carry):
        for copy in fetch(kv):
            copy.wait()
        at_kv = pl.ds(pl.multiple_of(kv * HEAD_SIZE, HEAD_SIZE), HEAD_SIZE)
        k_g = k_all[kv]
        v_g = v_all[:, at_kv]
        kt_g = k_turned[at_kv, :]
        for i in range(0, GROUP, 2):
            first = (kv * GROUP + i) * HEAD_SIZE
            at = [
                pl.ds(pl.multiple_of(first + n * HEAD_SIZE, HEAD_SIZE), HEAD_SIZE) for n in range(2)
            ]
            q_two = jnp.concatenate([q_ref[:, at[0]], q_ref[:, at[1]]], axis=0)
            g_two = jnp.concatenate([g_ref[:, at[0]], g_ref[:, at[1]]], axis=0)
            s = dot(k_g, jnp.concatenate([q_two, pick], axis=1), 1, 1)
            d_prob = dot(v_g, g_two, 1, 1)
            weights = jnp.exp2((s - jnp.max(s, axis=0, keepdims=True)) * to_log2)
            inverse = 1.0 / jnp.sum(weights, axis=0, keepdims=True)
            delta = jnp.sum(weights * d_prob, axis=0, keepdims=True) * inverse
            dscore = (weights * (d_prob - delta)).astype(BF16)
            dq = dot(kt_g, dscore, 1, 0) * (inverse * scale)
            dq_turned[at[0], :] = dq[:, :tok].astype(BF16)
            dq_turned[at[1], :] = dq[:, tok:].astype(BF16)
        return carry

    lax.fori_loop(0, KEY_VALUE_HEADS, one_group, 0)

    per, n_quarters, _, part = out_refs[0].shape
    n_groups = per * len(out_refs)
    own = group_rows(rank, n_groups, tok, seq, by_slot) == group
    act = jnp.concatenate([act_ref[...].astype(F32)] * n_groups, axis=0)
    act_cols = jnp.where(own, act, 0.0).astype(BF16)
    for j in range(n_quarters):
        quarter = lax.rem(head + j, n_quarters) if by_slot else j
        at = pl.ds(pl.multiple_of(quarter * part, part), part)
        up = dot(act_cols, dq_turned[at, :], 1, 1).astype(BF16)
        for n in range(n_groups):
            out_refs[n // per][n % per, j] = up[n * rank : (n + 1) * rank, :]


def rank_kernel(by_slot, place_ref, length_ref, adapter_ref, dq_ref, *refs):
    *w_refs, out_ref = refs
    tok = dq_ref.shape[1]
    seq, head = place_ref[0], place_ref[1]
    n_adapters, n_quarters, rank, part = w_refs[0].shape
    position = head * tok + lax.broadcasted_iota(I32, (1, tok), 1)
    (adapter,) = of_tokens(position, length_ref, lambda s, start: (adapter_ref[0, s],))
    total = jnp.zeros((rank, tok), F32)
    for c, w_ref in enumerate(w_refs):
        rows = None
        for j in range(n_quarters):
            quarter = lax.rem(head + n_quarters - j, n_quarters) if by_slot else j
            dq = dq_ref[pl.ds(pl.multiple_of(quarter * part, part), part), :]
            new = dot(w_ref[:, j].reshape(n_adapters * rank, part), dq, 1, 0)
            rows = new if rows is None else rows + new
        for m in range(n_adapters):
            a = (2 * m + c) ^ seq if by_slot else m
            total = total + jnp.where(adapter == a, rows[m * rank : (m + 1) * rank, :], 0.0)
    out_ref[...] = total.astype(BF16)


def down_kernel(by_slot, n_quarters, place_ref, length_ref, adapter_ref, owner_ref, x_ref, *refs):
    rank_refs = refs[:n_quarters]
    *out_refs, cols = refs[n_quarters:]
    rank, tok = rank_refs[0].shape
    seq, head = place_ref[0], place_ref[1]
    per = out_refs[0].shape[0]
    n_groups = per * len(out_refs)
    rows = group_rows(rank, n_groups, tok, seq, by_slot)
    for j, rank_ref in enumerate(rank_refs):
        source = lax.rem(head + n_quarters - j, n_quarters)
        position = source * tok + lax.broadcasted_iota(I32, (1, tok), 1)
        (group,) = of_tokens(
            position,
            length_ref,
            lambda s, start: (owner_ref[adapter_ref[0, s]] if by_slot else s,),
        )
        low = jnp.concatenate([rank_ref[...].astype(F32)] * n_groups, axis=0)
        at = pl.ds(pl.multiple_of(source * tok, tok), tok)
        cols[:, at] = jnp.where(rows == group, low, 0.0).astype(BF16)
    step = 512
    for start in range(0, x_ref.shape[1], step):
        at = slice(start, start + step)
        down = dot(cols[...], x_ref[:, at], 1, 0).astype(BF16)
        for n in range(n_groups):
            out_refs[n // per][n % per, :, at] = down[n * rank : (n + 1) * rank, :]


def shifted(x, n_head, j):
    return lax.ppermute(x, "head", [(i, (i + j) % n_head) for i in range(n_head)])


def partnered(x, n_seq, bits):
    return lax.ppermute(x, "seq", [(i, i ^ bits) for i in range(n_seq)])


def on_device(
    queries, keys, values, output_gradient, inputs, adapter_activation,
    adapter_up_weight, segment_length, segment_adapter, owner,
):
    n_head = lax.axis_size("head")
    n_seq = lax.axis_size("seq")
    tok, width = queries.shape
    pack = tok * n_head
    rank = adapter_up_weight.shape[1]
    n_adapters = owner.shape[0]
    n_seg = segment_length.shape[1]
    by_slot = n_adapters == n_seq == 8
    place = jnp.stack([lax.axis_index("seq"), lax.axis_index("head")]).astype(I32)

    need = pack * 3 // 8
    key_values = jnp.concatenate([keys, values], axis=1)
    halos = []
    hop = 1
    while need > 0:
        rows = min(need, tok)
        shift = [(i, i + hop) for i in range(n_head - hop)]
        halos.insert(0, lax.ppermute(key_values[tok - rows :], "head", shift))
        need -= rows
        hop += 1
    key_rows = tok + sum(h.shape[0] for h in halos)

    if by_slot:
        w = [adapter_up_weight] + [shifted(adapter_up_weight, n_head, j) for j in range(1, n_head)]
        w = jnp.concatenate(w, axis=0)[None]
        w = jnp.concatenate([w] + [partnered(w, n_seq, 2 * m) for m in range(1, n_seq // 2)], axis=0)
        up_weight = [w, partnered(w, n_seq, 1)]
    else:
        w = lax.all_gather(adapter_up_weight, "seq", axis=0, tiled=True)
        up_weight = [lax.all_gather(w, "head", axis=1, tiled=False)]

    x = inputs.reshape(tok, n_head, -1).transpose(1, 0, 2)
    x = lax.all_to_all(x, "head", split_axis=0, concat_axis=0, tiled=True)
    x = x.reshape(pack, -1)

    n_out = 2 if by_slot else 1
    n_groups = n_seq if by_slot else n_seg
    part = width // n_head
    params = pltpu.CompilerParams(vmem_limit_bytes=32 * 2**20)
    dq_turned, *up = pl.pallas_call(
        functools.partial(attention_kernel, len(halos), by_slot),
        out_shape=[jax.ShapeDtypeStruct((width, tok), BF16)]
        + [jax.ShapeDtypeStruct((n_groups // n_out, n_head, rank, part), BF16)] * n_out,
        in_specs=[SMEM] * 4 + [ANY] * 2 + [VMEM] * (3 + len(halos)),
        out_specs=[VMEM] * (1 + n_out),
        scratch_shapes=[
            pltpu.VMEM((tok, width), BF16),
            pltpu.VMEM((tok, width), BF16),
            pltpu.SemaphoreType.DMA((KEY_VALUE_HEADS,)),
            pltpu.SemaphoreType.DMA((KEY_VALUE_HEADS,)),
            pltpu.VMEM((KEY_VALUE_HEADS, key_rows, 2 * HEAD_SIZE), BF16),
            pltpu.VMEM((key_rows, keys.shape[1]), BF16),
            pltpu.VMEM((keys.shape[1], key_rows), BF16),
        ],
        compiler_params=params,
        cost_estimate=pl.CostEstimate(
            flops=2 * tok * width * key_rows * 3,
            bytes_accessed=4 * tok * width * 2,
            transcendentals=tok * key_rows * QUERY_HEADS,
        ),
        name="attention",
    )(
        place, segment_length, segment_adapter, owner, queries, output_gradient, keys, values,
        *halos, adapter_activation.T,
    )

    rank_low = pl.pallas_call(
        functools.partial(rank_kernel, by_slot),
        out_shape=jax.ShapeDtypeStruct((rank, tok), BF16),
        in_specs=[SMEM] * 3 + [VMEM] * (1 + len(up_weight)),
        out_specs=VMEM,
        compiler_params=params,
        name="rank_gradient",
    )(place, segment_length, segment_adapter, dq_turned, *up_weight)
    rank_lows = [rank_low] + [shifted(rank_low, n_head, j) for j in range(1, n_head)]

    down = pl.pallas_call(
        functools.partial(down_kernel, by_slot, n_head),
        out_shape=[jax.ShapeDtypeStruct((n_groups // n_out, rank, x.shape[1]), BF16)] * n_out,
        in_specs=[SMEM] * 4 + [VMEM] * (1 + n_head),
        out_specs=[VMEM] * n_out,
        scratch_shapes=[pltpu.VMEM((n_groups * rank, pack), BF16)],
        compiler_params=params,
        name="down_parts",
    )(place, segment_length, segment_adapter, owner, x, *rank_lows)

    if by_slot:
        up = over_seq(up, n_seq)
        total = up[0]
        for j in range(1, n_head):
            total = total + shifted(up[j].astype(BF16), n_head, j).astype(F32)
        up, down = total, over_seq(down, n_seq)
    else:
        up = lax.all_to_all(up[0], "head", split_axis=1, concat_axis=1, tiled=True)
        up = spread(jnp.sum(up.astype(F32), axis=1), segment_adapter, owner, n_seq)
        down = spread(down[0].astype(F32), segment_adapter, owner, n_seq)
    return down.T[None] * ADAPTER_SCALE, up[None] * ADAPTER_SCALE


def over_seq(parts, n_seq):
    keep, send = parts
    both = (keep.astype(F32) + partnered(send, n_seq, 1).astype(F32)).astype(BF16)
    total = both[0].astype(F32)
    for m in range(1, n_seq // 2):
        total = total + partnered(both[m], n_seq, 2 * m).astype(F32)
    return total


def spread(part, segment_adapter, owner, n_seq):
    goes_to = owner[segment_adapter[0]]
    slots = (goes_to[:, None] == jnp.arange(n_seq, dtype=I32)[None, :]).astype(F32)
    slotted = jnp.einsum("srw,so->orw", part, slots, precision=lax.Precision.HIGHEST)
    slotted = lax.all_to_all(slotted.astype(BF16), "seq", split_axis=0, concat_axis=0, tiled=True)
    return jnp.sum(slotted.astype(F32), axis=0)


def solution(mesh):
    return jax.shard_map(
        on_device,
        mesh=mesh,
        in_specs=(
            P(("seq", "head"), None),
            P(("seq", "head"), None),
            P(("seq", "head"), None),
            P(("seq", "head"), None),
            P(("seq", "head"), None),
            P(("seq", "head"), None),
            P("seq", None, "head"),
            P("seq", None),
            P("seq", None),
            P(),
        ),
        out_specs=(P("seq", "head", None), P("seq", None, "head")),
        check_vma=False,
    )
```

```python
import functools
import math

import jax
import jax.numpy as jnp
from jax import lax
from jax.experimental import pallas as pl
from jax.experimental.pallas import tpu as pltpu
from jax.sharding import PartitionSpec as P

QUERY_HEADS = 32
KEY_VALUE_HEADS = 4
HEAD_SIZE = 128
GROUP = QUERY_HEADS // KEY_VALUE_HEADS
ADAPTER_SCALE = 2.0
NEVER = -1e30
BF16 = jnp.bfloat16
F32 = jnp.float32
I32 = jnp.int32
VMEM = pl.BlockSpec(memory_space=pltpu.VMEM)
SMEM = pl.BlockSpec(memory_space=pltpu.SMEM)
ANY = pl.BlockSpec(memory_space=pl.ANY)


def dot(a, b, a_dim, b_dim):
    return lax.dot_general(a, b, (((a_dim,), (b_dim,)), ((), ())), preferred_element_type=F32)


def of_tokens(position, length_ref, values_of):
    end = 0
    found = None
    for s in range(length_ref.shape[1]):
        new = values_of(s, end)
        if found is None:
            found = [jnp.zeros_like(position) + value for value in new]
        else:
            inside = position >= end
            found = [jnp.where(inside, value, old) for value, old in zip(new, found)]
        end = end + length_ref[0, s]
    return found


def group_rows(rows_of_group, n_groups, width, seq, by_slot):
    row = lax.broadcasted_iota(I32, (n_groups * rows_of_group, width), 0) // rows_of_group
    if by_slot:
        half = n_groups // 2
        row = jnp.where(row < half, row * 2, (row - half) * 2 + 1) ^ seq
    return row


def pack_kernel(n_out, tails, k_ref, v_ref, *out_refs):
    part = k_ref.shape[1] // n_out
    tok = k_ref.shape[0]
    for h in range(n_out):
        at = slice(h * part, (h + 1) * part)
        for i, rows in enumerate(tails):
            out_ref = out_refs[h * len(tails) + i]
            out_ref[:, :part] = k_ref[tok - rows :, at]
            out_ref[:, part:] = v_ref[tok - rows :, at]


def attention_kernel(
    n_halo, by_slot, first_kv, n_kv,
    place_ref, length_ref, adapter_ref, owner_ref,
    q_hbm, g_hbm, k_ref, v_ref, *refs,
):
    halo_refs = refs[:n_halo]
    n_before = 2 if first_kv else 0
    before = refs[n_halo : n_halo + n_before]
    dq_turned, *up_refs = refs[n_halo + n_before : -7]
    q_ref, g_ref, q_sem, g_sem, k_all, v_all, k_turned = refs[-7:]
    tok = q_ref.shape[0]
    kv_width = n_kv * HEAD_SIZE
    key_rows = v_all.shape[0]
    seq, head = place_ref[0], place_ref[1]
    per_kv = GROUP * HEAD_SIZE

    def fetch(kv):
        to = pl.ds(kv * per_kv, per_kv)
        at = pl.ds((first_kv + kv) * per_kv, per_kv)
        return (
            pltpu.make_async_copy(q_hbm.at[:, at], q_ref.at[:, to], q_sem.at[kv]),
            pltpu.make_async_copy(g_hbm.at[:, at], g_ref.at[:, to], g_sem.at[kv]),
        )

    for kv in range(n_kv):
        for copy in fetch(kv):
            copy.start()

    position = head * tok + lax.broadcasted_iota(I32, (1, tok), 1)
    seg_start, group = of_tokens(
        position,
        length_ref,
        lambda s, start: (start, owner_ref[adapter_ref[0, s]] if by_slot else s),
    )
    key_position = (
        head * tok - (key_rows - tok) + lax.broadcasted_iota(I32, (key_rows, tok), 0)
    )
    allowed = (key_position >= seg_start) & (key_position <= position)
    bias = jnp.where(allowed, 0.0, NEVER).astype(BF16)

    for kv in range(n_kv):
        start = 0
        at = slice(kv * HEAD_SIZE, (kv + 1) * HEAD_SIZE)
        for halo_ref in halo_refs:
            rows = halo_ref.shape[0]
            k_all[kv, start : start + rows, :HEAD_SIZE] = halo_ref[:, at]
            v_all[start : start + rows, at] = halo_ref[:, kv_width + at.start : kv_width + at.stop]
            start += rows
        own = slice((first_kv + kv) * HEAD_SIZE, (first_kv + kv + 1) * HEAD_SIZE)
        k_all[kv, start:, :HEAD_SIZE] = k_ref[:, own]
        v_all[start:, at] = v_ref[:, own]
        k_all[kv, :, HEAD_SIZE:] = bias
        k_turned[at, :] = k_all[kv, :, :HEAD_SIZE].T

    one = lax.broadcasted_iota(I32, (2 * tok, tok), 0) % tok
    pick = (one == lax.broadcasted_iota(I32, (2 * tok, tok), 1)).astype(F32).astype(BF16)
    scale = 1.0 / HEAD_SIZE**0.5
    to_log2 = scale * math.log2(math.e)

    def one_group(kv, carry):
        for copy in fetch(kv):
            copy.wait()
        at_kv = pl.ds(pl.multiple_of(kv * HEAD_SIZE, HEAD_SIZE), HEAD_SIZE)
        k_g = k_all[kv]
        v_g = v_all[:, at_kv]
        kt_g = k_turned[at_kv, :]
        for i in range(0, GROUP, 2):
            first = (kv * GROUP + i) * HEAD_SIZE
            at = [
                pl.ds(pl.multiple_of(first + n * HEAD_SIZE, HEAD_SIZE), HEAD_SIZE) for n in range(2)
            ]
            q_two = jnp.concatenate([q_ref[:, at[0]], q_ref[:, at[1]]], axis=0)
            g_two = jnp.concatenate([g_ref[:, at[0]], g_ref[:, at[1]]], axis=0)
            s = dot(k_g, jnp.concatenate([q_two, pick], axis=1), 1, 1)
            d_prob = dot(v_g, g_two, 1, 1)
            weights = jnp.exp2((s - jnp.max(s, axis=0, keepdims=True)) * to_log2)
            inverse = 1.0 / jnp.sum(weights, axis=0, keepdims=True)
            delta = jnp.sum(weights * d_prob, axis=0, keepdims=True) * inverse
            dscore = (weights * (d_prob - delta)).astype(BF16)
            dq = dot(kt_g, dscore, 1, 0) * (inverse * scale)
            dq_turned[at[0], :] = dq[:, :tok].astype(BF16)
            dq_turned[at[1], :] = dq[:, tok:].astype(BF16)
        return carry

    lax.fori_loop(0, n_kv, one_group, 0)
    if not up_refs:
        return

    act_ref, dq_before = before
    rank = act_ref.shape[0]
    n_quarters, per, _, part = up_refs[0].shape
    n_groups = per * len(up_refs)
    own = group_rows(rank, n_groups, tok, seq, by_slot) == group
    act = jnp.concatenate([act_ref[...].astype(F32)] * n_groups, axis=0)
    act_cols = jnp.where(own, act, 0.0).astype(BF16)
    n_before = dq_before.shape[0] // part

    def write(i, dq_ref, quarter):
        at = pl.ds(pl.multiple_of(i * part, part), part)
        up = dot(act_cols, dq_ref[at, :], 1, 1).astype(BF16)
        j = lax.rem(quarter + n_quarters - head, n_quarters) if by_slot else quarter
        for n in range(n_groups):
            up_refs[n // per][j, n % per] = up[n * rank : (n + 1) * rank, :]

    for i in range(n_quarters):
        if i < n_before:
            write(i, dq_before, i)
        else:
            write(i - n_before, dq_turned, i)


def down_kernel(
    by_slot, n_w, place_ref, length_ref, adapter_ref, owner_ref, x_hbm, *refs
):
    w_refs, refs = refs[:n_w], refs[n_w:]
    dq_a, dq_b, *out_refs, x_ref, x_sem = refs
    tok = x_ref.shape[0]
    seq, head = place_ref[0], place_ref[1]
    n_adapters, n_quarters, rank, part = w_refs[0].shape
    per, _, _, x_part = out_refs[0].shape
    n_groups = per * len(out_refs)

    def fetch(j):
        quarter = lax.rem(head + j, n_quarters) if by_slot else j
        at = pl.ds(pl.multiple_of(quarter * x_part, x_part), x_part)
        to = pl.ds(j * x_part, x_part)
        return pltpu.make_async_copy(x_hbm.at[:, at], x_ref.at[:, to], x_sem.at[j])

    for j in range(n_quarters):
        fetch(j).start()

    position = head * tok + lax.broadcasted_iota(I32, (1, tok), 1)
    adapter, group = of_tokens(
        position,
        length_ref,
        lambda s, start: (adapter_ref[0, s], owner_ref[adapter_ref[0, s]] if by_slot else s),
    )
    total = jnp.zeros((rank, tok), F32)
    n_a = dq_a.shape[0] // part
    for c, w_ref in enumerate(w_refs):
        rows = None
        for quarter in range(n_quarters):
            j = lax.rem(head + n_quarters - quarter, n_quarters) if by_slot else quarter
            i, dq_ref = (quarter, dq_a) if quarter < n_a else (quarter - n_a, dq_b)
            dq = dq_ref[i * part : (i + 1) * part, :]
            new = dot(w_ref[:, j].reshape(n_adapters * rank, part), dq, 1, 0)
            rows = new if rows is None else rows + new
        for m in range(n_adapters):
            a = (2 * m + c) ^ seq if by_slot else m
            total = total + jnp.where(adapter == a, rows[m * rank : (m + 1) * rank, :], 0.0)

    own = group_rows(rank, n_groups, tok, seq, by_slot) == group
    low = jnp.concatenate([total.astype(BF16).astype(F32)] * n_groups, axis=0)
    cols = jnp.where(own, low, 0.0).astype(BF16)
    step = min(512, x_part)
    for j in range(n_quarters):
        fetch(j).wait()
        for start in range(0, x_part, step):
            down = dot(cols, x_ref[:, j * x_part + start : j * x_part + start + step], 1, 0)
            down = down.astype(BF16)
            for n in range(n_groups):
                piece = down[n * rank : (n + 1) * rank, :]
                out_refs[n // per][n % per, j, :, start : start + step] = piece


def shifted(x, n_head, j):
    return lax.ppermute(x, "head", [(i, (i + j) % n_head) for i in range(n_head)])


def partnered(x, n_seq, bits):
    return lax.ppermute(x, "seq", [(i, i ^ bits) for i in range(n_seq)])


def on_device(
    queries, keys, values, output_gradient, inputs, adapter_activation,
    adapter_up_weight, segment_length, segment_adapter, owner,
):
    n_head = lax.axis_size("head")
    n_seq = lax.axis_size("seq")
    tok, width = queries.shape
    pack = tok * n_head
    rank = adapter_up_weight.shape[1]
    n_adapters = owner.shape[0]
    n_seg = segment_length.shape[1]
    by_slot = n_adapters == n_seq == 8
    place = jnp.stack([lax.axis_index("seq"), lax.axis_index("head")]).astype(I32)

    reach = []
    while sum(reach) < pack * 3 // 8:
        reach.append(min(pack * 3 // 8 - sum(reach), tok))
    tails = sorted(set(reach))
    key_rows = tok + sum(reach)
    halves = 2
    n_kv = KEY_VALUE_HEADS // halves
    kv_width = n_kv * HEAD_SIZE
    packed = pl.pallas_call(
        functools.partial(pack_kernel, halves, tails),
        out_shape=[jax.ShapeDtypeStruct((rows, 2 * kv_width), BF16) for rows in tails] * halves,
        in_specs=[VMEM] * 2,
        out_specs=[VMEM] * (halves * len(tails)),
        name="pack_halo",
    )(keys, values)

    def halo_of(h):
        got = []
        for hop, rows in enumerate(reach, 1):
            shift = [(i, i + hop) for i in range(n_head - hop)]
            got.insert(0, lax.ppermute(packed[h * len(tails) + tails.index(rows)], "head", shift))
        return got

    halo_a, halo_b = halo_of(0), halo_of(1)
    if by_slot:
        w = [adapter_up_weight] + [shifted(adapter_up_weight, n_head, j) for j in range(1, n_head)]
        w = jnp.concatenate(w, axis=0)[None]
        halo_a, w = lax.optimization_barrier((halo_a, w))
        w = [w] + [partnered(w, n_seq, 2 * m) for m in range(1, n_seq // 2)]
        w = jnp.concatenate(w, axis=0)
    else:
        w = lax.all_gather(adapter_up_weight, "seq", axis=0, tiled=True)
        up_weight = [lax.all_gather(w, "head", axis=1, tiled=False)]

    n_out = 2 if by_slot else 1
    n_groups = n_seq if by_slot else n_seg
    part = width // n_head
    x_part = inputs.shape[1] // n_head
    params = pltpu.CompilerParams(vmem_limit_bytes=32 * 2**20)

    def attention(h, halos, before, up_shapes):
        half = width // halves
        return pl.pallas_call(
            functools.partial(attention_kernel, len(halos), by_slot, h * n_kv, n_kv),
            out_shape=[jax.ShapeDtypeStruct((half, tok), BF16)] + up_shapes,
            in_specs=[SMEM] * 4 + [ANY] * 2 + [VMEM] * (2 + len(halos) + len(before)),
            out_specs=[VMEM] * (1 + len(up_shapes)),
            scratch_shapes=[
                pltpu.VMEM((tok, half), BF16),
                pltpu.VMEM((tok, half), BF16),
                pltpu.SemaphoreType.DMA((n_kv,)),
                pltpu.SemaphoreType.DMA((n_kv,)),
                pltpu.VMEM((n_kv, key_rows, 2 * HEAD_SIZE), BF16),
                pltpu.VMEM((key_rows, kv_width), BF16),
                pltpu.VMEM((kv_width, key_rows), BF16),
            ],
            compiler_params=params,
            cost_estimate=pl.CostEstimate(
                flops=2 * tok * half * key_rows * 3,
                bytes_accessed=4 * tok * half * 2,
                transcendentals=tok * key_rows * QUERY_HEADS // halves,
            ),
            name="attention_%d" % h,
        )(
            place, segment_length, segment_adapter, owner, queries, output_gradient, keys, values,
            *halos, *before,
        )

    (dq_a,) = attention(0, halo_a, [], [])
    if by_slot:
        halo_b, dq_a, w = lax.optimization_barrier((halo_b, dq_a, w))
        up_weight = [w, partnered(w, n_seq, 1)]
    up_shape = jax.ShapeDtypeStruct((n_head, n_groups // n_out, rank, part), BF16)
    dq_b, *up = attention(1, halo_b, [adapter_activation.T, dq_a], [up_shape] * n_out)

    down_shape = jax.ShapeDtypeStruct((n_groups // n_out, n_head, rank, x_part), BF16)
    down = pl.pallas_call(
        functools.partial(down_kernel, by_slot, len(up_weight)),
        out_shape=[down_shape] * n_out,
        in_specs=[SMEM] * 4 + [ANY] + [VMEM] * (2 + len(up_weight)),
        out_specs=[VMEM] * n_out,
        scratch_shapes=[
            pltpu.VMEM(inputs.shape, BF16),
            pltpu.SemaphoreType.DMA((n_head,)),
        ],
        compiler_params=params,
        cost_estimate=pl.CostEstimate(
            flops=2 * n_groups * rank * tok * (width + inputs.shape[1]),
            bytes_accessed=4 * tok * inputs.shape[1] * 2,
            transcendentals=0,
        ),
        name="down_parts",
    )(place, segment_length, segment_adapter, owner, inputs, *up_weight, dq_a, dq_b)

    if by_slot:
        up = over_chips(over_z(over_cores(up, n_seq), n_head).astype(BF16), n_seq)
        down = over_z(over_chips(over_cores(down, n_seq), n_seq).astype(BF16), n_head)
    else:
        up = lax.all_to_all(up[0], "head", split_axis=0, concat_axis=0, tiled=True)
        up = spread(jnp.sum(up.astype(F32), axis=0), segment_adapter, owner, n_seq)
        down = lax.all_to_all(down[0], "head", split_axis=1, concat_axis=1, tiled=True)
        down = spread(jnp.sum(down.astype(F32), axis=1), segment_adapter, owner, n_seq)
    return down.T[None] * ADAPTER_SCALE, up[None] * ADAPTER_SCALE


def over_cores(parts, n_seq):
    keep, send = parts
    return (keep.astype(F32) + partnered(send, n_seq, 1).astype(F32)).astype(BF16)


def over_chips(both, n_seq):
    total = both[0].astype(F32)
    for m in range(1, n_seq // 2):
        total = total + partnered(both[m], n_seq, 2 * m).astype(F32)
    return total


def over_z(both, n_head):
    total = both[0].astype(F32)
    for j in range(1, n_head):
        total = total + shifted(both[j], n_head, j).astype(F32)
    return total


def spread(part, segment_adapter, owner, n_seq):
    goes_to = owner[segment_adapter[0]]
    slots = (goes_to[:, None] == jnp.arange(n_seq, dtype=I32)[None, :]).astype(F32)
    slotted = jnp.einsum("srw,so->orw", part, slots, precision=lax.Precision.HIGHEST)
    slotted = lax.all_to_all(slotted.astype(BF16), "seq", split_axis=0, concat_axis=0, tiled=True)
    return jnp.sum(slotted.astype(F32), axis=0)


def solution(mesh):
    return jax.shard_map(
        on_device,
        mesh=mesh,
        in_specs=(
            P(("seq", "head"), None),
            P(("seq", "head"), None),
            P(("seq", "head"), None),
            P(("seq", "head"), None),
            P(("seq", "head"), None),
            P(("seq", "head"), None),
            P("seq", None, "head"),
            P("seq", None),
            P("seq", None),
            P(),
        ),
        out_specs=(P("seq", "head", None), P("seq", None, "head")),
        check_vma=False,
    )
```

```python
import functools
import math

import jax
import jax.numpy as jnp
from jax import lax
from jax.experimental import pallas as pl
from jax.experimental.pallas import tpu as pltpu
from jax.sharding import PartitionSpec as P

QUERY_HEADS = 32
KEY_VALUE_HEADS = 4
HEAD_SIZE = 128
GROUP = QUERY_HEADS // KEY_VALUE_HEADS
ADAPTER_SCALE = 2.0
NEVER = -1e30
BF16 = jnp.bfloat16
F32 = jnp.float32
I32 = jnp.int32
VMEM = pl.BlockSpec(memory_space=pltpu.VMEM)
ANY = pl.BlockSpec(memory_space=pl.ANY)


def dot(a, b, a_dim, b_dim):
    return lax.dot_general(a, b, (((a_dim,), (b_dim,)), ((), ())), preferred_element_type=F32)


def group_rows(rows_of_group, n_groups, width, seq, by_slot):
    row = lax.broadcasted_iota(I32, (n_groups * rows_of_group, width), 0) // rows_of_group
    if by_slot:
        half = n_groups // 2
        row = jnp.where(row < half, row * 2, (row - half) * 2 + 1) ^ seq
    return row


def pack_kernel(k_hbm, v_hbm, out_hbm, sems):
    width = k_hbm.shape[1]
    copies = [
        pltpu.make_async_copy(hbm, out_hbm.at[:, pl.ds(i * width, width)], sems.at[i])
        for i, hbm in enumerate((k_hbm, v_hbm))
    ]
    for copy in copies:
        copy.start()
    for copy in copies:
        copy.wait()


def ready_kernel(
    by_slot,
    length_hbm, adapter_hbm, owner_hbm, act_hbm, q_hbm, g_hbm,
    facts_ref, bias_ref, act_cols_ref, q_turned, g_turned,
    length_ref, adapter_ref, owner_ref, act_ref, q_ref, g_ref, sems, q_sem, g_sem,
):
    small = [
        pltpu.make_async_copy(source, target, sems.at[i])
        for i, (source, target) in enumerate(
            [
                (length_hbm, length_ref),
                (adapter_hbm, adapter_ref),
                (owner_hbm, owner_ref),
                (act_hbm, act_ref),
            ]
        )
    ]
    for copy in small:
        copy.start()
    per_kv = GROUP * HEAD_SIZE
    tok = q_ref.shape[0]

    def fetch(kv):
        at = pl.ds(kv * per_kv, per_kv)
        return (
            pltpu.make_async_copy(q_hbm.at[:, at], q_ref.at[:, at], q_sem.at[kv]),
            pltpu.make_async_copy(g_hbm.at[:, at], g_ref.at[:, at], g_sem.at[kv]),
        )

    for kv in range(KEY_VALUE_HEADS):
        for copy in fetch(kv):
            copy.start()
    for copy in small:
        copy.wait()

    head = lax.axis_index("head")
    position = head * tok + lax.broadcasted_iota(I32, (1, tok), 1)
    end = 0
    facts = [jnp.zeros((1, tok), I32)] * 3
    for s in range(length_ref.shape[1]):
        adapter = adapter_ref[0, s]
        new = (end, adapter, owner_ref[adapter] if by_slot else s)
        inside = position >= end
        facts = [jnp.where(inside, value, old) for value, old in zip(new, facts)]
        end = end + length_ref[0, s]
    for i, fact in enumerate(facts):
        facts_ref[i : i + 1, :] = fact

    key_rows = bias_ref.shape[0]
    key_position = (
        head * tok - (key_rows - tok) + lax.broadcasted_iota(I32, (key_rows, tok), 0)
    )
    allowed = (key_position >= facts[0]) & (key_position <= position)
    bias = jnp.where(allowed, 0.0, NEVER)
    bias_ref[:, :tok] = bias
    bias_ref[:, tok:] = bias

    rank = act_ref.shape[0]
    n_groups = act_cols_ref.shape[0] // rank
    own = group_rows(rank, n_groups, tok, lax.axis_index("seq"), by_slot) == facts[2]
    act = jnp.concatenate([act_ref[...].astype(F32)] * n_groups, axis=0)
    act_cols_ref[...] = jnp.where(own, act, 0.0).astype(BF16)

    for kv in range(KEY_VALUE_HEADS):
        for copy in fetch(kv):
            copy.wait()
        for i in range(GROUP):
            at = slice(kv * per_kv + i * HEAD_SIZE, kv * per_kv + (i + 1) * HEAD_SIZE)
            q_turned[at, :] = q_ref[:, at].T
            g_turned[at, :] = g_ref[:, at].T


def attention_kernel(by_slot, n_halo, *refs):
    bias_hbm, act_hbm, k_hbm, v_hbm, q_hbm, g_hbm, *refs = refs
    halo_hbms, refs = refs[:n_halo], refs[n_halo:]
    n_out = 2 if by_slot else 1
    dq_hbm, *refs = refs
    up_hbms, refs = refs[:n_out], refs[n_out:]
    bias_ref, act_ref, k_all, v_all, k_turned, q_ref, g_ref, dq_ref, *refs = refs
    up_refs, (first_sem, q_sem, g_sem, dq_sem, up_sem) = refs[:n_out], refs[n_out:]
    kv_width = k_all.shape[1]
    tok = q_ref.shape[1]
    head = lax.axis_index("head")
    n_quarters, per, rank, part = up_refs[0].shape
    n_groups = per * n_out
    per_kv = GROUP * HEAD_SIZE
    heads_per_quarter = part // HEAD_SIZE
    quarters_per_kv = GROUP // heads_per_quarter

    moves = [(bias_hbm, bias_ref), (act_hbm, act_ref)]
    start = 0
    for halo in halo_hbms:
        rows = pl.ds(start, halo.shape[0])
        moves.append((halo.at[:, pl.ds(0, kv_width)], k_all.at[rows, :]))
        moves.append((halo.at[:, pl.ds(kv_width, kv_width)], v_all.at[rows, :]))
        start += halo.shape[0]
    moves.append((k_hbm, k_all.at[pl.ds(start, tok), :]))
    moves.append((v_hbm, v_all.at[pl.ds(start, tok), :]))
    first = [pltpu.make_async_copy(a, b, first_sem.at[i]) for i, (a, b) in enumerate(moves)]

    def rows_of(kv):
        return pl.ds(pl.multiple_of(kv * per_kv, per_kv), per_kv)

    def fetch(kv):
        at = rows_of(kv)
        return (
            pltpu.make_async_copy(q_hbm.at[at, :], q_ref.at[at, :], q_sem.at[kv]),
            pltpu.make_async_copy(g_hbm.at[at, :], g_ref.at[at, :], g_sem.at[kv]),
        )

    def place_of(quarter):
        return lax.rem(quarter + n_quarters - head, n_quarters) if by_slot else quarter

    def put(kv):
        at = rows_of(kv)
        copies = [pltpu.make_async_copy(dq_ref.at[at, :], dq_hbm.at[at, :], dq_sem.at[kv])]
        for i in range(quarters_per_kv):
            j = place_of(kv * quarters_per_kv + i)
            for o in range(n_out):
                sem = up_sem.at[kv * quarters_per_kv + i, o]
                copies.append(pltpu.make_async_copy(up_refs[o].at[j], up_hbms[o].at[j], sem))
        return copies

    for copy in first:
        copy.start()
    for kv in range(KEY_VALUE_HEADS):
        for copy in fetch(kv):
            copy.start()
    for copy in first:
        copy.wait()
    k_turned[...] = k_all[...].T

    scale = 1.0 / HEAD_SIZE**0.5
    to_log2 = scale * math.log2(math.e)

    def one_group(kv, carry):
        for copy in fetch(kv):
            copy.wait()
        at_kv = pl.ds(pl.multiple_of(kv * HEAD_SIZE, HEAD_SIZE), HEAD_SIZE)
        k_g = k_all[:, at_kv]
        v_g = v_all[:, at_kv]
        kt_g = k_turned[at_kv, :]
        for i in range(0, GROUP, 2):
            from_row = (kv * GROUP + i) * HEAD_SIZE
            at = [
                pl.ds(pl.multiple_of(from_row + n * HEAD_SIZE, HEAD_SIZE), HEAD_SIZE)
                for n in range(2)
            ]
            q_two = jnp.concatenate([q_ref[at[0], :], q_ref[at[1], :]], axis=1)
            g_two = jnp.concatenate([g_ref[at[0], :], g_ref[at[1], :]], axis=1)
            s = dot(k_g, q_two, 1, 0) + bias_ref[...]
            d_prob = dot(v_g, g_two, 1, 0)
            weights = jnp.exp2((s - jnp.max(s, axis=0, keepdims=True)) * to_log2)
            inverse = 1.0 / jnp.sum(weights, axis=0, keepdims=True)
            delta = jnp.sum(weights * d_prob, axis=0, keepdims=True) * inverse
            dscore = (weights * (d_prob - delta)).astype(BF16)
            dq = (dot(kt_g, dscore, 1, 0) * (inverse * scale)).astype(BF16)
            j = place_of(kv * quarters_per_kv + i // heads_per_quarter)
            for n in range(2):
                dq_one = dq[:, n * tok : (n + 1) * tok]
                dq_ref[at[n], :] = dq_one
                up = dot(act_ref[...], dq_one, 1, 1).astype(BF16)
                to = (i % heads_per_quarter + n) * HEAD_SIZE
                for r in range(n_groups):
                    piece = up[r * rank : (r + 1) * rank, :]
                    up_refs[r // per][j, r % per, :, to : to + HEAD_SIZE] = piece
        for copy in put(kv):
            copy.start()
        return carry

    lax.fori_loop(0, KEY_VALUE_HEADS, one_group, 0)
    for kv in range(KEY_VALUE_HEADS):
        for copy in put(kv):
            copy.wait()


def down_kernel(by_slot, n_w, *refs):
    facts_hbm, dq_hbm, *refs = refs
    w_hbms, (x_hbm, *refs) = refs[:n_w], refs[n_w:]
    n_out = 2 if by_slot else 1
    down_hbms, (facts_ref, dq_ref, *refs) = refs[:n_out], refs[n_out:]
    w_refs, (x_ref, *refs) = refs[:n_w], refs[n_w:]
    down_refs, (facts_sem, dq_sem, w_sem, x_sem, down_sem) = refs[:n_out], refs[n_out:]
    tok = dq_ref.shape[1]
    seq, head = lax.axis_index("seq"), lax.axis_index("head")
    n_adapters, n_quarters, rank, part = w_refs[0].shape
    per, _, _, x_part = down_refs[0].shape
    n_groups = per * n_out

    facts_copy = pltpu.make_async_copy(facts_hbm, facts_ref, facts_sem)
    w_copies = [
        pltpu.make_async_copy(a, b, w_sem.at[i]) for i, (a, b) in enumerate(zip(w_hbms, w_refs))
    ]

    def fetch_dq(quarter):
        at = pl.ds(quarter * part, part)
        return pltpu.make_async_copy(dq_hbm.at[at, :], dq_ref.at[at, :], dq_sem.at[quarter])

    def fetch_x(j):
        quarter = lax.rem(head + j, n_quarters) if by_slot else j
        at = pl.ds(pl.multiple_of(quarter * x_part, x_part), x_part)
        to = pl.ds(j * x_part, x_part)
        return pltpu.make_async_copy(x_hbm.at[:, at], x_ref.at[:, to], x_sem.at[j])

    def put(j, o):
        to = down_hbms[o].at[:, j]
        return pltpu.make_async_copy(down_refs[o].at[:, j], to, down_sem.at[j, o])

    for copy in w_copies:
        copy.start()
    for quarter in range(n_quarters):
        fetch_dq(quarter).start()
    facts_copy.start()
    for j in range(n_quarters):
        fetch_x(j).start()

    for copy in w_copies:
        copy.wait()
    sums = [None] * n_w
    for quarter in range(n_quarters):
        fetch_dq(quarter).wait()
        j = lax.rem(head + n_quarters - quarter, n_quarters) if by_slot else quarter
        dq = dq_ref[quarter * part : (quarter + 1) * part, :]
        for c, w_ref in enumerate(w_refs):
            new = dot(w_ref[:, j].reshape(n_adapters * rank, part), dq, 1, 0)
            sums[c] = new if sums[c] is None else sums[c] + new
    facts_copy.wait()
    adapter = facts_ref[1:2, :]
    total = jnp.zeros((rank, tok), F32)
    for c in range(n_w):
        for m in range(n_adapters):
            a = (2 * m + c) ^ seq if by_slot else m
            rows = sums[c][m * rank : (m + 1) * rank, :]
            total = total + jnp.where(adapter == a, rows, 0.0)
    own = group_rows(rank, n_groups, tok, seq, by_slot) == facts_ref[2:3, :]
    low = jnp.concatenate([total.astype(BF16).astype(F32)] * n_groups, axis=0)
    cols = jnp.where(own, low, 0.0).astype(BF16)

    step = min(512, x_part)
    for j in range(n_quarters):
        fetch_x(j).wait()
        for start in range(0, x_part, step):
            down = dot(cols, x_ref[:, j * x_part + start : j * x_part + start + step], 1, 0)
            down = down.astype(BF16)
            for n in range(n_groups):
                piece = down[n * rank : (n + 1) * rank, :]
                down_refs[n // per][n % per, j, :, start : start + step] = piece
        for o in range(n_out):
            put(j, o).start()
    for o in range(n_out):
        for j in range(n_quarters):
            put(j, o).wait()


def shifted(x, n_head, j):
    return lax.ppermute(x, "head", [(i, (i + j) % n_head) for i in range(n_head)])


def partnered(x, n_seq, bits):
    return lax.ppermute(x, "seq", [(i, i ^ bits) for i in range(n_seq)])


def on_device(
    queries, keys, values, output_gradient, inputs, adapter_activation,
    adapter_up_weight, segment_length, segment_adapter, owner,
):
    n_head = lax.axis_size("head")
    n_seq = lax.axis_size("seq")
    tok, width = queries.shape
    pack = tok * n_head
    rank = adapter_up_weight.shape[1]
    n_adapters = owner.shape[0]
    n_seg = segment_length.shape[1]
    by_slot = n_adapters == n_seq == 8

    reach = []
    while sum(reach) < pack * 3 // 8:
        reach.append(min(pack * 3 // 8 - sum(reach), tok))
    key_rows = tok + sum(reach)
    packed = pl.pallas_call(
        pack_kernel,
        out_shape=jax.ShapeDtypeStruct((tok, 2 * keys.shape[1]), BF16),
        in_specs=[ANY] * 2,
        out_specs=ANY,
        scratch_shapes=[pltpu.SemaphoreType.DMA((2,))],
        name="pack_halo",
    )(keys, values)
    def forward(x):
        return lax.ppermute(x, "head", [(i, i + 1) for i in range(n_head - 1)])

    halos = [forward(packed[tok - reach[0] :])]

    if by_slot:
        w = [adapter_up_weight] + [shifted(adapter_up_weight, n_head, j) for j in range(1, n_head)]
        w = jnp.concatenate(w, axis=0)[None]
        w = [w] + [partnered(w, n_seq, 2 * m) for m in range(1, n_seq // 2)]
    else:
        w = lax.all_gather(adapter_up_weight, "seq", axis=0, tiled=True)
        up_weight = [lax.all_gather(w, "head", axis=1, tiled=False)]
    for rows in reach[1:]:
        halos.insert(0, forward(halos[0][tok - rows :]))
    n_out = 2 if by_slot else 1
    n_groups = n_seq if by_slot else n_seg
    part = width // n_head
    x_part = inputs.shape[1] // n_head
    ready = pl.pallas_call(
        functools.partial(ready_kernel, by_slot),
        out_shape=[
            jax.ShapeDtypeStruct((8, tok), I32),
            jax.ShapeDtypeStruct((key_rows, 2 * tok), F32),
            jax.ShapeDtypeStruct((n_groups * rank, tok), BF16),
            jax.ShapeDtypeStruct((width, tok), BF16),
            jax.ShapeDtypeStruct((width, tok), BF16),
        ],
        in_specs=[ANY] * 6,
        out_specs=[VMEM] * 5,
        scratch_shapes=[
            pltpu.SMEM(segment_length.shape, I32),
            pltpu.SMEM(segment_adapter.shape, I32),
            pltpu.SMEM(owner.shape, I32),
            pltpu.VMEM((rank, tok), BF16),
            pltpu.VMEM((tok, width), BF16),
            pltpu.VMEM((tok, width), BF16),
            pltpu.SemaphoreType.DMA((4,)),
            pltpu.SemaphoreType.DMA((KEY_VALUE_HEADS,)),
            pltpu.SemaphoreType.DMA((KEY_VALUE_HEADS,)),
        ],
        cost_estimate=pl.CostEstimate(
            flops=tok * width * 64, bytes_accessed=8 * tok * width * 2, transcendentals=0
        ),
        name="ready",
    )(
        segment_length, segment_adapter, owner, adapter_activation.T, queries, output_gradient,
    )

    if by_slot:
        _, _, w = lax.optimization_barrier((halos, ready, w))
        w = jnp.concatenate(w, axis=0)
        up_weight = [w, partnered(w, n_seq, 1)]

    up_shape = ((n_head, n_groups // n_out, rank, part), BF16)
    down_shape = ((n_groups // n_out, n_head, rank, x_part), BF16)
    facts, bias, act_cols, q_turned, g_turned = ready
    dq, *up = pl.pallas_call(
        functools.partial(attention_kernel, by_slot, len(halos)),
        out_shape=[jax.ShapeDtypeStruct((width, tok), BF16)]
        + [jax.ShapeDtypeStruct(*up_shape)] * n_out,
        in_specs=[ANY] * (6 + len(halos)),
        out_specs=[ANY] * (1 + n_out),
        scratch_shapes=[
            pltpu.VMEM(bias.shape, F32),
            pltpu.VMEM(act_cols.shape, BF16),
            pltpu.VMEM((key_rows, keys.shape[1]), BF16),
            pltpu.VMEM((key_rows, keys.shape[1]), BF16),
            pltpu.VMEM((keys.shape[1], key_rows), BF16),
            pltpu.VMEM((width, tok), BF16),
            pltpu.VMEM((width, tok), BF16),
            pltpu.VMEM((width, tok), BF16),
        ]
        + [pltpu.VMEM(*up_shape)] * n_out
        + [
            pltpu.SemaphoreType.DMA((4 + 2 * len(halos),)),
            pltpu.SemaphoreType.DMA((KEY_VALUE_HEADS,)),
            pltpu.SemaphoreType.DMA((KEY_VALUE_HEADS,)),
            pltpu.SemaphoreType.DMA((KEY_VALUE_HEADS,)),
            pltpu.SemaphoreType.DMA((n_head, n_out)),
        ],
        cost_estimate=pl.CostEstimate(
            flops=2 * tok * width * key_rows * 3,
            bytes_accessed=4 * tok * width * 2,
            transcendentals=tok * key_rows * QUERY_HEADS,
        ),
        name="attention",
    )(bias, act_cols, keys, values, q_turned, g_turned, *halos)

    down = pl.pallas_call(
        functools.partial(down_kernel, by_slot, len(up_weight)),
        out_shape=[jax.ShapeDtypeStruct(*down_shape)] * n_out,
        in_specs=[ANY] * (3 + len(up_weight)),
        out_specs=[ANY] * n_out,
        scratch_shapes=[pltpu.VMEM(facts.shape, I32), pltpu.VMEM((width, tok), BF16)]
        + [pltpu.VMEM(w.shape, BF16) for w in up_weight]
        + [pltpu.VMEM(inputs.shape, BF16)]
        + [pltpu.VMEM(*down_shape)] * n_out
        + [
            pltpu.SemaphoreType.DMA,
            pltpu.SemaphoreType.DMA((n_head,)),
            pltpu.SemaphoreType.DMA((len(up_weight),)),
            pltpu.SemaphoreType.DMA((n_head,)),
            pltpu.SemaphoreType.DMA((n_head, n_out)),
        ],
        cost_estimate=pl.CostEstimate(
            flops=2 * n_groups * rank * tok * (width + inputs.shape[1]),
            bytes_accessed=4 * tok * inputs.shape[1] * 2,
            transcendentals=0,
        ),
        name="down_parts",
    )(facts, dq, *up_weight, inputs)

    if by_slot:
        up = over_chips(over_z(over_cores(up, n_seq), n_head).astype(BF16), n_seq)
        down = over_z(over_chips(over_cores(down, n_seq), n_seq).astype(BF16), n_head)
    else:
        up = lax.all_to_all(up[0], "head", split_axis=0, concat_axis=0, tiled=True)
        up = spread(jnp.sum(up.astype(F32), axis=0), segment_adapter, owner, n_seq)
        down = lax.all_to_all(down[0], "head", split_axis=1, concat_axis=1, tiled=True)
        down = spread(jnp.sum(down.astype(F32), axis=1), segment_adapter, owner, n_seq)
    return down.T[None] * ADAPTER_SCALE, up[None] * ADAPTER_SCALE


def over_cores(parts, n_seq):
    keep, send = parts
    return (keep.astype(F32) + partnered(send, n_seq, 1).astype(F32)).astype(BF16)


def over_chips(both, n_seq):
    total = both[0].astype(F32)
    for m in range(1, n_seq // 2):
        total = total + partnered(both[m], n_seq, 2 * m).astype(F32)
    return total


def over_z(both, n_head):
    total = both[0].astype(F32)
    for j in range(1, n_head):
        total = total + shifted(both[j], n_head, j).astype(F32)
    return total


def spread(part, segment_adapter, owner, n_seq):
    goes_to = owner[segment_adapter[0]]
    slots = (goes_to[:, None] == jnp.arange(n_seq, dtype=I32)[None, :]).astype(F32)
    slotted = jnp.einsum("srw,so->orw", part, slots, precision=lax.Precision.HIGHEST)
    slotted = lax.all_to_all(slotted.astype(BF16), "seq", split_axis=0, concat_axis=0, tiled=True)
    return jnp.sum(slotted.astype(F32), axis=0)


def solution(mesh):
    return jax.shard_map(
        on_device,
        mesh=mesh,
        in_specs=(
            P(("seq", "head"), None),
            P(("seq", "head"), None),
            P(("seq", "head"), None),
            P(("seq", "head"), None),
            P(("seq", "head"), None),
            P(("seq", "head"), None),
            P("seq", None, "head"),
            P("seq", None),
            P("seq", None),
            P(),
        ),
        out_specs=(P("seq", "head", None), P("seq", None, "head")),
        check_vma=False,
    )
```

```python
import functools
import math

import jax
import jax.numpy as jnp
from jax import lax
from jax.experimental import pallas as pl
from jax.experimental.pallas import tpu as pltpu
from jax.sharding import PartitionSpec as P

QUERY_HEADS = 32
KEY_VALUE_HEADS = 4
HEAD_SIZE = 128
GROUP = QUERY_HEADS // KEY_VALUE_HEADS
ADAPTER_SCALE = 2.0
NEVER = -1e30
BF16 = jnp.bfloat16
F32 = jnp.float32
I32 = jnp.int32
VMEM = pl.BlockSpec(memory_space=pltpu.VMEM)
ANY = pl.BlockSpec(memory_space=pl.ANY)


def dot(a, b, a_dim, b_dim):
    return lax.dot_general(a, b, (((a_dim,), (b_dim,)), ((), ())), preferred_element_type=F32)


def group_rows(rows_of_group, n_groups, width, seq, by_slot):
    row = lax.broadcasted_iota(I32, (n_groups * rows_of_group, width), 0) // rows_of_group
    if by_slot:
        half = n_groups // 2
        row = jnp.where(row < half, row * 2, (row - half) * 2 + 1) ^ seq
    return row


def attention_kernel(
    n_halo, by_slot, first_kv, n_kv,
    facts_ref, q_hbm, g_hbm, own_ref, *refs,
):
    halo_refs = refs[:n_halo]
    n_before = 2 if first_kv else 0
    before = refs[n_halo : n_halo + n_before]
    dq_turned, *up_refs = refs[n_halo + n_before : -7]
    q_ref, g_ref, q_sem, g_sem, k_all, v_all, k_turned = refs[-7:]
    tok = q_ref.shape[0]
    kv_width = n_kv * HEAD_SIZE
    key_rows = v_all.shape[0]
    seq, head = lax.axis_index("seq"), lax.axis_index("head")
    per_kv = GROUP * HEAD_SIZE

    def fetch(kv):
        to = pl.ds(kv * per_kv, per_kv)
        at = pl.ds((first_kv + kv) * per_kv, per_kv)
        return (
            pltpu.make_async_copy(q_hbm.at[:, at], q_ref.at[:, to], q_sem.at[kv]),
            pltpu.make_async_copy(g_hbm.at[:, at], g_ref.at[:, to], g_sem.at[kv]),
        )

    for kv in range(n_kv):
        for copy in fetch(kv):
            copy.start()

    position = head * tok + lax.broadcasted_iota(I32, (1, tok), 1)
    seg_start = facts_ref[0:1, :]
    key_position = (
        head * tok - (key_rows - tok) + lax.broadcasted_iota(I32, (key_rows, tok), 0)
    )
    allowed = (key_position >= seg_start) & (key_position <= position)
    bias = jnp.where(allowed, 0.0, NEVER).astype(BF16)

    for kv in range(n_kv):
        start = 0
        at = slice(kv * HEAD_SIZE, (kv + 1) * HEAD_SIZE)
        for halo_ref in (*halo_refs, own_ref):
            rows = halo_ref.shape[0]
            k_all[kv, start : start + rows, :HEAD_SIZE] = halo_ref[:, at]
            v_all[start : start + rows, at] = halo_ref[:, kv_width + at.start : kv_width + at.stop]
            start += rows
        k_all[kv, :, HEAD_SIZE:] = bias
        k_turned[at, :] = k_all[kv, :, :HEAD_SIZE].T

    one = lax.broadcasted_iota(I32, (2 * tok, tok), 0) % tok
    pick = (one == lax.broadcasted_iota(I32, (2 * tok, tok), 1)).astype(F32).astype(BF16)
    scale = 1.0 / HEAD_SIZE**0.5
    to_log2 = scale * math.log2(math.e)

    def one_group(kv, carry):
        for copy in fetch(kv):
            copy.wait()
        at_kv = pl.ds(pl.multiple_of(kv * HEAD_SIZE, HEAD_SIZE), HEAD_SIZE)
        k_g = k_all[kv]
        v_g = v_all[:, at_kv]
        kt_g = k_turned[at_kv, :]
        for i in range(0, GROUP, 2):
            first = (kv * GROUP + i) * HEAD_SIZE
            at = [
                pl.ds(pl.multiple_of(first + n * HEAD_SIZE, HEAD_SIZE), HEAD_SIZE) for n in range(2)
            ]
            q_two = jnp.concatenate([q_ref[:, at[0]], q_ref[:, at[1]]], axis=0)
            g_two = jnp.concatenate([g_ref[:, at[0]], g_ref[:, at[1]]], axis=0)
            s = dot(k_g, jnp.concatenate([q_two, pick], axis=1), 1, 1)
            d_prob = dot(v_g, g_two, 1, 1)
            weights = jnp.exp2((s - jnp.max(s, axis=0, keepdims=True)) * to_log2)
            inverse = 1.0 / jnp.sum(weights, axis=0, keepdims=True)
            delta = jnp.sum(weights * d_prob, axis=0, keepdims=True) * inverse
            dscore = (weights * (d_prob - delta)).astype(BF16)
            dq = dot(kt_g, dscore, 1, 0) * (inverse * scale)
            dq_turned[at[0], :] = dq[:, :tok].astype(BF16)
            dq_turned[at[1], :] = dq[:, tok:].astype(BF16)
        return carry

    lax.fori_loop(0, n_kv, one_group, 0)
    if not up_refs:
        return

    act_ref, dq_before = before
    rank = act_ref.shape[0]
    n_quarters, per, _, part = up_refs[0].shape
    n_groups = per * len(up_refs)
    own = group_rows(rank, n_groups, tok, seq, by_slot) == facts_ref[2:3, :]
    act = jnp.concatenate([act_ref[...].astype(F32)] * n_groups, axis=0)
    act_cols = jnp.where(own, act, 0.0).astype(BF16)
    n_before = dq_before.shape[0] // part

    def write(i, dq_ref, quarter):
        at = pl.ds(pl.multiple_of(i * part, part), part)
        up = dot(act_cols, dq_ref[at, :], 1, 1).astype(BF16)
        j = lax.rem(quarter + n_quarters - head, n_quarters) if by_slot else quarter
        for n in range(n_groups):
            up_refs[n // per][j, n % per] = up[n * rank : (n + 1) * rank, :]

    for i in range(n_quarters):
        if i < n_before:
            write(i, dq_before, i)
        else:
            write(i - n_before, dq_turned, i)


def rank_kernel(by_slot, n_w, facts_ref, *refs):
    w_refs, (dq_a, dq_b, out_ref) = refs[:n_w], refs[n_w:]
    tok = dq_a.shape[1]
    seq, head = lax.axis_index("seq"), lax.axis_index("head")
    n_adapters, n_quarters, rank, part = w_refs[0].shape
    adapter = facts_ref[1:2, :]
    total = jnp.zeros((rank, tok), F32)
    n_a = dq_a.shape[0] // part
    for c, w_ref in enumerate(w_refs):
        rows = None
        for quarter in range(n_quarters):
            j = lax.rem(head + n_quarters - quarter, n_quarters) if by_slot else quarter
            i, dq_ref = (quarter, dq_a) if quarter < n_a else (quarter - n_a, dq_b)
            dq = dq_ref[i * part : (i + 1) * part, :]
            new = dot(w_ref[:, j].reshape(n_adapters * rank, part), dq, 1, 0)
            rows = new if rows is None else rows + new
        for m in range(n_adapters):
            a = (2 * m + c) ^ seq if by_slot else m
            total = total + jnp.where(adapter == a, rows[m * rank : (m + 1) * rank, :], 0.0)
    out_ref[...] = total.astype(BF16)


def down_kernel(by_slot, facts_ref, x_ref, rank_ref, *out_refs):
    rank, tok = rank_ref.shape
    seq, head = lax.axis_index("seq"), lax.axis_index("head")
    per, n_quarters, _, x_part = out_refs[0].shape
    n_groups = per * len(out_refs)
    own = group_rows(rank, n_groups, tok, seq, by_slot) == facts_ref[2:3, :]
    low = jnp.concatenate([rank_ref[...].astype(F32)] * n_groups, axis=0)
    cols = jnp.where(own, low, 0.0).astype(BF16)
    step = min(512, x_part)
    for j in range(n_quarters):
        quarter = lax.rem(head + j, n_quarters) if by_slot else j
        for start in range(0, x_part, step):
            at = pl.ds(pl.multiple_of(quarter * x_part + start, step), step)
            down = dot(cols, x_ref[:, at], 1, 0).astype(BF16)
            for n in range(n_groups):
                piece = down[n * rank : (n + 1) * rank, :]
                out_refs[n // per][n % per, j, :, start : start + step] = piece


def token_facts(tok, lengths, adapters, owner, by_slot):
    n_seg = lengths.shape[0]
    order = jnp.arange(n_seg, dtype=I32)
    starts = jnp.sum(jnp.where(order[None, :] < order[:, None], lengths[None, :], 0), axis=1)
    if by_slot:
        hits = adapters[:, None] == jnp.arange(owner.shape[0], dtype=I32)[None, :]
        groups = jnp.sum(jnp.where(hits, owner[None, :], 0), axis=1)
    else:
        groups = order
    position = lax.axis_index("head") * tok + jnp.arange(tok, dtype=I32)
    inside = (position >= starts[:, None]) & (position < (starts + lengths)[:, None])
    told = jnp.stack([starts, adapters, groups] + [jnp.zeros_like(starts)] * 5)
    return jnp.sum(jnp.where(inside[None], told[:, :, None], 0), axis=1)


def shifted(x, n_head, j):
    return lax.ppermute(x, "head", [(i, (i + j) % n_head) for i in range(n_head)])


def partnered(x, n_seq, bits):
    return lax.ppermute(x, "seq", [(i, i ^ bits) for i in range(n_seq)])


def on_device(
    queries, keys, values, output_gradient, inputs, adapter_activation,
    adapter_up_weight, segment_length, segment_adapter, owner,
):
    n_head = lax.axis_size("head")
    n_seq = lax.axis_size("seq")
    tok, width = queries.shape
    pack = tok * n_head
    rank = adapter_up_weight.shape[1]
    n_adapters = owner.shape[0]
    n_seg = segment_length.shape[1]
    by_slot = n_adapters == n_seq == 8
    facts = token_facts(tok, segment_length[0], segment_adapter[0], owner, by_slot)

    reach = []
    while sum(reach) < pack * 3 // 8:
        reach.append(min(pack * 3 // 8 - sum(reach), tok))
    tails = sorted(set(reach))
    key_rows = tok + sum(reach)
    halves = 2
    n_kv = KEY_VALUE_HEADS // halves
    kv_width = n_kv * HEAD_SIZE
    def pack_of(h):
        at = slice(h * kv_width, (h + 1) * kv_width)
        return jnp.concatenate([keys[:, at], values[:, at]], axis=1)

    own = [pack_of(h) for h in range(halves)]
    packed = [own[h][tok - rows :] for h in range(halves) for rows in tails]

    def halo_of(h):
        got = []
        for hop, rows in enumerate(reach, 1):
            shift = [(i, i + hop) for i in range(n_head - hop)]
            got.insert(0, lax.ppermute(packed[h * len(tails) + tails.index(rows)], "head", shift))
        return got

    halo_a, halo_b = halo_of(0), halo_of(1)
    if by_slot:
        w = [adapter_up_weight] + [shifted(adapter_up_weight, n_head, j) for j in range(1, n_head)]
        w = jnp.concatenate(w, axis=0)[None]
        halo_a, w = lax.optimization_barrier((halo_a, w))
        w = [w] + [partnered(w, n_seq, 2 * m) for m in range(1, n_seq // 2)]
        w = jnp.concatenate(w, axis=0)
    else:
        w = lax.all_gather(adapter_up_weight, "seq", axis=0, tiled=True)
        up_weight = [lax.all_gather(w, "head", axis=1, tiled=False)]

    n_out = 2 if by_slot else 1
    n_groups = n_seq if by_slot else n_seg
    part = width // n_head
    x_part = inputs.shape[1] // n_head
    params = pltpu.CompilerParams(vmem_limit_bytes=32 * 2**20)

    def attention(h, halos, before, up_shapes):
        half = width // halves
        return pl.pallas_call(
            functools.partial(attention_kernel, len(halos), by_slot, h * n_kv, n_kv),
            out_shape=[jax.ShapeDtypeStruct((half, tok), BF16)] + up_shapes,
            in_specs=[VMEM] + [ANY] * 2 + [VMEM] * (1 + len(halos) + len(before)),
            out_specs=[VMEM] * (1 + len(up_shapes)),
            scratch_shapes=[
                pltpu.VMEM((tok, half), BF16),
                pltpu.VMEM((tok, half), BF16),
                pltpu.SemaphoreType.DMA((n_kv,)),
                pltpu.SemaphoreType.DMA((n_kv,)),
                pltpu.VMEM((n_kv, key_rows, 2 * HEAD_SIZE), BF16),
                pltpu.VMEM((key_rows, kv_width), BF16),
                pltpu.VMEM((kv_width, key_rows), BF16),
            ],
            compiler_params=params,
            cost_estimate=pl.CostEstimate(
                flops=2 * tok * half * key_rows * 3,
                bytes_accessed=4 * tok * half * 2,
                transcendentals=tok * key_rows * QUERY_HEADS // halves,
            ),
            name="attention_%d" % h,
        )(facts, queries, output_gradient, own[h], *halos, *before)

    (dq_a,) = attention(0, halo_a, [], [])
    if by_slot:
        halo_b, dq_a, w = lax.optimization_barrier((halo_b, dq_a, w))
        up_weight = [w, partnered(w, n_seq, 1)]
    up_shape = jax.ShapeDtypeStruct((n_head, n_groups // n_out, rank, part), BF16)
    dq_b, *up = attention(1, halo_b, [adapter_activation.T, dq_a], [up_shape] * n_out)

    if by_slot:
        up, up_weight = lax.optimization_barrier((up, up_weight))
    rank_low = pl.pallas_call(
        functools.partial(rank_kernel, by_slot, len(up_weight)),
        out_shape=jax.ShapeDtypeStruct((rank, tok), BF16),
        in_specs=[VMEM] * (3 + len(up_weight)),
        out_specs=VMEM,
        compiler_params=params,
        name="rank_gradient",
    )(facts, *up_weight, dq_a, dq_b)
    if by_slot:
        rank_low, up = lax.optimization_barrier((rank_low, over_cores(up, n_seq)))

    down_shape = jax.ShapeDtypeStruct((n_groups // n_out, n_head, rank, x_part), BF16)
    down = pl.pallas_call(
        functools.partial(down_kernel, by_slot),
        out_shape=[down_shape] * n_out,
        in_specs=[VMEM] * 3,
        out_specs=[VMEM] * n_out,
        compiler_params=params,
        cost_estimate=pl.CostEstimate(
            flops=2 * n_groups * rank * tok * inputs.shape[1],
            bytes_accessed=4 * tok * inputs.shape[1] * 2,
            transcendentals=0,
        ),
        name="down_parts",
    )(facts, inputs, rank_low)

    if by_slot:
        up = over_chips(over_z(up, n_head).astype(BF16), n_seq)
        down = over_z(over_chips(over_cores(down, n_seq), n_seq).astype(BF16), n_head)
    else:
        up = lax.all_to_all(up[0], "head", split_axis=0, concat_axis=0, tiled=True)
        up = spread(jnp.sum(up.astype(F32), axis=0), segment_adapter, owner, n_seq)
        down = lax.all_to_all(down[0], "head", split_axis=1, concat_axis=1, tiled=True)
        down = spread(jnp.sum(down.astype(F32), axis=1), segment_adapter, owner, n_seq)
    return down.T[None] * ADAPTER_SCALE, up[None] * ADAPTER_SCALE


def over_cores(parts, n_seq):
    keep, send = parts
    return (keep.astype(F32) + partnered(send, n_seq, 1).astype(F32)).astype(BF16)


def over_chips(both, n_seq):
    total = both[0].astype(F32)
    for m in range(1, n_seq // 2):
        total = total + partnered(both[m], n_seq, 2 * m).astype(F32)
    return total


def over_z(both, n_head):
    total = both[0].astype(F32)
    for j in range(1, n_head):
        total = total + shifted(both[j], n_head, j).astype(F32)
    return total


def spread(part, segment_adapter, owner, n_seq):
    goes_to = owner[segment_adapter[0]]
    slots = (goes_to[:, None] == jnp.arange(n_seq, dtype=I32)[None, :]).astype(F32)
    slotted = jnp.einsum("srw,so->orw", part, slots, precision=lax.Precision.HIGHEST)
    slotted = lax.all_to_all(slotted.astype(BF16), "seq", split_axis=0, concat_axis=0, tiled=True)
    return jnp.sum(slotted.astype(F32), axis=0)


def solution(mesh):
    return jax.shard_map(
        on_device,
        mesh=mesh,
        in_specs=(
            P(("seq", "head"), None),
            P(("seq", "head"), None),
            P(("seq", "head"), None),
            P(("seq", "head"), None),
            P(("seq", "head"), None),
            P(("seq", "head"), None),
            P("seq", None, "head"),
            P("seq", None),
            P("seq", None),
            P(),
        ),
        out_specs=(P("seq", "head", None), P("seq", None, "head")),
        check_vma=False,
    )
```

```python
import functools
import math

import jax
import jax.numpy as jnp
from jax import lax
from jax.experimental import pallas as pl
from jax.experimental.pallas import tpu as pltpu
from jax.sharding import PartitionSpec as P

QUERY_HEADS = 32
KEY_VALUE_HEADS = 4
HEAD_SIZE = 128
GROUP = QUERY_HEADS // KEY_VALUE_HEADS
ADAPTER_SCALE = 2.0
NEVER = -1e30
LAYOUT_BYTES = 16 * 2**20
BF16 = jnp.bfloat16
F32 = jnp.float32
I32 = jnp.int32
SEQ = ("plane", "core")
VMEM = pl.BlockSpec(memory_space=pltpu.VMEM)
ANY = pl.BlockSpec(memory_space=pl.ANY)


def dot(a, b, a_dim, b_dim):
    return lax.dot_general(a, b, (((a_dim,), (b_dim,)), ((), ())), preferred_element_type=F32)


def seq_index():
    return lax.axis_index("plane") * lax.axis_size("core") + lax.axis_index("core")


def group_rows(rows_of_group, n_groups, width, by_slot):
    row = lax.broadcasted_iota(I32, (n_groups * rows_of_group, width), 0) // rows_of_group
    if by_slot:
        half = n_groups // 2
        core = lax.axis_index("core")
        row = jnp.where(row < half, row * 2 + core, (row - half) * 2 + 1 - core)
    return row


def layout_kernel(n_parts, facts_ref, *refs):
    parts, (k_all, v_all, k_turned) = refs[:n_parts], refs[n_parts:]
    tok = facts_ref.shape[1]
    kv_width = v_all.shape[1]
    key_rows = v_all.shape[0]
    head = lax.axis_index("head")
    position = head * tok + lax.broadcasted_iota(I32, (1, tok), 1)
    key_position = (
        head * tok - (key_rows - tok) + lax.broadcasted_iota(I32, (key_rows, tok), 0)
    )
    allowed = (key_position >= facts_ref[0:1, :]) & (key_position <= position)
    bias = jnp.where(allowed, 0.0, NEVER).astype(BF16)
    for kv in range(KEY_VALUE_HEADS):
        start = 0
        at = slice(kv * HEAD_SIZE, (kv + 1) * HEAD_SIZE)
        for part in parts:
            rows = part.shape[0]
            k_all[kv, start : start + rows, :HEAD_SIZE] = part[:, at]
            v_all[start : start + rows, at] = part[:, kv_width + at.start : kv_width + at.stop]
            start += rows
        k_all[kv, :, HEAD_SIZE:] = bias
        k_turned[at, :] = k_all[kv, :, :HEAD_SIZE].T


def attention_kernel(
    by_slot, facts_ref, act_ref, k_all, v_all, k_turned, q_hbm, g_hbm, dq_turned, *refs
):
    *up_refs, q_ref, g_ref, q_sem, g_sem = refs
    tok = q_ref.shape[0]
    per_kv = GROUP * HEAD_SIZE

    def fetch(kv):
        at = pl.ds(kv * per_kv, per_kv)
        return (
            pltpu.make_async_copy(q_hbm.at[:, at], q_ref.at[:, at], q_sem.at[kv]),
            pltpu.make_async_copy(g_hbm.at[:, at], g_ref.at[:, at], g_sem.at[kv]),
        )

    for kv in range(KEY_VALUE_HEADS):
        for copy in fetch(kv):
            copy.start()

    one = lax.broadcasted_iota(I32, (2 * tok, tok), 0) % tok
    pick = (one == lax.broadcasted_iota(I32, (2 * tok, tok), 1)).astype(F32).astype(BF16)
    scale = 1.0 / HEAD_SIZE**0.5
    to_log2 = scale * math.log2(math.e)

    def one_group(kv, carry):
        for copy in fetch(kv):
            copy.wait()
        at_kv = pl.ds(pl.multiple_of(kv * HEAD_SIZE, HEAD_SIZE), HEAD_SIZE)
        k_g = k_all[kv]
        v_g = v_all[:, at_kv]
        kt_g = k_turned[at_kv, :]
        for i in range(0, GROUP, 2):
            first = (kv * GROUP + i) * HEAD_SIZE
            at = [
                pl.ds(pl.multiple_of(first + n * HEAD_SIZE, HEAD_SIZE), HEAD_SIZE) for n in range(2)
            ]
            q_two = jnp.concatenate([q_ref[:, at[0]], q_ref[:, at[1]]], axis=0)
            g_two = jnp.concatenate([g_ref[:, at[0]], g_ref[:, at[1]]], axis=0)
            s = dot(k_g, jnp.concatenate([q_two, pick], axis=1), 1, 1)
            d_prob = dot(v_g, g_two, 1, 1)
            weights = jnp.exp2((s - jnp.max(s, axis=0, keepdims=True)) * to_log2)
            inverse = 1.0 / jnp.sum(weights, axis=0, keepdims=True)
            delta = jnp.sum(weights * d_prob, axis=0, keepdims=True) * inverse
            dscore = (weights * (d_prob - delta)).astype(BF16)
            dq = dot(kt_g, dscore, 1, 0) * (inverse * scale)
            dq_turned[at[0], :] = dq[:, :tok].astype(BF16)
            dq_turned[at[1], :] = dq[:, tok:].astype(BF16)
        return carry

    lax.fori_loop(0, KEY_VALUE_HEADS, one_group, 0)

    rank = act_ref.shape[0]
    per, n_quarters, _, part = up_refs[0].shape
    n_groups = per * len(up_refs)
    own = group_rows(rank, n_groups, tok, by_slot) == facts_ref[2:3, :]
    act = jnp.concatenate([act_ref[...].astype(F32)] * n_groups, axis=0)
    act_cols = jnp.where(own, act, 0.0).astype(BF16)
    for quarter in range(n_quarters):
        at = slice(quarter * part, (quarter + 1) * part)
        up = dot(act_cols, dq_turned[at, :], 1, 1).astype(BF16)
        for n in range(n_groups):
            up_refs[n // per][n % per, quarter] = up[n * rank : (n + 1) * rank, :]


def rank_kernel(by_slot, n_w, facts_ref, *refs):
    w_refs, (dq_ref, out_ref) = refs[:n_w], refs[n_w:]
    tok = dq_ref.shape[1]
    seq, head = seq_index(), lax.axis_index("head")
    n_adapters, n_quarters, rank, part = w_refs[0].shape
    adapter = facts_ref[1:2, :]
    total = jnp.zeros((rank, tok), F32)
    for c, w_ref in enumerate(w_refs):
        rows = None
        for quarter in range(n_quarters):
            j = lax.rem(head + n_quarters - quarter, n_quarters) if by_slot else quarter
            dq = dq_ref[quarter * part : (quarter + 1) * part, :]
            new = dot(w_ref[:, j].reshape(n_adapters * rank, part), dq, 1, 0)
            rows = new if rows is None else rows + new
        for m in range(n_adapters):
            a = (2 * m + c) ^ seq if by_slot else m
            total = total + jnp.where(adapter == a, rows[m * rank : (m + 1) * rank, :], 0.0)
    out_ref[...] = total.astype(BF16)


def down_kernel(by_slot, facts_ref, x_ref, rank_ref, *out_refs):
    rank, tok = rank_ref.shape
    per, n_quarters, _, x_part = out_refs[0].shape
    n_groups = per * len(out_refs)
    own = group_rows(rank, n_groups, tok, by_slot) == facts_ref[2:3, :]
    low = jnp.concatenate([rank_ref[...].astype(F32)] * n_groups, axis=0)
    cols = jnp.where(own, low, 0.0).astype(BF16)
    step = min(512, x_part)
    for j in range(n_quarters):
        for start in range(0, x_part, step):
            at = slice(j * x_part + start, j * x_part + start + step)
            down = dot(cols, x_ref[:, at], 1, 0).astype(BF16)
            for n in range(n_groups):
                piece = down[n * rank : (n + 1) * rank, :]
                out_refs[n // per][n % per, j, :, start : start + step] = piece


def token_facts(tok, lengths, adapters, owner, by_slot):
    n_seg = lengths.shape[0]
    order = jnp.arange(n_seg, dtype=I32)
    starts = jnp.sum(jnp.where(order[None, :] < order[:, None], lengths[None, :], 0), axis=1)
    if by_slot:
        hits = adapters[:, None] == jnp.arange(owner.shape[0], dtype=I32)[None, :]
        groups = jnp.sum(jnp.where(hits, owner[None, :], 0), axis=1)
    else:
        groups = order
    position = lax.axis_index("head") * tok + jnp.arange(tok, dtype=I32)
    inside = (position >= starts[:, None]) & (position < (starts + lengths)[:, None])
    told = jnp.stack([starts, adapters, groups] + [jnp.zeros_like(starts)] * 5)
    return jnp.sum(jnp.where(inside[None], told[:, :, None], 0), axis=1)


def shifted(x, n_head, j):
    return lax.ppermute(x, "head", [(i, (i + j) % n_head) for i in range(n_head)])


def partnered(x, n_seq, bits):
    return lax.ppermute(x, SEQ, [(i, i ^ bits) for i in range(n_seq)])


def on_device(
    queries, keys, values, output_gradient, inputs, adapter_activation,
    adapter_up_weight, segment_length, segment_adapter, owner,
):
    n_head = lax.axis_size("head")
    n_seq = lax.axis_size(SEQ)
    tok, width = queries.shape
    pack = tok * n_head
    rank = adapter_up_weight.shape[1]
    n_adapters = owner.shape[0]
    n_seg = segment_length.shape[1]
    by_slot = n_adapters == n_seq == 8
    facts = token_facts(tok, segment_length[0], segment_adapter[0], owner, by_slot)

    reach = []
    while sum(reach) < pack * 3 // 8:
        reach.append(min(pack * 3 // 8 - sum(reach), tok))
    key_rows = tok + sum(reach)
    own = jnp.concatenate([keys, values], axis=1)
    parts = [own]
    for hop, rows in enumerate(reach, 1):
        shift = [(i, i + hop) for i in range(n_head - hop)]
        parts.insert(0, lax.ppermute(own[tok - rows :], "head", shift))

    if by_slot:
        w = [adapter_up_weight] + [shifted(adapter_up_weight, n_head, j) for j in range(1, n_head)]
        w = jnp.concatenate(w, axis=0)[None]
        w = [w] + [partnered(w, n_seq, 2 * m) for m in range(1, n_seq // 2)]
        w = jnp.concatenate(w, axis=0)
        up_weight = [w, partnered(w, n_seq, 1)]
    else:
        w = lax.all_gather(adapter_up_weight, SEQ, axis=0, tiled=True)
        up_weight = [lax.all_gather(w, "head", axis=1, tiled=False)]

    n_out = 2 if by_slot else 1
    n_groups = n_seq if by_slot else n_seg
    part = width // n_head
    x_part = inputs.shape[1] // n_head
    params = pltpu.CompilerParams(vmem_limit_bytes=32 * 2**20)

    laid_out = pl.pallas_call(
        functools.partial(layout_kernel, len(parts)),
        out_shape=[
            jax.ShapeDtypeStruct((KEY_VALUE_HEADS, key_rows, 2 * HEAD_SIZE), BF16),
            jax.ShapeDtypeStruct((key_rows, keys.shape[1]), BF16),
            jax.ShapeDtypeStruct((keys.shape[1], key_rows), BF16),
        ],
        in_specs=[VMEM] * (1 + len(parts)),
        out_specs=[VMEM] * 3,
        compiler_params=params,
        cost_estimate=pl.CostEstimate(
            flops=0, bytes_accessed=LAYOUT_BYTES, transcendentals=0
        ),
        name="layout",
    )(facts, *parts)
    if by_slot:
        laid_out, up_weight = lax.optimization_barrier((laid_out, up_weight))

    up_shape = jax.ShapeDtypeStruct((n_groups // n_out, n_head, rank, part), BF16)
    dq, *up = pl.pallas_call(
        functools.partial(attention_kernel, by_slot),
        out_shape=[jax.ShapeDtypeStruct((width, tok), BF16)] + [up_shape] * n_out,
        in_specs=[VMEM] * 5 + [ANY] * 2,
        out_specs=[VMEM] * (1 + n_out),
        scratch_shapes=[
            pltpu.VMEM((tok, width), BF16),
            pltpu.VMEM((tok, width), BF16),
            pltpu.SemaphoreType.DMA((KEY_VALUE_HEADS,)),
            pltpu.SemaphoreType.DMA((KEY_VALUE_HEADS,)),
        ],
        compiler_params=params,
        cost_estimate=pl.CostEstimate(
            flops=2 * tok * width * key_rows * 3,
            bytes_accessed=4 * tok * width * 2,
            transcendentals=tok * key_rows * QUERY_HEADS,
        ),
        name="attention",
    )(facts, adapter_activation.T, *laid_out, queries, output_gradient)

    rank_low = pl.pallas_call(
        functools.partial(rank_kernel, by_slot, len(up_weight)),
        out_shape=jax.ShapeDtypeStruct((rank, tok), BF16),
        in_specs=[VMEM] * (2 + len(up_weight)),
        out_specs=VMEM,
        compiler_params=params,
        name="rank_gradient",
    )(facts, *up_weight, dq)
    if by_slot:
        rank_low, up = lax.optimization_barrier((rank_low, over_cores(up, n_seq)))

    down_shape = jax.ShapeDtypeStruct((n_groups // n_out, n_head, rank, x_part), BF16)
    down = pl.pallas_call(
        functools.partial(down_kernel, by_slot),
        out_shape=[down_shape] * n_out,
        in_specs=[VMEM] * 3,
        out_specs=[VMEM] * n_out,
        compiler_params=params,
        cost_estimate=pl.CostEstimate(
            flops=2 * n_groups * rank * tok * inputs.shape[1],
            bytes_accessed=4 * tok * inputs.shape[1] * 2,
            transcendentals=0,
        ),
        name="down_parts",
    )(facts, inputs, rank_low)

    if by_slot:
        up = added(up.reshape(-1, rank, part), ("plane", "head"))
        down = added(over_cores(down, n_seq), "plane").astype(BF16)
        down = added(down, "head")
    else:
        up = spread(added(up[0].swapaxes(0, 1), "head"), segment_adapter, owner, n_seq)
        down = spread(added(down[0].swapaxes(0, 1), "head"), segment_adapter, owner, n_seq)
    return down.T[None] * ADAPTER_SCALE, up[None] * ADAPTER_SCALE


def over_cores(parts, n_seq):
    keep, send = parts
    return (keep.astype(F32) + partnered(send, n_seq, 1).astype(F32)).astype(BF16)


def added(parts, axes):
    got = lax.all_to_all(parts, axes, split_axis=0, concat_axis=0, tiled=True)
    return jnp.sum(got.astype(F32), axis=0)


def spread(part, segment_adapter, owner, n_seq):
    goes_to = owner[segment_adapter[0]]
    slots = (goes_to[:, None] == jnp.arange(n_seq, dtype=I32)[None, :]).astype(F32)
    slotted = jnp.einsum("srw,so->orw", part, slots, precision=lax.Precision.HIGHEST)
    return added(slotted.astype(BF16), SEQ)


def solution(mesh):
    n_seq, n_head = mesh.devices.shape
    devices = mesh.devices.reshape(n_seq // 2, 2, n_head)
    return jax.shard_map(
        on_device,
        mesh=jax.sharding.Mesh(devices, ("plane", "core", "head")),
        in_specs=(
            P((*SEQ, "head"), None),
            P((*SEQ, "head"), None),
            P((*SEQ, "head"), None),
            P((*SEQ, "head"), None),
            P((*SEQ, "head"), None),
            P((*SEQ, "head"), None),
            P(SEQ, None, "head"),
            P(SEQ, None),
            P(SEQ, None),
            P(),
        ),
        out_specs=(P(SEQ, "head", None), P(SEQ, None, "head")),
        check_vma=False,
    )
```

```python
import functools
import math

import jax
import jax.numpy as jnp
from jax import lax
from jax.experimental import pallas as pl
from jax.experimental.pallas import tpu as pltpu
from jax.sharding import PartitionSpec as P

QUERY_HEADS = 32
KEY_VALUE_HEADS = 4
HEAD_SIZE = 128
GROUP = QUERY_HEADS // KEY_VALUE_HEADS
ADAPTER_SCALE = 2.0
NEVER = -1e30
LAYOUT_BYTES = 16 * 2**20
SUM_BYTES = 16 * 2**20
BF16 = jnp.bfloat16
F32 = jnp.float32
I32 = jnp.int32
VMEM = pl.BlockSpec(memory_space=pltpu.VMEM)
ANY = pl.BlockSpec(memory_space=pl.ANY)


def dot(a, b, a_dim, b_dim):
    return lax.dot_general(a, b, (((a_dim,), (b_dim,)), ((), ())), preferred_element_type=F32)


def group_rows(rows_of_group, n_groups, width, seq, by_slot):
    row = lax.broadcasted_iota(I32, (n_groups * rows_of_group, width), 0) // rows_of_group
    if by_slot:
        half = n_groups // 2
        row = jnp.where(row < half, row * 2, (row - half) * 2 + 1) ^ seq
    return row


def layout_kernel(n_parts, facts_ref, *refs):
    parts, (k_all, v_all, k_turned) = refs[:n_parts], refs[n_parts:]
    tok = facts_ref.shape[1]
    kv_width = v_all.shape[1]
    key_rows = v_all.shape[0]
    head = lax.axis_index("head")
    position = head * tok + lax.broadcasted_iota(I32, (1, tok), 1)
    key_position = (
        head * tok - (key_rows - tok) + lax.broadcasted_iota(I32, (key_rows, tok), 0)
    )
    allowed = (key_position >= facts_ref[0:1, :]) & (key_position <= position)
    bias = jnp.where(allowed, 0.0, NEVER).astype(BF16)
    for kv in range(KEY_VALUE_HEADS):
        start = 0
        at = slice(kv * HEAD_SIZE, (kv + 1) * HEAD_SIZE)
        for part in parts:
            rows = part.shape[0]
            k_all[kv, start : start + rows, :HEAD_SIZE] = part[:, at]
            v_all[start : start + rows, at] = part[:, kv_width + at.start : kv_width + at.stop]
            start += rows
        k_all[kv, :, HEAD_SIZE:] = bias
        k_turned[at, :] = k_all[kv, :, :HEAD_SIZE].T


def attention_kernel(by_slot, first_kv, n_kv, k_all, v_all, k_turned, q_hbm, g_hbm, *refs):
    before, refs = (refs[:3], refs[3:]) if first_kv else ((), refs)
    dq_turned, *up_refs, q_ref, g_ref, q_sem, g_sem = refs
    tok = q_ref.shape[0]
    seq, head = lax.axis_index("seq"), lax.axis_index("head")
    per_kv = GROUP * HEAD_SIZE

    def fetch(kv):
        to = pl.ds(kv * per_kv, per_kv)
        at = pl.ds((first_kv + kv) * per_kv, per_kv)
        return (
            pltpu.make_async_copy(q_hbm.at[:, at], q_ref.at[:, to], q_sem.at[kv]),
            pltpu.make_async_copy(g_hbm.at[:, at], g_ref.at[:, to], g_sem.at[kv]),
        )

    for kv in range(n_kv):
        for copy in fetch(kv):
            copy.start()

    one = lax.broadcasted_iota(I32, (2 * tok, tok), 0) % tok
    pick = (one == lax.broadcasted_iota(I32, (2 * tok, tok), 1)).astype(F32).astype(BF16)
    scale = 1.0 / HEAD_SIZE**0.5
    to_log2 = scale * math.log2(math.e)

    def one_group(kv, carry):
        for copy in fetch(kv):
            copy.wait()
        at_kv = pl.ds(pl.multiple_of((first_kv + kv) * HEAD_SIZE, HEAD_SIZE), HEAD_SIZE)
        k_g = k_all[first_kv + kv]
        v_g = v_all[:, at_kv]
        kt_g = k_turned[at_kv, :]
        for i in range(0, GROUP, 2):
            first = (kv * GROUP + i) * HEAD_SIZE
            at = [
                pl.ds(pl.multiple_of(first + n * HEAD_SIZE, HEAD_SIZE), HEAD_SIZE) for n in range(2)
            ]
            q_two = jnp.concatenate([q_ref[:, at[0]], q_ref[:, at[1]]], axis=0)
            g_two = jnp.concatenate([g_ref[:, at[0]], g_ref[:, at[1]]], axis=0)
            s = dot(k_g, jnp.concatenate([q_two, pick], axis=1), 1, 1)
            d_prob = dot(v_g, g_two, 1, 1)
            weights = jnp.exp2((s - jnp.max(s, axis=0, keepdims=True)) * to_log2)
            inverse = 1.0 / jnp.sum(weights, axis=0, keepdims=True)
            delta = jnp.sum(weights * d_prob, axis=0, keepdims=True) * inverse
            dscore = (weights * (d_prob - delta)).astype(BF16)
            dq = dot(kt_g, dscore, 1, 0) * (inverse * scale)
            dq_turned[at[0], :] = dq[:, :tok].astype(BF16)
            dq_turned[at[1], :] = dq[:, tok:].astype(BF16)
        return carry

    lax.fori_loop(0, n_kv, one_group, 0)
    if not up_refs:
        return

    facts_ref, act_ref, dq_before = before
    rank = act_ref.shape[0]
    n_quarters, per, _, part = up_refs[0].shape
    n_groups = per * len(up_refs)
    own = group_rows(rank, n_groups, tok, seq, by_slot) == facts_ref[2:3, :]
    act = jnp.concatenate([act_ref[...].astype(F32)] * n_groups, axis=0)
    act_cols = jnp.where(own, act, 0.0).astype(BF16)
    n_before = dq_before.shape[0] // part
    for quarter in range(n_quarters):
        i, dq_ref = (quarter, dq_before) if quarter < n_before else (quarter - n_before, dq_turned)
        up = dot(act_cols, dq_ref[i * part : (i + 1) * part, :], 1, 1).astype(BF16)
        j = lax.rem(quarter + n_quarters - head, n_quarters) if by_slot else quarter
        for n in range(n_groups):
            up_refs[n // per][j, n % per] = up[n * rank : (n + 1) * rank, :]


def rank_kernel(by_slot, n_w, facts_ref, *refs):
    w_refs, (dq_a, dq_b, out_ref) = refs[:n_w], refs[n_w:]
    tok = dq_a.shape[1]
    seq, head = lax.axis_index("seq"), lax.axis_index("head")
    n_adapters, n_quarters, rank, part = w_refs[0].shape
    adapter = facts_ref[1:2, :]
    total = jnp.zeros((rank, tok), F32)
    n_a = dq_a.shape[0] // part
    for c, w_ref in enumerate(w_refs):
        rows = None
        for quarter in range(n_quarters):
            j = lax.rem(head + n_quarters - quarter, n_quarters) if by_slot else quarter
            i, dq_ref = (quarter, dq_a) if quarter < n_a else (quarter - n_a, dq_b)
            dq = dq_ref[i * part : (i + 1) * part, :]
            new = dot(w_ref[:, j].reshape(n_adapters * rank, part), dq, 1, 0)
            rows = new if rows is None else rows + new
        for m in range(n_adapters):
            a = (2 * m + c) ^ seq if by_slot else m
            total = total + jnp.where(adapter == a, rows[m * rank : (m + 1) * rank, :], 0.0)
    out_ref[...] = total.astype(BF16)


def down_kernel(by_slot, facts_ref, x_ref, rank_ref, *out_refs):
    rank, tok = rank_ref.shape
    seq, head = lax.axis_index("seq"), lax.axis_index("head")
    per, n_quarters, _, x_part = out_refs[0].shape
    n_groups = per * len(out_refs)
    own = group_rows(rank, n_groups, tok, seq, by_slot) == facts_ref[2:3, :]
    low = jnp.concatenate([rank_ref[...].astype(F32)] * n_groups, axis=0)
    cols = jnp.where(own, low, 0.0).astype(BF16)
    step = min(512, x_part)
    for j in range(n_quarters):
        quarter = lax.rem(head + j, n_quarters) if by_slot else j
        for start in range(0, x_part, step):
            at = pl.ds(pl.multiple_of(quarter * x_part + start, step), step)
            down = dot(cols, x_ref[:, at], 1, 0).astype(BF16)
            for n in range(n_groups):
                piece = down[n * rank : (n + 1) * rank, :]
                out_refs[n // per][n % per, j, :, start : start + step] = piece


def sum_kernel(a_ref, b_ref, *out_refs):
    for i, out_ref in enumerate(out_refs):
        out_ref[...] = (a_ref[i].astype(F32) + b_ref[i].astype(F32)).astype(BF16)


def token_facts(tok, lengths, adapters, owner, by_slot):
    n_seg = lengths.shape[0]
    order = jnp.arange(n_seg, dtype=I32)
    starts = jnp.sum(jnp.where(order[None, :] < order[:, None], lengths[None, :], 0), axis=1)
    if by_slot:
        hits = adapters[:, None] == jnp.arange(owner.shape[0], dtype=I32)[None, :]
        groups = jnp.sum(jnp.where(hits, owner[None, :], 0), axis=1)
    else:
        groups = order
    position = lax.axis_index("head") * tok + jnp.arange(tok, dtype=I32)
    inside = (position >= starts[:, None]) & (position < (starts + lengths)[:, None])
    told = jnp.stack([starts, adapters, groups] + [jnp.zeros_like(starts)] * 5)
    return jnp.sum(jnp.where(inside[None], told[:, :, None], 0), axis=1)


def shifted(x, n_head, j):
    return lax.ppermute(x, "head", [(i, (i + j) % n_head) for i in range(n_head)])


def partnered(x, n_seq, bits):
    return lax.ppermute(x, "seq", [(i, i ^ bits) for i in range(n_seq)])


def on_device(
    queries, keys, values, output_gradient, inputs, adapter_activation,
    adapter_up_weight, segment_length, segment_adapter, owner,
):
    n_head = lax.axis_size("head")
    n_seq = lax.axis_size("seq")
    tok, width = queries.shape
    pack = tok * n_head
    rank = adapter_up_weight.shape[1]
    n_adapters = owner.shape[0]
    n_seg = segment_length.shape[1]
    by_slot = n_adapters == n_seq == 8
    facts = token_facts(tok, segment_length[0], segment_adapter[0], owner, by_slot)

    reach = []
    while sum(reach) < pack * 3 // 8:
        reach.append(min(pack * 3 // 8 - sum(reach), tok))
    key_rows = tok + sum(reach)
    own = jnp.concatenate([keys, values], axis=1)
    parts = [own]
    for hop, rows in enumerate(reach, 1):
        shift = [(i, i + hop) for i in range(n_head - hop)]
        parts.insert(0, lax.ppermute(own[tok - rows :], "head", shift))

    if by_slot:
        w = [adapter_up_weight] + [shifted(adapter_up_weight, n_head, j) for j in range(1, n_head)]
        w = jnp.concatenate(w, axis=0)[None]
        w = [w] + [partnered(w, n_seq, 2 * m) for m in range(1, n_seq // 2)]
    else:
        w = lax.all_gather(adapter_up_weight, "seq", axis=0, tiled=True)
        up_weight = [lax.all_gather(w, "head", axis=1, tiled=False)]

    n_out = 2 if by_slot else 1
    n_groups = n_seq if by_slot else n_seg
    part = width // n_head
    x_part = inputs.shape[1] // n_head
    params = pltpu.CompilerParams(vmem_limit_bytes=32 * 2**20)

    laid_out = pl.pallas_call(
        functools.partial(layout_kernel, len(parts)),
        out_shape=[
            jax.ShapeDtypeStruct((KEY_VALUE_HEADS, key_rows, 2 * HEAD_SIZE), BF16),
            jax.ShapeDtypeStruct((key_rows, keys.shape[1]), BF16),
            jax.ShapeDtypeStruct((keys.shape[1], key_rows), BF16),
        ],
        in_specs=[VMEM] * (1 + len(parts)),
        out_specs=[VMEM] * 3,
        compiler_params=params,
        cost_estimate=pl.CostEstimate(
            flops=0, bytes_accessed=LAYOUT_BYTES, transcendentals=0
        ),
        name="layout",
    )(facts, *parts)
    halves = 2
    n_kv = KEY_VALUE_HEADS // halves
    half = width // halves

    def attention(h, before, up_shapes):
        return pl.pallas_call(
            functools.partial(attention_kernel, by_slot, h * n_kv, n_kv),
            out_shape=[jax.ShapeDtypeStruct((half, tok), BF16)] + up_shapes,
            in_specs=[VMEM] * 3 + [ANY] * 2 + [VMEM] * len(before),
            out_specs=[VMEM] * (1 + len(up_shapes)),
            scratch_shapes=[
                pltpu.VMEM((tok, half), BF16),
                pltpu.VMEM((tok, half), BF16),
                pltpu.SemaphoreType.DMA((n_kv,)),
                pltpu.SemaphoreType.DMA((n_kv,)),
            ],
            compiler_params=params,
            cost_estimate=pl.CostEstimate(
                flops=2 * tok * half * key_rows * 3,
                bytes_accessed=4 * tok * half * 2,
                transcendentals=tok * key_rows * QUERY_HEADS // halves,
            ),
            name="attention_%d" % h,
        )(*laid_out, queries, output_gradient, *before)

    (dq_a,) = attention(0, [], [])
    if by_slot:
        dq_a, w = lax.optimization_barrier((dq_a, w))
        w = jnp.concatenate(w, axis=0)
        up_weight = [w, partnered(w, n_seq, 1)]
    up_shape = jax.ShapeDtypeStruct((n_head, n_groups // n_out, rank, part), BF16)
    dq_b, *up = attention(1, [facts, adapter_activation.T, dq_a], [up_shape] * n_out)

    if by_slot:
        up, up_weight = lax.optimization_barrier((up, up_weight))
    rank_low = pl.pallas_call(
        functools.partial(rank_kernel, by_slot, len(up_weight)),
        out_shape=jax.ShapeDtypeStruct((rank, tok), BF16),
        in_specs=[VMEM] * (3 + len(up_weight)),
        out_specs=VMEM,
        compiler_params=params,
        name="rank_gradient",
    )(facts, *up_weight, dq_a, dq_b)
    if by_slot:
        rank_low, up = lax.optimization_barrier((rank_low, over_cores(up, n_seq)))

    down_shape = jax.ShapeDtypeStruct((n_groups // n_out, n_head, rank, x_part), BF16)
    down = pl.pallas_call(
        functools.partial(down_kernel, by_slot),
        out_shape=[down_shape] * n_out,
        in_specs=[VMEM] * 3,
        out_specs=[VMEM] * n_out,
        compiler_params=params,
        cost_estimate=pl.CostEstimate(
            flops=2 * n_groups * rank * tok * inputs.shape[1],
            bytes_accessed=4 * tok * inputs.shape[1] * 2,
            transcendentals=0,
        ),
        name="down_parts",
    )(facts, inputs, rank_low)

    if by_slot:
        down = pl.pallas_call(
            sum_kernel,
            out_shape=[jax.ShapeDtypeStruct(down[0].shape[1:], BF16)] * down[0].shape[0],
            in_specs=[VMEM] * 2,
            out_specs=[VMEM] * down[0].shape[0],
            compiler_params=params,
            cost_estimate=pl.CostEstimate(flops=0, bytes_accessed=SUM_BYTES, transcendentals=0),
            name="core_sum",
        )(down[0], partnered(down[1], n_seq, 1))
        down_got = [partnered(down[m], n_seq, 2 * m) for m in range(1, n_seq // 2)]
        up_got = [shifted(up[j], n_head, j) for j in range(1, n_head)]
        down_got, up_got = lax.optimization_barrier((down_got, up_got))
        up = over_chips(added(up[0], up_got).astype(BF16), n_seq)
        down = over_z(added(down[0], down_got).astype(BF16), n_head)
    else:
        up = lax.all_to_all(up[0], "head", split_axis=0, concat_axis=0, tiled=True)
        up = spread(jnp.sum(up.astype(F32), axis=0), segment_adapter, owner, n_seq)
        down = lax.all_to_all(down[0], "head", split_axis=1, concat_axis=1, tiled=True)
        down = spread(jnp.sum(down.astype(F32), axis=1), segment_adapter, owner, n_seq)
    return down.T[None] * ADAPTER_SCALE, up[None] * ADAPTER_SCALE


def over_cores(parts, n_seq):
    keep, send = parts
    return (keep.astype(F32) + partnered(send, n_seq, 1).astype(F32)).astype(BF16)


def added(own, got):
    total = own.astype(F32)
    for piece in got:
        total = total + piece.astype(F32)
    return total


def over_chips(both, n_seq):
    return added(both[0], [partnered(both[m], n_seq, 2 * m) for m in range(1, n_seq // 2)])


def over_z(both, n_head):
    return added(both[0], [shifted(both[j], n_head, j) for j in range(1, n_head)])


def spread(part, segment_adapter, owner, n_seq):
    goes_to = owner[segment_adapter[0]]
    slots = (goes_to[:, None] == jnp.arange(n_seq, dtype=I32)[None, :]).astype(F32)
    slotted = jnp.einsum("srw,so->orw", part, slots, precision=lax.Precision.HIGHEST)
    slotted = lax.all_to_all(slotted.astype(BF16), "seq", split_axis=0, concat_axis=0, tiled=True)
    return jnp.sum(slotted.astype(F32), axis=0)


def solution(mesh):
    return jax.shard_map(
        on_device,
        mesh=mesh,
        in_specs=(
            P(("seq", "head"), None),
            P(("seq", "head"), None),
            P(("seq", "head"), None),
            P(("seq", "head"), None),
            P(("seq", "head"), None),
            P(("seq", "head"), None),
            P("seq", None, "head"),
            P("seq", None),
            P("seq", None),
            P(),
        ),
        out_specs=(P("seq", "head", None), P("seq", None, "head")),
        check_vma=False,
    )
```

```python
import functools
import math

import jax
import jax.numpy as jnp
from jax import lax
from jax.experimental import pallas as pl
from jax.experimental.pallas import tpu as pltpu
from jax.sharding import PartitionSpec as P

QUERY_HEADS = 32
KEY_VALUE_HEADS = 4
HEAD_SIZE = 128
GROUP = QUERY_HEADS // KEY_VALUE_HEADS
ADAPTER_SCALE = 2.0
NEVER = -1e30
LAYOUT_BYTES = 16 * 2**20
SUM_BYTES = 16 * 2**20
BF16 = jnp.bfloat16
F32 = jnp.float32
I32 = jnp.int32
VMEM = pl.BlockSpec(memory_space=pltpu.VMEM)
ANY = pl.BlockSpec(memory_space=pl.ANY)


def dot(a, b, a_dim, b_dim):
    return lax.dot_general(a, b, (((a_dim,), (b_dim,)), ((), ())), preferred_element_type=F32)


def group_rows(rows_of_group, n_groups, width, seq, by_slot):
    row = lax.broadcasted_iota(I32, (n_groups * rows_of_group, width), 0) // rows_of_group
    if by_slot:
        half = n_groups // 2
        row = jnp.where(row < half, row * 2, (row - half) * 2 + 1) ^ seq
    return row


def layout_kernel(n_parts, facts_ref, *refs):
    own_turned, *parts = refs[: n_parts + 1]
    k_all, v_all, k_turned, bias = refs[n_parts + 1 :]
    tok = facts_ref.shape[1]
    kv_width = v_all.shape[1]
    key_rows = v_all.shape[0]
    head = lax.axis_index("head")
    position = head * tok + lax.broadcasted_iota(I32, (1, tok), 1)
    key_position = (
        head * tok - (key_rows - tok) + lax.broadcasted_iota(I32, (key_rows, tok), 0)
    )
    allowed = (key_position >= facts_ref[0:1, :]) & (key_position <= position)
    bias[...] = jnp.where(allowed, 0.0, NEVER)
    for kv in range(KEY_VALUE_HEADS):
        start = 0
        at = slice(kv * HEAD_SIZE, (kv + 1) * HEAD_SIZE)
        for part in parts:
            rows = part.shape[0]
            k_all[start : start + rows, at] = part[:, at]
            v_all[start : start + rows, at] = part[:, kv_width + at.start : kv_width + at.stop]
            start += rows
        k_turned[at, : start - tok] = k_all[: start - tok, at].T
        k_turned[at, start - tok :] = own_turned[at, :]


def attention_kernel(by_slot, first_kv, n_kv, k_all, v_all, k_turned, bias, q_hbm, g_hbm, *refs):
    before, refs = (refs[:3], refs[3:]) if first_kv else ((), refs)
    dq_turned, *up_refs, q_ref, g_ref, q_sem, g_sem = refs
    tok = q_ref.shape[0]
    seq, head = lax.axis_index("seq"), lax.axis_index("head")
    per_kv = GROUP * HEAD_SIZE

    def fetch(kv):
        to = pl.ds(kv * per_kv, per_kv)
        at = pl.ds((first_kv + kv) * per_kv, per_kv)
        return (
            pltpu.make_async_copy(q_hbm.at[:, at], q_ref.at[:, to], q_sem.at[kv]),
            pltpu.make_async_copy(g_hbm.at[:, at], g_ref.at[:, to], g_sem.at[kv]),
        )

    for kv in range(n_kv):
        for copy in fetch(kv):
            copy.start()

    scale = 1.0 / HEAD_SIZE**0.5
    to_log2 = scale * math.log2(math.e)

    def one_group(kv, carry):
        for copy in fetch(kv):
            copy.wait()
        at_kv = pl.ds(pl.multiple_of((first_kv + kv) * HEAD_SIZE, HEAD_SIZE), HEAD_SIZE)
        k_g = k_all[:, at_kv]
        v_g = v_all[:, at_kv]
        kt_g = k_turned[at_kv, :]
        for i in range(0, GROUP, 2):
            first = (kv * GROUP + i) * HEAD_SIZE
            at = [
                pl.ds(pl.multiple_of(first + n * HEAD_SIZE, HEAD_SIZE), HEAD_SIZE) for n in range(2)
            ]
            q_two = jnp.concatenate([q_ref[:, at[0]], q_ref[:, at[1]]], axis=0)
            g_two = jnp.concatenate([g_ref[:, at[0]], g_ref[:, at[1]]], axis=0)
            s = dot(k_g, q_two, 1, 1) + jnp.concatenate([bias[...]] * 2, axis=1)
            d_prob = dot(v_g, g_two, 1, 1)
            weights = jnp.exp2((s - jnp.max(s, axis=0, keepdims=True)) * to_log2)
            inverse = 1.0 / jnp.sum(weights, axis=0, keepdims=True)
            delta = jnp.sum(weights * d_prob, axis=0, keepdims=True) * inverse
            dscore = (weights * (d_prob - delta)).astype(BF16)
            dq = dot(kt_g, dscore, 1, 0) * (inverse * scale)
            dq_turned[at[0], :] = dq[:, :tok].astype(BF16)
            dq_turned[at[1], :] = dq[:, tok:].astype(BF16)
        return carry

    lax.fori_loop(0, n_kv, one_group, 0)
    if not up_refs:
        return

    facts_ref, act_ref, dq_before = before
    rank = act_ref.shape[0]
    n_quarters, per, _, part = up_refs[0].shape
    n_groups = per * len(up_refs)
    own = group_rows(rank, n_groups, tok, seq, by_slot) == facts_ref[2:3, :]
    act = jnp.concatenate([act_ref[...].astype(F32)] * n_groups, axis=0)
    act_cols = jnp.where(own, act, 0.0).astype(BF16)
    n_before = dq_before.shape[0] // part
    for quarter in range(n_quarters):
        i, dq_ref = (quarter, dq_before) if quarter < n_before else (quarter - n_before, dq_turned)
        up = dot(act_cols, dq_ref[i * part : (i + 1) * part, :], 1, 1).astype(BF16)
        j = lax.rem(quarter + n_quarters - head, n_quarters) if by_slot else quarter
        for n in range(n_groups):
            up_refs[n // per][j, n % per] = up[n * rank : (n + 1) * rank, :]


def rank_kernel(by_slot, n_w, facts_ref, *refs):
    w_refs, (dq_a, dq_b, out_ref) = refs[:n_w], refs[n_w:]
    tok = dq_a.shape[1]
    seq, head = lax.axis_index("seq"), lax.axis_index("head")
    n_adapters, n_quarters, rank, part = w_refs[0].shape
    adapter = facts_ref[1:2, :]
    total = jnp.zeros((rank, tok), F32)
    n_a = dq_a.shape[0] // part
    for c, w_ref in enumerate(w_refs):
        rows = None
        for quarter in range(n_quarters):
            j = lax.rem(head + n_quarters - quarter, n_quarters) if by_slot else quarter
            i, dq_ref = (quarter, dq_a) if quarter < n_a else (quarter - n_a, dq_b)
            dq = dq_ref[i * part : (i + 1) * part, :]
            new = dot(w_ref[:, j].reshape(n_adapters * rank, part), dq, 1, 0)
            rows = new if rows is None else rows + new
        for m in range(n_adapters):
            a = (2 * m + c) ^ seq if by_slot else m
            total = total + jnp.where(adapter == a, rows[m * rank : (m + 1) * rank, :], 0.0)
    out_ref[...] = total.astype(BF16)


def down_kernel(by_slot, facts_ref, x_ref, rank_ref, *out_refs):
    rank, tok = rank_ref.shape
    seq, head = lax.axis_index("seq"), lax.axis_index("head")
    per, n_quarters, _, x_part = out_refs[0].shape
    n_groups = per * len(out_refs)
    own = group_rows(rank, n_groups, tok, seq, by_slot) == facts_ref[2:3, :]
    low = jnp.concatenate([rank_ref[...].astype(F32)] * n_groups, axis=0)
    cols = jnp.where(own, low, 0.0).astype(BF16)
    step = min(512, x_part)
    for j in range(n_quarters):
        quarter = lax.rem(head + j, n_quarters) if by_slot else j
        for start in range(0, x_part, step):
            at = pl.ds(pl.multiple_of(quarter * x_part + start, step), step)
            down = dot(cols, x_ref[:, at], 1, 0).astype(BF16)
            for n in range(n_groups):
                piece = down[n * rank : (n + 1) * rank, :]
                out_refs[n // per][n % per, j, :, start : start + step] = piece


def sum_kernel(a_ref, b_ref, *out_refs):
    for i, out_ref in enumerate(out_refs):
        out_ref[...] = (a_ref[i].astype(F32) + b_ref[i].astype(F32)).astype(BF16)


def token_facts(tok, lengths, adapters, owner, by_slot):
    n_seg = lengths.shape[0]
    order = jnp.arange(n_seg, dtype=I32)
    starts = jnp.sum(jnp.where(order[None, :] < order[:, None], lengths[None, :], 0), axis=1)
    if by_slot:
        hits = adapters[:, None] == jnp.arange(owner.shape[0], dtype=I32)[None, :]
        groups = jnp.sum(jnp.where(hits, owner[None, :], 0), axis=1)
    else:
        groups = order
    position = lax.axis_index("head") * tok + jnp.arange(tok, dtype=I32)
    inside = (position >= starts[:, None]) & (position < (starts + lengths)[:, None])
    told = jnp.stack([starts, adapters, groups] + [jnp.zeros_like(starts)] * 5)
    return jnp.sum(jnp.where(inside[None], told[:, :, None], 0), axis=1)


def shifted(x, n_head, j):
    return lax.ppermute(x, "head", [(i, (i + j) % n_head) for i in range(n_head)])


def partnered(x, n_seq, bits):
    return lax.ppermute(x, "seq", [(i, i ^ bits) for i in range(n_seq)])


def on_device(
    queries, keys, values, output_gradient, inputs, adapter_activation,
    adapter_up_weight, segment_length, segment_adapter, owner,
):
    n_head = lax.axis_size("head")
    n_seq = lax.axis_size("seq")
    tok, width = queries.shape
    pack = tok * n_head
    rank = adapter_up_weight.shape[1]
    n_adapters = owner.shape[0]
    n_seg = segment_length.shape[1]
    by_slot = n_adapters == n_seq == 8
    facts = token_facts(tok, segment_length[0], segment_adapter[0], owner, by_slot)

    reach = []
    while sum(reach) < pack * 3 // 8:
        reach.append(min(pack * 3 // 8 - sum(reach), tok))
    key_rows = tok + sum(reach)
    own = jnp.concatenate([keys, values], axis=1)
    parts = [own]
    for hop, rows in enumerate(reach, 1):
        shift = [(i, i + hop) for i in range(n_head - hop)]
        parts.insert(0, lax.ppermute(own[tok - rows :], "head", shift))

    if by_slot:
        w = [adapter_up_weight] + [shifted(adapter_up_weight, n_head, j) for j in range(1, n_head)]
        w = jnp.concatenate(w, axis=0)[None]
        w = [w] + [partnered(w, n_seq, 2 * m) for m in range(1, n_seq // 2)]
    else:
        w = lax.all_gather(adapter_up_weight, "seq", axis=0, tiled=True)
        up_weight = [lax.all_gather(w, "head", axis=1, tiled=False)]

    n_out = 2 if by_slot else 1
    n_groups = n_seq if by_slot else n_seg
    part = width // n_head
    x_part = inputs.shape[1] // n_head
    params = pltpu.CompilerParams(vmem_limit_bytes=32 * 2**20)

    laid_out = pl.pallas_call(
        functools.partial(layout_kernel, len(parts)),
        out_shape=[
            jax.ShapeDtypeStruct((key_rows, keys.shape[1]), BF16),
            jax.ShapeDtypeStruct((key_rows, keys.shape[1]), BF16),
            jax.ShapeDtypeStruct((keys.shape[1], key_rows), BF16),
            jax.ShapeDtypeStruct((key_rows, tok), F32),
        ],
        in_specs=[VMEM] * (2 + len(parts)),
        out_specs=[VMEM] * 4,
        compiler_params=params,
        cost_estimate=pl.CostEstimate(
            flops=0, bytes_accessed=LAYOUT_BYTES, transcendentals=0
        ),
        name="layout",
    )(facts, keys.T, *parts)
    halves = 2
    n_kv = KEY_VALUE_HEADS // halves
    half = width // halves

    def attention(h, before, up_shapes):
        return pl.pallas_call(
            functools.partial(attention_kernel, by_slot, h * n_kv, n_kv),
            out_shape=[jax.ShapeDtypeStruct((half, tok), BF16)] + up_shapes,
            in_specs=[VMEM] * 4 + [ANY] * 2 + [VMEM] * len(before),
            out_specs=[VMEM] * (1 + len(up_shapes)),
            scratch_shapes=[
                pltpu.VMEM((tok, half), BF16),
                pltpu.VMEM((tok, half), BF16),
                pltpu.SemaphoreType.DMA((n_kv,)),
                pltpu.SemaphoreType.DMA((n_kv,)),
            ],
            compiler_params=params,
            cost_estimate=pl.CostEstimate(
                flops=2 * tok * half * key_rows * 3,
                bytes_accessed=4 * tok * half * 2,
                transcendentals=tok * key_rows * QUERY_HEADS // halves,
            ),
            name="attention_%d" % h,
        )(*laid_out, queries, output_gradient, *before)

    (dq_a,) = attention(0, [], [])
    if by_slot:
        dq_a, w = lax.optimization_barrier((dq_a, w))
        w = jnp.concatenate(w, axis=0)
        up_weight = [w, partnered(w, n_seq, 1)]
    up_shape = jax.ShapeDtypeStruct((n_head, n_groups // n_out, rank, part), BF16)
    dq_b, *up = attention(1, [facts, adapter_activation.T, dq_a], [up_shape] * n_out)

    if by_slot:
        up, up_weight = lax.optimization_barrier((up, up_weight))
    rank_low = pl.pallas_call(
        functools.partial(rank_kernel, by_slot, len(up_weight)),
        out_shape=jax.ShapeDtypeStruct((rank, tok), BF16),
        in_specs=[VMEM] * (3 + len(up_weight)),
        out_specs=VMEM,
        compiler_params=params,
        name="rank_gradient",
    )(facts, *up_weight, dq_a, dq_b)

    down_shape = jax.ShapeDtypeStruct((n_groups // n_out, n_head, rank, x_part), BF16)
    down = pl.pallas_call(
        functools.partial(down_kernel, by_slot),
        out_shape=[down_shape] * n_out,
        in_specs=[VMEM] * 3,
        out_specs=[VMEM] * n_out,
        compiler_params=params,
        cost_estimate=pl.CostEstimate(
            flops=2 * n_groups * rank * tok * inputs.shape[1],
            bytes_accessed=4 * tok * inputs.shape[1] * 2,
            transcendentals=0,
        ),
        name="down_parts",
    )(facts, inputs, rank_low)

    if by_slot:
        down = pl.pallas_call(
            sum_kernel,
            out_shape=[jax.ShapeDtypeStruct(down[0].shape[1:], BF16)] * down[0].shape[0],
            in_specs=[VMEM] * 2,
            out_specs=[VMEM] * down[0].shape[0],
            compiler_params=params,
            cost_estimate=pl.CostEstimate(flops=0, bytes_accessed=SUM_BYTES, transcendentals=0),
            name="core_sum",
        )(down[0], partnered(down[1], n_seq, 1))
        down_got = [partnered(down[m], n_seq, 2 * m) for m in range(1, n_seq // 2)]
        up = over_cores(up, n_seq)
        up_got = [shifted(up[j], n_head, j) for j in range(1, n_head)]
        down_got, up_got = lax.optimization_barrier((down_got, up_got))
        up = added(up[0], up_got).astype(BF16)
        down = added(down[0], down_got).astype(BF16)
        up_got = [partnered(up[m], n_seq, 2 * m) for m in range(1, n_seq // 2)]
        down_got = [shifted(down[j], n_head, j) for j in range(1, n_head)]
        down_got, up_got = lax.optimization_barrier((down_got, up_got))
        up, down = added(up[0], up_got), added(down[0], down_got)
    else:
        up = lax.all_to_all(up[0], "head", split_axis=0, concat_axis=0, tiled=True)
        up = spread(jnp.sum(up.astype(F32), axis=0), segment_adapter, owner, n_seq)
        down = lax.all_to_all(down[0], "head", split_axis=1, concat_axis=1, tiled=True)
        down = spread(jnp.sum(down.astype(F32), axis=1), segment_adapter, owner, n_seq)
    return down.T[None] * ADAPTER_SCALE, up[None] * ADAPTER_SCALE


def over_cores(parts, n_seq):
    keep, send = parts
    return (keep.astype(F32) + partnered(send, n_seq, 1).astype(F32)).astype(BF16)


def added(own, got):
    total = own.astype(F32)
    for piece in got:
        total = total + piece.astype(F32)
    return total


def over_chips(both, n_seq):
    return added(both[0], [partnered(both[m], n_seq, 2 * m) for m in range(1, n_seq // 2)])


def over_z(both, n_head):
    return added(both[0], [shifted(both[j], n_head, j) for j in range(1, n_head)])


def spread(part, segment_adapter, owner, n_seq):
    goes_to = owner[segment_adapter[0]]
    slots = (goes_to[:, None] == jnp.arange(n_seq, dtype=I32)[None, :]).astype(F32)
    slotted = jnp.einsum("srw,so->orw", part, slots, precision=lax.Precision.HIGHEST)
    slotted = lax.all_to_all(slotted.astype(BF16), "seq", split_axis=0, concat_axis=0, tiled=True)
    return jnp.sum(slotted.astype(F32), axis=0)


def solution(mesh):
    return jax.shard_map(
        on_device,
        mesh=mesh,
        in_specs=(
            P(("seq", "head"), None),
            P(("seq", "head"), None),
            P(("seq", "head"), None),
            P(("seq", "head"), None),
            P(("seq", "head"), None),
            P(("seq", "head"), None),
            P("seq", None, "head"),
            P("seq", None),
            P("seq", None),
            P(),
        ),
        out_specs=(P("seq", "head", None), P("seq", None, "head")),
        check_vma=False,
    )
```

```python
import functools
import math

import jax
import jax.numpy as jnp
from jax import lax
from jax.experimental import pallas as pl
from jax.experimental.pallas import tpu as pltpu
from jax.sharding import PartitionSpec as P

QUERY_HEADS = 32
KEY_VALUE_HEADS = 4
HEAD_SIZE = 128
GROUP = QUERY_HEADS // KEY_VALUE_HEADS
ADAPTER_SCALE = 2.0
NEVER = -1e30
LAYOUT_BYTES = 16 * 2**20
SUM_BYTES = 16 * 2**20
BF16 = jnp.bfloat16
F32 = jnp.float32
I32 = jnp.int32
VMEM = pl.BlockSpec(memory_space=pltpu.VMEM)
ANY = pl.BlockSpec(memory_space=pl.ANY)


def dot(a, b, a_dim, b_dim):
    return lax.dot_general(a, b, (((a_dim,), (b_dim,)), ((), ())), preferred_element_type=F32)


def group_rows(rows_of_group, n_groups, width, seq, by_slot):
    row = lax.broadcasted_iota(I32, (n_groups * rows_of_group, width), 0) // rows_of_group
    if by_slot:
        half = n_groups // 2
        row = jnp.where(row < half, row * 2, (row - half) * 2 + 1) ^ seq
    return row


def layout_kernel(n_parts, facts_ref, *refs):
    own_turned, *parts = refs[: n_parts + 1]
    k_all, v_all, k_turned, bias = refs[n_parts + 1 :]
    tok = facts_ref.shape[1]
    kv_width = v_all.shape[1]
    key_rows = v_all.shape[0]
    head = lax.axis_index("head")
    position = head * tok + lax.broadcasted_iota(I32, (1, tok), 1)
    key_position = (
        head * tok - (key_rows - tok) + lax.broadcasted_iota(I32, (key_rows, tok), 0)
    )
    allowed = (key_position >= facts_ref[0:1, :]) & (key_position <= position)
    bias[...] = jnp.where(allowed, 0.0, NEVER)
    for kv in range(KEY_VALUE_HEADS):
        start = 0
        at = slice(kv * HEAD_SIZE, (kv + 1) * HEAD_SIZE)
        for part in parts:
            rows = part.shape[0]
            k_all[start : start + rows, at] = part[:, at]
            v_all[start : start + rows, at] = part[:, kv_width + at.start : kv_width + at.stop]
            start += rows
        k_turned[at, : start - tok] = k_all[: start - tok, at].T
        k_turned[at, start - tok :] = own_turned[at, :]


def attention_kernel(by_slot, first_kv, n_kv, k_all, v_all, k_turned, bias, q_hbm, g_hbm, *refs):
    before, refs = (refs[:3], refs[3:]) if first_kv else ((), refs)
    dq_turned, *up_refs, q_ref, g_ref, q_sem, g_sem = refs
    tok = q_ref.shape[0]
    seq, head = lax.axis_index("seq"), lax.axis_index("head")
    per_kv = GROUP * HEAD_SIZE

    def fetch(kv):
        to = pl.ds(kv * per_kv, per_kv)
        at = pl.ds((first_kv + kv) * per_kv, per_kv)
        return (
            pltpu.make_async_copy(q_hbm.at[:, at], q_ref.at[:, to], q_sem.at[kv]),
            pltpu.make_async_copy(g_hbm.at[:, at], g_ref.at[:, to], g_sem.at[kv]),
        )

    for kv in range(n_kv):
        for copy in fetch(kv):
            copy.start()

    scale = 1.0 / HEAD_SIZE**0.5
    to_log2 = scale * math.log2(math.e)

    def one_group(kv, carry):
        for copy in fetch(kv):
            copy.wait()
        at_kv = pl.ds(pl.multiple_of((first_kv + kv) * HEAD_SIZE, HEAD_SIZE), HEAD_SIZE)
        k_g = k_all[:, at_kv]
        v_g = v_all[:, at_kv]
        kt_g = k_turned[at_kv, :]
        for i in range(0, GROUP, 2):
            first = (kv * GROUP + i) * HEAD_SIZE
            at = [
                pl.ds(pl.multiple_of(first + n * HEAD_SIZE, HEAD_SIZE), HEAD_SIZE) for n in range(2)
            ]
            q_two = jnp.concatenate([q_ref[:, at[0]], q_ref[:, at[1]]], axis=0)
            g_two = jnp.concatenate([g_ref[:, at[0]], g_ref[:, at[1]]], axis=0)
            s = dot(k_g, q_two, 1, 1) + jnp.concatenate([bias[...]] * 2, axis=1)
            d_prob = dot(v_g, g_two, 1, 1)
            weights = jnp.exp2((s - jnp.max(s, axis=0, keepdims=True)) * to_log2)
            inverse = 1.0 / jnp.sum(weights, axis=0, keepdims=True)
            delta = jnp.sum(weights * d_prob, axis=0, keepdims=True) * inverse
            dscore = (weights * (d_prob - delta)).astype(BF16)
            dq = dot(kt_g, dscore, 1, 0) * (inverse * scale)
            dq_turned[at[0], :] = dq[:, :tok].astype(BF16)
            dq_turned[at[1], :] = dq[:, tok:].astype(BF16)
        return carry

    lax.fori_loop(0, n_kv, one_group, 0)
    if not up_refs:
        return

    facts_ref, act_ref, dq_before = before
    rank = act_ref.shape[0]
    n_quarters, per, _, part = up_refs[0].shape
    n_groups = per * len(up_refs)
    own = group_rows(rank, n_groups, tok, seq, by_slot) == facts_ref[2:3, :]
    act = jnp.concatenate([act_ref[...].astype(F32)] * n_groups, axis=0)
    act_cols = jnp.where(own, act, 0.0).astype(BF16)
    n_before = dq_before.shape[0] // part
    for quarter in range(n_quarters):
        i, dq_ref = (quarter, dq_before) if quarter < n_before else (quarter - n_before, dq_turned)
        up = dot(act_cols, dq_ref[i * part : (i + 1) * part, :], 1, 1).astype(BF16)
        for n in range(n_groups):
            up_refs[n // per][quarter, n % per] = up[n * rank : (n + 1) * rank, :]


def rank_kernel(by_slot, n_w, facts_ref, *refs):
    w_refs, (dq_a, dq_b, out_ref) = refs[:n_w], refs[n_w:]
    tok = dq_a.shape[1]
    seq, head = lax.axis_index("seq"), lax.axis_index("head")
    n_adapters, n_quarters, rank, part = w_refs[0].shape
    adapter = facts_ref[1:2, :]
    total = jnp.zeros((rank, tok), F32)
    n_a = dq_a.shape[0] // part
    for c, w_ref in enumerate(w_refs):
        rows = None
        for quarter in range(n_quarters):
            j = lax.rem(head + n_quarters - quarter, n_quarters) if by_slot else quarter
            i, dq_ref = (quarter, dq_a) if quarter < n_a else (quarter - n_a, dq_b)
            dq = dq_ref[i * part : (i + 1) * part, :]
            new = dot(w_ref[:, j].reshape(n_adapters * rank, part), dq, 1, 0)
            rows = new if rows is None else rows + new
        for m in range(n_adapters):
            a = (2 * m + c) ^ seq if by_slot else m
            total = total + jnp.where(adapter == a, rows[m * rank : (m + 1) * rank, :], 0.0)
    out_ref[...] = total.astype(BF16)


def down_kernel(by_slot, facts_ref, x_ref, rank_ref, *out_refs):
    rank, tok = rank_ref.shape
    seq, head = lax.axis_index("seq"), lax.axis_index("head")
    per, n_quarters, _, x_part = out_refs[0].shape
    n_groups = per * len(out_refs)
    own = group_rows(rank, n_groups, tok, seq, by_slot) == facts_ref[2:3, :]
    low = jnp.concatenate([rank_ref[...].astype(F32)] * n_groups, axis=0)
    cols = jnp.where(own, low, 0.0).astype(BF16)
    step = min(512, x_part)
    for j in range(n_quarters):
        quarter = lax.rem(head + j, n_quarters) if by_slot else j
        for start in range(0, x_part, step):
            at = pl.ds(pl.multiple_of(quarter * x_part + start, step), step)
            down = dot(cols, x_ref[:, at], 1, 0).astype(BF16)
            for n in range(n_groups):
                piece = down[n * rank : (n + 1) * rank, :]
                out_refs[n // per][n % per, j, :, start : start + step] = piece


def sum_kernel(a_ref, b_ref, *out_refs):
    for i, out_ref in enumerate(out_refs):
        out_ref[...] = (a_ref[i].astype(F32) + b_ref[i].astype(F32)).astype(BF16)


def token_facts(tok, lengths, adapters, owner, by_slot):
    n_seg = lengths.shape[0]
    order = jnp.arange(n_seg, dtype=I32)
    starts = jnp.sum(jnp.where(order[None, :] < order[:, None], lengths[None, :], 0), axis=1)
    if by_slot:
        hits = adapters[:, None] == jnp.arange(owner.shape[0], dtype=I32)[None, :]
        groups = jnp.sum(jnp.where(hits, owner[None, :], 0), axis=1)
    else:
        groups = order
    position = lax.axis_index("head") * tok + jnp.arange(tok, dtype=I32)
    inside = (position >= starts[:, None]) & (position < (starts + lengths)[:, None])
    told = jnp.stack([starts, adapters, groups] + [jnp.zeros_like(starts)] * 5)
    return jnp.sum(jnp.where(inside[None], told[:, :, None], 0), axis=1)


def shifted(x, n_head, j):
    return lax.ppermute(x, "head", [(i, (i + j) % n_head) for i in range(n_head)])


def partnered(x, n_seq, bits):
    return lax.ppermute(x, "seq", [(i, i ^ bits) for i in range(n_seq)])


def on_device(
    queries, keys, values, output_gradient, inputs, adapter_activation,
    adapter_up_weight, segment_length, segment_adapter, owner,
):
    n_head = lax.axis_size("head")
    n_seq = lax.axis_size("seq")
    tok, width = queries.shape
    pack = tok * n_head
    rank = adapter_up_weight.shape[1]
    n_adapters = owner.shape[0]
    n_seg = segment_length.shape[1]
    by_slot = n_adapters == n_seq == 8
    facts = token_facts(tok, segment_length[0], segment_adapter[0], owner, by_slot)

    reach = []
    while sum(reach) < pack * 3 // 8:
        reach.append(min(pack * 3 // 8 - sum(reach), tok))
    key_rows = tok + sum(reach)
    own = jnp.concatenate([keys, values], axis=1)
    parts = [own]
    for hop, rows in enumerate(reach, 1):
        shift = [(i, i + hop) for i in range(n_head - hop)]
        parts.insert(0, lax.ppermute(own[tok - rows :], "head", shift))

    if by_slot:
        w = [adapter_up_weight] + [shifted(adapter_up_weight, n_head, j) for j in range(1, n_head)]
        w = jnp.concatenate(w, axis=0)[None]
        w = [w] + [partnered(w, n_seq, 2 * m) for m in range(1, n_seq // 2)]
    else:
        w = lax.all_gather(adapter_up_weight, "seq", axis=0, tiled=True)
        up_weight = [lax.all_gather(w, "head", axis=1, tiled=False)]

    n_out = 2 if by_slot else 1
    n_groups = n_seq if by_slot else n_seg
    part = width // n_head
    x_part = inputs.shape[1] // n_head
    params = pltpu.CompilerParams(vmem_limit_bytes=32 * 2**20)

    laid_out = pl.pallas_call(
        functools.partial(layout_kernel, len(parts)),
        out_shape=[
            jax.ShapeDtypeStruct((key_rows, keys.shape[1]), BF16),
            jax.ShapeDtypeStruct((key_rows, keys.shape[1]), BF16),
            jax.ShapeDtypeStruct((keys.shape[1], key_rows), BF16),
            jax.ShapeDtypeStruct((key_rows, tok), F32),
        ],
        in_specs=[VMEM] * (2 + len(parts)),
        out_specs=[VMEM] * 4,
        compiler_params=params,
        cost_estimate=pl.CostEstimate(
            flops=0, bytes_accessed=LAYOUT_BYTES, transcendentals=0
        ),
        name="layout",
    )(facts, keys.T, *parts)
    halves = 2
    n_kv = KEY_VALUE_HEADS // halves
    half = width // halves

    def attention(h, before, up_shapes):
        return pl.pallas_call(
            functools.partial(attention_kernel, by_slot, h * n_kv, n_kv),
            out_shape=[jax.ShapeDtypeStruct((half, tok), BF16)] + up_shapes,
            in_specs=[VMEM] * 4 + [ANY] * 2 + [VMEM] * len(before),
            out_specs=[VMEM] * (1 + len(up_shapes)),
            scratch_shapes=[
                pltpu.VMEM((tok, half), BF16),
                pltpu.VMEM((tok, half), BF16),
                pltpu.SemaphoreType.DMA((n_kv,)),
                pltpu.SemaphoreType.DMA((n_kv,)),
            ],
            compiler_params=params,
            cost_estimate=pl.CostEstimate(
                flops=2 * tok * half * key_rows * 3,
                bytes_accessed=4 * tok * half * 2,
                transcendentals=tok * key_rows * QUERY_HEADS // halves,
            ),
            name="attention_%d" % h,
        )(*laid_out, queries, output_gradient, *before)

    (dq_a,) = attention(0, [], [])
    if by_slot:
        dq_a, w = lax.optimization_barrier((dq_a, w))
        w = jnp.concatenate(w, axis=0)
        up_weight = [w, partnered(w, n_seq, 1)]
    up_shape = jax.ShapeDtypeStruct((n_head, n_groups // n_out, rank, part), BF16)
    dq_b, *up = attention(1, [facts, adapter_activation.T, dq_a], [up_shape] * n_out)

    if by_slot:
        up, up_weight = lax.optimization_barrier((up, up_weight))
    rank_low = pl.pallas_call(
        functools.partial(rank_kernel, by_slot, len(up_weight)),
        out_shape=jax.ShapeDtypeStruct((rank, tok), BF16),
        in_specs=[VMEM] * (3 + len(up_weight)),
        out_specs=VMEM,
        compiler_params=params,
        name="rank_gradient",
    )(facts, *up_weight, dq_a, dq_b)

    down_shape = jax.ShapeDtypeStruct((n_groups // n_out, n_head, rank, x_part), BF16)
    down = pl.pallas_call(
        functools.partial(down_kernel, by_slot),
        out_shape=[down_shape] * n_out,
        in_specs=[VMEM] * 3,
        out_specs=[VMEM] * n_out,
        compiler_params=params,
        cost_estimate=pl.CostEstimate(
            flops=2 * n_groups * rank * tok * inputs.shape[1],
            bytes_accessed=4 * tok * inputs.shape[1] * 2,
            transcendentals=0,
        ),
        name="down_parts",
    )(facts, inputs, rank_low)

    if by_slot:
        down = pl.pallas_call(
            sum_kernel,
            out_shape=[jax.ShapeDtypeStruct(down[0].shape[1:], BF16)] * down[0].shape[0],
            in_specs=[VMEM] * 2,
            out_specs=[VMEM] * down[0].shape[0],
            compiler_params=params,
            cost_estimate=pl.CostEstimate(flops=0, bytes_accessed=SUM_BYTES, transcendentals=0),
            name="core_sum",
        )(down[0], partnered(down[1], n_seq, 1))
        up = lax.all_to_all(over_cores(up, n_seq), "head", split_axis=0, concat_axis=0, tiled=True)
        up = over_chips(jnp.sum(up.astype(F32), axis=0).astype(BF16), n_seq)
        down = over_z(over_chips(down, n_seq).astype(BF16), n_head)
    else:
        up = lax.all_to_all(up[0], "head", split_axis=0, concat_axis=0, tiled=True)
        up = spread(jnp.sum(up.astype(F32), axis=0), segment_adapter, owner, n_seq)
        down = lax.all_to_all(down[0], "head", split_axis=1, concat_axis=1, tiled=True)
        down = spread(jnp.sum(down.astype(F32), axis=1), segment_adapter, owner, n_seq)
    return down.T[None] * ADAPTER_SCALE, up[None] * ADAPTER_SCALE


def over_cores(parts, n_seq):
    keep, send = parts
    return (keep.astype(F32) + partnered(send, n_seq, 1).astype(F32)).astype(BF16)


def added(own, got):
    total = own.astype(F32)
    for piece in got:
        total = total + piece.astype(F32)
    return total


def over_chips(both, n_seq):
    return added(both[0], [partnered(both[m], n_seq, 2 * m) for m in range(1, n_seq // 2)])


def over_z(both, n_head):
    return added(both[0], [shifted(both[j], n_head, j) for j in range(1, n_head)])


def spread(part, segment_adapter, owner, n_seq):
    goes_to = owner[segment_adapter[0]]
    slots = (goes_to[:, None] == jnp.arange(n_seq, dtype=I32)[None, :]).astype(F32)
    slotted = jnp.einsum("srw,so->orw", part, slots, precision=lax.Precision.HIGHEST)
    slotted = lax.all_to_all(slotted.astype(BF16), "seq", split_axis=0, concat_axis=0, tiled=True)
    return jnp.sum(slotted.astype(F32), axis=0)


def solution(mesh):
    return jax.shard_map(
        on_device,
        mesh=mesh,
        in_specs=(
            P(("seq", "head"), None),
            P(("seq", "head"), None),
            P(("seq", "head"), None),
            P(("seq", "head"), None),
            P(("seq", "head"), None),
            P(("seq", "head"), None),
            P("seq", None, "head"),
            P("seq", None),
            P("seq", None),
            P(),
        ),
        out_specs=(P("seq", "head", None), P("seq", None, "head")),
        check_vma=False,
    )
```

```python
import functools
import math

import jax
import jax.numpy as jnp
from jax import lax
from jax.experimental import pallas as pl
from jax.experimental.pallas import tpu as pltpu
from jax.sharding import PartitionSpec as P

QUERY_HEADS = 32
KEY_VALUE_HEADS = 4
HEAD_SIZE = 128
GROUP = QUERY_HEADS // KEY_VALUE_HEADS
ADAPTER_SCALE = 2.0
NEVER = -1e30
LAYOUT_BYTES = 16 * 2**20
SUM_BYTES = 16 * 2**20
BF16 = jnp.bfloat16
F32 = jnp.float32
I32 = jnp.int32
VMEM = pl.BlockSpec(memory_space=pltpu.VMEM)
ANY = pl.BlockSpec(memory_space=pl.ANY)


def dot(a, b, a_dim, b_dim):
    return lax.dot_general(a, b, (((a_dim,), (b_dim,)), ((), ())), preferred_element_type=F32)


def group_rows(rows_of_group, n_groups, width, seq, by_slot):
    row = lax.broadcasted_iota(I32, (n_groups * rows_of_group, width), 0) // rows_of_group
    if by_slot:
        half = n_groups // 2
        row = jnp.where(row < half, row * 2, (row - half) * 2 + 1) ^ seq
    return row


def layout_kernel(n_parts, facts_ref, *refs):
    own_turned, *parts = refs[: n_parts + 1]
    k_all, v_all, k_turned, bias = refs[n_parts + 1 :]
    tok = facts_ref.shape[1]
    kv_width = v_all.shape[1]
    key_rows = v_all.shape[0]
    head = lax.axis_index("head")
    position = head * tok + lax.broadcasted_iota(I32, (1, tok), 1)
    key_position = (
        head * tok - (key_rows - tok) + lax.broadcasted_iota(I32, (key_rows, tok), 0)
    )
    allowed = (key_position >= facts_ref[0:1, :]) & (key_position <= position)
    bias[...] = jnp.where(allowed, 0.0, NEVER)
    for kv in range(KEY_VALUE_HEADS):
        start = 0
        at = slice(kv * HEAD_SIZE, (kv + 1) * HEAD_SIZE)
        for part in parts:
            rows = part.shape[0]
            k_all[start : start + rows, at] = part[:, at]
            v_all[start : start + rows, at] = part[:, kv_width + at.start : kv_width + at.stop]
            start += rows
        k_turned[at, : start - tok] = k_all[: start - tok, at].T
        k_turned[at, start - tok :] = own_turned[at, :]


def attention_kernel(by_slot, first_kv, n_kv, k_all, v_all, k_turned, bias, q_hbm, g_hbm, *refs):
    before, refs = (refs[:3], refs[3:]) if first_kv else ((), refs)
    dq_turned, *up_refs, q_ref, g_ref, q_sem, g_sem = refs
    tok = q_ref.shape[0]
    seq, head = lax.axis_index("seq"), lax.axis_index("head")
    per_kv = GROUP * HEAD_SIZE

    def fetch(kv):
        to = pl.ds(kv * per_kv, per_kv)
        at = pl.ds((first_kv + kv) * per_kv, per_kv)
        return (
            pltpu.make_async_copy(q_hbm.at[:, at], q_ref.at[:, to], q_sem.at[kv]),
            pltpu.make_async_copy(g_hbm.at[:, at], g_ref.at[:, to], g_sem.at[kv]),
        )

    for kv in range(n_kv):
        for copy in fetch(kv):
            copy.start()

    scale = 1.0 / HEAD_SIZE**0.5
    to_log2 = scale * math.log2(math.e)

    def one_group(kv, carry):
        for copy in fetch(kv):
            copy.wait()
        at_kv = pl.ds(pl.multiple_of((first_kv + kv) * HEAD_SIZE, HEAD_SIZE), HEAD_SIZE)
        k_g = k_all[:, at_kv]
        v_g = v_all[:, at_kv]
        kt_g = k_turned[at_kv, :]
        for i in range(0, GROUP, 2):
            first = (kv * GROUP + i) * HEAD_SIZE
            at = [
                pl.ds(pl.multiple_of(first + n * HEAD_SIZE, HEAD_SIZE), HEAD_SIZE) for n in range(2)
            ]
            q_two = jnp.concatenate([q_ref[:, at[0]], q_ref[:, at[1]]], axis=0)
            g_two = jnp.concatenate([g_ref[:, at[0]], g_ref[:, at[1]]], axis=0)
            s = dot(k_g, q_two, 1, 1) + jnp.concatenate([bias[...]] * 2, axis=1)
            d_prob = dot(v_g, g_two, 1, 1)
            weights = jnp.exp2((s - jnp.max(s, axis=0, keepdims=True)) * to_log2)
            inverse = 1.0 / jnp.sum(weights, axis=0, keepdims=True)
            delta = jnp.sum(weights * d_prob, axis=0, keepdims=True) * inverse
            dscore = (weights * (d_prob - delta)).astype(BF16)
            dq = dot(kt_g, dscore, 1, 0) * (inverse * scale)
            dq_turned[at[0], :] = dq[:, :tok].astype(BF16)
            dq_turned[at[1], :] = dq[:, tok:].astype(BF16)
        return carry

    lax.fori_loop(0, n_kv, one_group, 0)
    if not up_refs:
        return

    facts_ref, act_ref, dq_before = before
    rank = act_ref.shape[0]
    per, n_quarters, _, part = up_refs[0].shape
    n_groups = per * len(up_refs)
    own = group_rows(rank, n_groups, tok, seq, by_slot) == facts_ref[2:3, :]
    act = jnp.concatenate([act_ref[...].astype(F32)] * n_groups, axis=0)
    act_cols = jnp.where(own, act, 0.0).astype(BF16)
    n_before = dq_before.shape[0] // part
    for quarter in range(n_quarters):
        i, dq_ref = (quarter, dq_before) if quarter < n_before else (quarter - n_before, dq_turned)
        up = dot(act_cols, dq_ref[i * part : (i + 1) * part, :], 1, 1).astype(BF16)
        j = lax.rem(quarter + n_quarters - head, n_quarters) if by_slot else quarter
        for n in range(n_groups):
            up_refs[n // per][n % per, j] = up[n * rank : (n + 1) * rank, :]


def rank_kernel(by_slot, n_w, facts_ref, *refs):
    w_refs, (dq_a, dq_b, out_ref) = refs[:n_w], refs[n_w:]
    tok = dq_a.shape[1]
    seq, head = lax.axis_index("seq"), lax.axis_index("head")
    n_adapters, n_quarters, rank, part = w_refs[0].shape
    adapter = facts_ref[1:2, :]
    total = jnp.zeros((rank, tok), F32)
    n_a = dq_a.shape[0] // part
    for c, w_ref in enumerate(w_refs):
        rows = None
        for quarter in range(n_quarters):
            j = lax.rem(head + n_quarters - quarter, n_quarters) if by_slot else quarter
            i, dq_ref = (quarter, dq_a) if quarter < n_a else (quarter - n_a, dq_b)
            dq = dq_ref[i * part : (i + 1) * part, :]
            new = dot(w_ref[:, j].reshape(n_adapters * rank, part), dq, 1, 0)
            rows = new if rows is None else rows + new
        for m in range(n_adapters):
            a = (2 * m + c) ^ seq if by_slot else m
            total = total + jnp.where(adapter == a, rows[m * rank : (m + 1) * rank, :], 0.0)
    out_ref[...] = total.astype(BF16)


def down_kernel(by_slot, facts_ref, x_ref, rank_ref, *out_refs):
    rank, tok = rank_ref.shape
    seq, head = lax.axis_index("seq"), lax.axis_index("head")
    per, n_quarters, _, x_part = out_refs[0].shape
    n_groups = per * len(out_refs)
    own = group_rows(rank, n_groups, tok, seq, by_slot) == facts_ref[2:3, :]
    low = jnp.concatenate([rank_ref[...].astype(F32)] * n_groups, axis=0)
    cols = jnp.where(own, low, 0.0).astype(BF16)
    step = min(512, x_part)
    for j in range(n_quarters):
        quarter = lax.rem(head + j, n_quarters) if by_slot else j
        for start in range(0, x_part, step):
            at = pl.ds(pl.multiple_of(quarter * x_part + start, step), step)
            down = dot(cols, x_ref[:, at], 1, 0).astype(BF16)
            for n in range(n_groups):
                piece = down[n * rank : (n + 1) * rank, :]
                out_refs[n // per][n % per, j, :, start : start + step] = piece


def sum_kernel(a_ref, b_ref, *out_refs):
    for i, out_ref in enumerate(out_refs):
        out_ref[...] = (a_ref[i].astype(F32) + b_ref[i].astype(F32)).astype(BF16)


def token_facts(tok, lengths, adapters, owner, by_slot):
    n_seg = lengths.shape[0]
    order = jnp.arange(n_seg, dtype=I32)
    starts = jnp.sum(jnp.where(order[None, :] < order[:, None], lengths[None, :], 0), axis=1)
    if by_slot:
        hits = adapters[:, None] == jnp.arange(owner.shape[0], dtype=I32)[None, :]
        groups = jnp.sum(jnp.where(hits, owner[None, :], 0), axis=1)
    else:
        groups = order
    position = lax.axis_index("head") * tok + jnp.arange(tok, dtype=I32)
    inside = (position >= starts[:, None]) & (position < (starts + lengths)[:, None])
    told = jnp.stack([starts, adapters, groups] + [jnp.zeros_like(starts)] * 5)
    return jnp.sum(jnp.where(inside[None], told[:, :, None], 0), axis=1)


def shifted(x, n_head, j):
    return lax.ppermute(x, "head", [(i, (i + j) % n_head) for i in range(n_head)])


def partnered(x, n_seq, bits):
    return lax.ppermute(x, "seq", [(i, i ^ bits) for i in range(n_seq)])


def on_device(
    queries, keys, values, output_gradient, inputs, adapter_activation,
    adapter_up_weight, segment_length, segment_adapter, owner,
):
    n_head = lax.axis_size("head")
    n_seq = lax.axis_size("seq")
    tok, width = queries.shape
    pack = tok * n_head
    rank = adapter_up_weight.shape[1]
    n_adapters = owner.shape[0]
    n_seg = segment_length.shape[1]
    by_slot = n_adapters == n_seq == 8
    facts = token_facts(tok, segment_length[0], segment_adapter[0], owner, by_slot)

    reach = []
    while sum(reach) < pack * 3 // 8:
        reach.append(min(pack * 3 // 8 - sum(reach), tok))
    key_rows = tok + sum(reach)
    own = jnp.concatenate([keys, values], axis=1)
    parts = [own]
    for hop, rows in enumerate(reach, 1):
        shift = [(i, i + hop) for i in range(n_head - hop)]
        parts.insert(0, lax.ppermute(own[tok - rows :], "head", shift))

    if by_slot:
        w = [adapter_up_weight] + [shifted(adapter_up_weight, n_head, j) for j in range(1, n_head)]
        w = jnp.concatenate(w, axis=0)[None]
        w = [w] + [partnered(w, n_seq, 2 * m) for m in range(1, n_seq // 2)]
    else:
        w = lax.all_gather(adapter_up_weight, "seq", axis=0, tiled=True)
        up_weight = [lax.all_gather(w, "head", axis=1, tiled=False)]

    n_out = 2 if by_slot else 1
    n_groups = n_seq if by_slot else n_seg
    part = width // n_head
    x_part = inputs.shape[1] // n_head
    params = pltpu.CompilerParams(vmem_limit_bytes=32 * 2**20)

    laid_out = pl.pallas_call(
        functools.partial(layout_kernel, len(parts)),
        out_shape=[
            jax.ShapeDtypeStruct((key_rows, keys.shape[1]), BF16),
            jax.ShapeDtypeStruct((key_rows, keys.shape[1]), BF16),
            jax.ShapeDtypeStruct((keys.shape[1], key_rows), BF16),
            jax.ShapeDtypeStruct((key_rows, tok), F32),
        ],
        in_specs=[VMEM] * (2 + len(parts)),
        out_specs=[VMEM] * 4,
        compiler_params=params,
        cost_estimate=pl.CostEstimate(
            flops=0, bytes_accessed=LAYOUT_BYTES, transcendentals=0
        ),
        name="layout",
    )(facts, keys.T, *parts)
    halves = 2
    n_kv = KEY_VALUE_HEADS // halves
    half = width // halves

    def attention(h, before, up_shapes):
        return pl.pallas_call(
            functools.partial(attention_kernel, by_slot, h * n_kv, n_kv),
            out_shape=[jax.ShapeDtypeStruct((half, tok), BF16)] + up_shapes,
            in_specs=[VMEM] * 4 + [ANY] * 2 + [VMEM] * len(before),
            out_specs=[VMEM] * (1 + len(up_shapes)),
            scratch_shapes=[
                pltpu.VMEM((tok, half), BF16),
                pltpu.VMEM((tok, half), BF16),
                pltpu.SemaphoreType.DMA((n_kv,)),
                pltpu.SemaphoreType.DMA((n_kv,)),
            ],
            compiler_params=params,
            cost_estimate=pl.CostEstimate(
                flops=2 * tok * half * key_rows * 3,
                bytes_accessed=4 * tok * half * 2,
                transcendentals=tok * key_rows * QUERY_HEADS // halves,
            ),
            name="attention_%d" % h,
        )(*laid_out, queries, output_gradient, *before)

    (dq_a,) = attention(0, [], [])
    if by_slot:
        dq_a, w = lax.optimization_barrier((dq_a, w))
        w = jnp.concatenate(w, axis=0)
        up_weight = [w, partnered(w, n_seq, 1)]
    up_shape = jax.ShapeDtypeStruct((n_groups // n_out, n_head, rank, part), BF16)
    dq_b, *up = attention(1, [facts, adapter_activation.T, dq_a], [up_shape] * n_out)

    if by_slot:
        up, up_weight = lax.optimization_barrier((up, up_weight))
    rank_low = pl.pallas_call(
        functools.partial(rank_kernel, by_slot, len(up_weight)),
        out_shape=jax.ShapeDtypeStruct((rank, tok), BF16),
        in_specs=[VMEM] * (3 + len(up_weight)),
        out_specs=VMEM,
        compiler_params=params,
        name="rank_gradient",
    )(facts, *up_weight, dq_a, dq_b)

    down_shape = jax.ShapeDtypeStruct((n_groups // n_out, n_head, rank, x_part), BF16)
    down = pl.pallas_call(
        functools.partial(down_kernel, by_slot),
        out_shape=[down_shape] * n_out,
        in_specs=[VMEM] * 3,
        out_specs=[VMEM] * n_out,
        compiler_params=params,
        cost_estimate=pl.CostEstimate(
            flops=2 * n_groups * rank * tok * inputs.shape[1],
            bytes_accessed=4 * tok * inputs.shape[1] * 2,
            transcendentals=0,
        ),
        name="down_parts",
    )(facts, inputs, rank_low)

    if by_slot:
        down = pl.pallas_call(
            sum_kernel,
            out_shape=[jax.ShapeDtypeStruct(down[0].shape[1:], BF16)] * down[0].shape[0],
            in_specs=[VMEM] * 2,
            out_specs=[VMEM] * down[0].shape[0],
            compiler_params=params,
            cost_estimate=pl.CostEstimate(flops=0, bytes_accessed=SUM_BYTES, transcendentals=0),
            name="core_sum",
        )(down[0], partnered(down[1], n_seq, 1))
        up = over_z(over_chips(over_cores(up, n_seq), n_seq).astype(BF16), n_head)
        down = over_z(over_chips(down, n_seq).astype(BF16), n_head)
    else:
        up = lax.all_to_all(up[0], "head", split_axis=1, concat_axis=1, tiled=True)
        up = spread(jnp.sum(up.astype(F32), axis=1), segment_adapter, owner, n_seq)
        down = lax.all_to_all(down[0], "head", split_axis=1, concat_axis=1, tiled=True)
        down = spread(jnp.sum(down.astype(F32), axis=1), segment_adapter, owner, n_seq)
    return down.T[None] * ADAPTER_SCALE, up[None] * ADAPTER_SCALE


def over_cores(parts, n_seq):
    keep, send = parts
    return (keep.astype(F32) + partnered(send, n_seq, 1).astype(F32)).astype(BF16)


def added(own, got):
    total = own.astype(F32)
    for piece in got:
        total = total + piece.astype(F32)
    return total


def over_chips(both, n_seq):
    return added(both[0], [partnered(both[m], n_seq, 2 * m) for m in range(1, n_seq // 2)])


def over_z(both, n_head):
    return added(both[0], [shifted(both[j], n_head, j) for j in range(1, n_head)])


def spread(part, segment_adapter, owner, n_seq):
    goes_to = owner[segment_adapter[0]]
    slots = (goes_to[:, None] == jnp.arange(n_seq, dtype=I32)[None, :]).astype(F32)
    slotted = jnp.einsum("srw,so->orw", part, slots, precision=lax.Precision.HIGHEST)
    slotted = lax.all_to_all(slotted.astype(BF16), "seq", split_axis=0, concat_axis=0, tiled=True)
    return jnp.sum(slotted.astype(F32), axis=0)


def solution(mesh):
    return jax.shard_map(
        on_device,
        mesh=mesh,
        in_specs=(
            P(("seq", "head"), None),
            P(("seq", "head"), None),
            P(("seq", "head"), None),
            P(("seq", "head"), None),
            P(("seq", "head"), None),
            P(("seq", "head"), None),
            P("seq", None, "head"),
            P("seq", None),
            P("seq", None),
            P(),
        ),
        out_specs=(P("seq", "head", None), P("seq", None, "head")),
        check_vma=False,
    )
```

```python
import functools
import math

import jax
import jax.numpy as jnp
from jax import lax
from jax.experimental import pallas as pl
from jax.experimental.pallas import tpu as pltpu
from jax.sharding import PartitionSpec as P

QUERY_HEADS = 32
KEY_VALUE_HEADS = 4
HEAD_SIZE = 128
GROUP = QUERY_HEADS // KEY_VALUE_HEADS
ADAPTER_SCALE = 2.0
NEVER = -1e30
LAYOUT_BYTES = 16 * 2**20
SUM_BYTES = 16 * 2**20
BF16 = jnp.bfloat16
F32 = jnp.float32
I32 = jnp.int32
VMEM = pl.BlockSpec(memory_space=pltpu.VMEM)
ANY = pl.BlockSpec(memory_space=pl.ANY)


def dot(a, b, a_dim, b_dim):
    return lax.dot_general(a, b, (((a_dim,), (b_dim,)), ((), ())), preferred_element_type=F32)


def group_rows(rows_of_group, n_groups, width, seq, by_slot):
    row = lax.broadcasted_iota(I32, (n_groups * rows_of_group, width), 0) // rows_of_group
    if by_slot:
        half = n_groups // 2
        row = jnp.where(row < half, row * 2, (row - half) * 2 + 1) ^ seq
    return row


def layout_kernel(n_parts, facts_ref, *refs):
    own_turned, *parts = refs[: n_parts + 1]
    k_all, v_all, k_turned, bias = refs[n_parts + 1 :]
    tok = facts_ref.shape[1]
    kv_width = v_all.shape[1]
    key_rows = v_all.shape[0]
    head = lax.axis_index("head")
    position = head * tok + lax.broadcasted_iota(I32, (1, tok), 1)
    key_position = (
        head * tok - (key_rows - tok) + lax.broadcasted_iota(I32, (key_rows, tok), 0)
    )
    allowed = (key_position >= facts_ref[0:1, :]) & (key_position <= position)
    bias[...] = jnp.where(allowed, 0.0, NEVER)
    for kv in range(KEY_VALUE_HEADS):
        start = 0
        at = slice(kv * HEAD_SIZE, (kv + 1) * HEAD_SIZE)
        for part in parts:
            rows = part.shape[0]
            k_all[start : start + rows, at] = part[:, at]
            v_all[start : start + rows, at] = part[:, kv_width + at.start : kv_width + at.stop]
            start += rows
        k_turned[at, : start - tok] = k_all[: start - tok, at].T
        k_turned[at, start - tok :] = own_turned[at, :]


def attention_kernel(by_slot, first_kv, n_kv, k_all, v_all, k_turned, bias, q_hbm, g_hbm, *refs):
    before, refs = (refs[:3], refs[3:]) if first_kv else ((), refs)
    dq_turned, *up_refs, q_ref, g_ref, q_sem, g_sem = refs
    tok = q_ref.shape[0]
    seq, head = lax.axis_index("seq"), lax.axis_index("head")
    per_kv = GROUP * HEAD_SIZE

    def fetch(kv):
        to = pl.ds(kv * per_kv, per_kv)
        at = pl.ds((first_kv + kv) * per_kv, per_kv)
        return (
            pltpu.make_async_copy(q_hbm.at[:, at], q_ref.at[:, to], q_sem.at[kv]),
            pltpu.make_async_copy(g_hbm.at[:, at], g_ref.at[:, to], g_sem.at[kv]),
        )

    for kv in range(n_kv):
        for copy in fetch(kv):
            copy.start()

    scale = 1.0 / HEAD_SIZE**0.5
    to_log2 = scale * math.log2(math.e)

    def one_group(kv, carry):
        for copy in fetch(kv):
            copy.wait()
        at_kv = pl.ds(pl.multiple_of((first_kv + kv) * HEAD_SIZE, HEAD_SIZE), HEAD_SIZE)
        k_g = k_all[:, at_kv]
        v_g = v_all[:, at_kv]
        kt_g = k_turned[at_kv, :]
        for i in range(0, GROUP, 2):
            first = (kv * GROUP + i) * HEAD_SIZE
            at = [
                pl.ds(pl.multiple_of(first + n * HEAD_SIZE, HEAD_SIZE), HEAD_SIZE) for n in range(2)
            ]
            q_two = jnp.concatenate([q_ref[:, at[0]], q_ref[:, at[1]]], axis=0)
            g_two = jnp.concatenate([g_ref[:, at[0]], g_ref[:, at[1]]], axis=0)
            s = dot(k_g, q_two, 1, 1) + jnp.concatenate([bias[...]] * 2, axis=1)
            d_prob = dot(v_g, g_two, 1, 1)
            weights = jnp.exp2((s - jnp.max(s, axis=0, keepdims=True)) * to_log2)
            inverse = 1.0 / jnp.sum(weights, axis=0, keepdims=True)
            delta = jnp.sum(weights * d_prob, axis=0, keepdims=True) * inverse
            dscore = (weights * (d_prob - delta)).astype(BF16)
            dq = dot(kt_g, dscore, 1, 0) * (inverse * scale)
            dq_turned[at[0], :] = dq[:, :tok].astype(BF16)
            dq_turned[at[1], :] = dq[:, tok:].astype(BF16)
        return carry

    lax.fori_loop(0, n_kv, one_group, 0)
    if not up_refs:
        return

    facts_ref, act_ref, dq_before = before
    rank = act_ref.shape[0]
    n_quarters, per, _, part = up_refs[0].shape
    n_groups = per * len(up_refs)
    own = group_rows(rank, n_groups, tok, seq, by_slot) == facts_ref[2:3, :]
    act = jnp.concatenate([act_ref[...].astype(F32)] * n_groups, axis=0)
    act_cols = jnp.where(own, act, 0.0).astype(BF16)
    n_before = dq_before.shape[0] // part
    for quarter in range(n_quarters):
        i, dq_ref = (quarter, dq_before) if quarter < n_before else (quarter - n_before, dq_turned)
        up = dot(act_cols, dq_ref[i * part : (i + 1) * part, :], 1, 1).astype(BF16)
        j = head ^ quarter if by_slot else quarter
        for n in range(n_groups):
            up_refs[n // per][j, n % per] = up[n * rank : (n + 1) * rank, :]


def rank_kernel(by_slot, n_w, facts_ref, *refs):
    w_refs, (dq_a, dq_b, out_ref) = refs[:n_w], refs[n_w:]
    tok = dq_a.shape[1]
    seq, head = lax.axis_index("seq"), lax.axis_index("head")
    n_adapters, n_quarters, rank, part = w_refs[0].shape
    adapter = facts_ref[1:2, :]
    total = jnp.zeros((rank, tok), F32)
    n_a = dq_a.shape[0] // part
    for c, w_ref in enumerate(w_refs):
        rows = None
        for quarter in range(n_quarters):
            j = head ^ quarter if by_slot else quarter
            i, dq_ref = (quarter, dq_a) if quarter < n_a else (quarter - n_a, dq_b)
            dq = dq_ref[i * part : (i + 1) * part, :]
            new = dot(w_ref[:, j].reshape(n_adapters * rank, part), dq, 1, 0)
            rows = new if rows is None else rows + new
        for m in range(n_adapters):
            a = (2 * m + c) ^ seq if by_slot else m
            total = total + jnp.where(adapter == a, rows[m * rank : (m + 1) * rank, :], 0.0)
    out_ref[...] = total.astype(BF16)


def down_kernel(by_slot, facts_ref, x_ref, rank_ref, *out_refs):
    rank, tok = rank_ref.shape
    seq, head = lax.axis_index("seq"), lax.axis_index("head")
    per, n_quarters, _, x_part = out_refs[0].shape
    n_groups = per * len(out_refs)
    own = group_rows(rank, n_groups, tok, seq, by_slot) == facts_ref[2:3, :]
    low = jnp.concatenate([rank_ref[...].astype(F32)] * n_groups, axis=0)
    cols = jnp.where(own, low, 0.0).astype(BF16)
    step = min(512, x_part)
    for j in range(n_quarters):
        quarter = head ^ j if by_slot else j
        for start in range(0, x_part, step):
            at = pl.ds(pl.multiple_of(quarter * x_part + start, step), step)
            down = dot(cols, x_ref[:, at], 1, 0).astype(BF16)
            for n in range(n_groups):
                piece = down[n * rank : (n + 1) * rank, :]
                out_refs[n // per][n % per, j, :, start : start + step] = piece


def sum_kernel(a_ref, b_ref, *out_refs):
    for i, out_ref in enumerate(out_refs):
        out_ref[...] = (a_ref[i].astype(F32) + b_ref[i].astype(F32)).astype(BF16)


def token_facts(tok, lengths, adapters, owner, by_slot):
    n_seg = lengths.shape[0]
    order = jnp.arange(n_seg, dtype=I32)
    starts = jnp.sum(jnp.where(order[None, :] < order[:, None], lengths[None, :], 0), axis=1)
    if by_slot:
        hits = adapters[:, None] == jnp.arange(owner.shape[0], dtype=I32)[None, :]
        groups = jnp.sum(jnp.where(hits, owner[None, :], 0), axis=1)
    else:
        groups = order
    position = lax.axis_index("head") * tok + jnp.arange(tok, dtype=I32)
    inside = (position >= starts[:, None]) & (position < (starts + lengths)[:, None])
    told = jnp.stack([starts, adapters, groups] + [jnp.zeros_like(starts)] * 5)
    return jnp.sum(jnp.where(inside[None], told[:, :, None], 0), axis=1)


def across(x, n_head, j):
    return lax.ppermute(x, "head", [(i, i ^ j) for i in range(n_head)])


def partnered(x, n_seq, bits):
    return lax.ppermute(x, "seq", [(i, i ^ bits) for i in range(n_seq)])


def on_device(
    queries, keys, values, output_gradient, inputs, adapter_activation,
    adapter_up_weight, segment_length, segment_adapter, owner,
):
    n_head = lax.axis_size("head")
    n_seq = lax.axis_size("seq")
    tok, width = queries.shape
    pack = tok * n_head
    rank = adapter_up_weight.shape[1]
    n_adapters = owner.shape[0]
    n_seg = segment_length.shape[1]
    by_slot = n_adapters == n_seq == 8 and n_head == 4
    facts = token_facts(tok, segment_length[0], segment_adapter[0], owner, by_slot)

    reach = []
    while sum(reach) < pack * 3 // 8:
        reach.append(min(pack * 3 // 8 - sum(reach), tok))
    key_rows = tok + sum(reach)
    own = jnp.concatenate([keys, values], axis=1)
    parts = [own]
    for hop, rows in enumerate(reach, 1):
        shift = [(i, i + hop) for i in range(n_head - hop)]
        parts.insert(0, lax.ppermute(own[tok - rows :], "head", shift))

    if by_slot:
        w = [adapter_up_weight] + [across(adapter_up_weight, n_head, j) for j in range(1, n_head)]
        w = jnp.concatenate(w, axis=0)[None]
        w = [w] + [partnered(w, n_seq, 2 * m) for m in range(1, n_seq // 2)]
    else:
        w = lax.all_gather(adapter_up_weight, "seq", axis=0, tiled=True)
        up_weight = [lax.all_gather(w, "head", axis=1, tiled=False)]

    n_out = 2 if by_slot else 1
    n_groups = n_seq if by_slot else n_seg
    part = width // n_head
    x_part = inputs.shape[1] // n_head
    params = pltpu.CompilerParams(vmem_limit_bytes=32 * 2**20)

    laid_out = pl.pallas_call(
        functools.partial(layout_kernel, len(parts)),
        out_shape=[
            jax.ShapeDtypeStruct((key_rows, keys.shape[1]), BF16),
            jax.ShapeDtypeStruct((key_rows, keys.shape[1]), BF16),
            jax.ShapeDtypeStruct((keys.shape[1], key_rows), BF16),
            jax.ShapeDtypeStruct((key_rows, tok), F32),
        ],
        in_specs=[VMEM] * (2 + len(parts)),
        out_specs=[VMEM] * 4,
        compiler_params=params,
        cost_estimate=pl.CostEstimate(
            flops=0, bytes_accessed=LAYOUT_BYTES, transcendentals=0
        ),
        name="layout",
    )(facts, keys.T, *parts)
    halves = 2
    n_kv = KEY_VALUE_HEADS // halves
    half = width // halves

    def attention(h, before, up_shapes):
        return pl.pallas_call(
            functools.partial(attention_kernel, by_slot, h * n_kv, n_kv),
            out_shape=[jax.ShapeDtypeStruct((half, tok), BF16)] + up_shapes,
            in_specs=[VMEM] * 4 + [ANY] * 2 + [VMEM] * len(before),
            out_specs=[VMEM] * (1 + len(up_shapes)),
            scratch_shapes=[
                pltpu.VMEM((tok, half), BF16),
                pltpu.VMEM((tok, half), BF16),
                pltpu.SemaphoreType.DMA((n_kv,)),
                pltpu.SemaphoreType.DMA((n_kv,)),
            ],
            compiler_params=params,
            cost_estimate=pl.CostEstimate(
                flops=2 * tok * half * key_rows * 3,
                bytes_accessed=4 * tok * half * 2,
                transcendentals=tok * key_rows * QUERY_HEADS // halves,
            ),
            name="attention_%d" % h,
        )(*laid_out, queries, output_gradient, *before)

    (dq_a,) = attention(0, [], [])
    if by_slot:
        dq_a, w = lax.optimization_barrier((dq_a, w))
        w = jnp.concatenate(w, axis=0)
        up_weight = [w, partnered(w, n_seq, 1)]
    up_shape = jax.ShapeDtypeStruct((n_head, n_groups // n_out, rank, part), BF16)
    dq_b, *up = attention(1, [facts, adapter_activation.T, dq_a], [up_shape] * n_out)

    if by_slot:
        up, up_weight = lax.optimization_barrier((up, up_weight))
    rank_low = pl.pallas_call(
        functools.partial(rank_kernel, by_slot, len(up_weight)),
        out_shape=jax.ShapeDtypeStruct((rank, tok), BF16),
        in_specs=[VMEM] * (3 + len(up_weight)),
        out_specs=VMEM,
        compiler_params=params,
        name="rank_gradient",
    )(facts, *up_weight, dq_a, dq_b)

    down_shape = jax.ShapeDtypeStruct((n_groups // n_out, n_head, rank, x_part), BF16)
    down = pl.pallas_call(
        functools.partial(down_kernel, by_slot),
        out_shape=[down_shape] * n_out,
        in_specs=[VMEM] * 3,
        out_specs=[VMEM] * n_out,
        compiler_params=params,
        cost_estimate=pl.CostEstimate(
            flops=2 * n_groups * rank * tok * inputs.shape[1],
            bytes_accessed=4 * tok * inputs.shape[1] * 2,
            transcendentals=0,
        ),
        name="down_parts",
    )(facts, inputs, rank_low)

    if by_slot:
        down = pl.pallas_call(
            sum_kernel,
            out_shape=[jax.ShapeDtypeStruct(down[0].shape[1:], BF16)] * down[0].shape[0],
            in_specs=[VMEM] * 2,
            out_specs=[VMEM] * down[0].shape[0],
            compiler_params=params,
            cost_estimate=pl.CostEstimate(flops=0, bytes_accessed=SUM_BYTES, transcendentals=0),
            name="core_sum",
        )(down[0], partnered(down[1], n_seq, 1))
        up = over_chips(over_z(over_cores(up, n_seq), n_head).astype(BF16), n_seq)
        down = over_z(over_chips(down, n_seq).astype(BF16), n_head)
    else:
        up = lax.all_to_all(up[0], "head", split_axis=0, concat_axis=0, tiled=True)
        up = spread(jnp.sum(up.astype(F32), axis=0), segment_adapter, owner, n_seq)
        down = lax.all_to_all(down[0], "head", split_axis=1, concat_axis=1, tiled=True)
        down = spread(jnp.sum(down.astype(F32), axis=1), segment_adapter, owner, n_seq)
    return down.T[None] * ADAPTER_SCALE, up[None] * ADAPTER_SCALE


def over_cores(parts, n_seq):
    keep, send = parts
    return (keep.astype(F32) + partnered(send, n_seq, 1).astype(F32)).astype(BF16)


def added(own, got):
    total = own.astype(F32)
    for piece in got:
        total = total + piece.astype(F32)
    return total


def over_chips(both, n_seq):
    return added(both[0], [partnered(both[m], n_seq, 2 * m) for m in range(1, n_seq // 2)])


def over_z(both, n_head):
    return added(both[0], [across(both[j], n_head, j) for j in range(1, n_head)])


def spread(part, segment_adapter, owner, n_seq):
    goes_to = owner[segment_adapter[0]]
    slots = (goes_to[:, None] == jnp.arange(n_seq, dtype=I32)[None, :]).astype(F32)
    slotted = jnp.einsum("srw,so->orw", part, slots, precision=lax.Precision.HIGHEST)
    slotted = lax.all_to_all(slotted.astype(BF16), "seq", split_axis=0, concat_axis=0, tiled=True)
    return jnp.sum(slotted.astype(F32), axis=0)


def solution(mesh):
    return jax.shard_map(
        on_device,
        mesh=mesh,
        in_specs=(
            P(("seq", "head"), None),
            P(("seq", "head"), None),
            P(("seq", "head"), None),
            P(("seq", "head"), None),
            P(("seq", "head"), None),
            P(("seq", "head"), None),
            P("seq", None, "head"),
            P("seq", None),
            P("seq", None),
            P(),
        ),
        out_specs=(P("seq", "head", None), P("seq", None, "head")),
        check_vma=False,
    )
```

```python
import functools
import math

import jax
import jax.numpy as jnp
from jax import lax
from jax.experimental import pallas as pl
from jax.experimental.pallas import tpu as pltpu
from jax.sharding import PartitionSpec as P

QUERY_HEADS = 32
KEY_VALUE_HEADS = 4
HEAD_SIZE = 128
GROUP = QUERY_HEADS // KEY_VALUE_HEADS
ADAPTER_SCALE = 2.0
NEVER = -1e30
LAYOUT_BYTES = 16 * 2**20
SUM_BYTES = 16 * 2**20
BF16 = jnp.bfloat16
F32 = jnp.float32
I32 = jnp.int32
VMEM = pl.BlockSpec(memory_space=pltpu.VMEM)
ANY = pl.BlockSpec(memory_space=pl.ANY)


def dot(a, b, a_dim, b_dim):
    return lax.dot_general(a, b, (((a_dim,), (b_dim,)), ((), ())), preferred_element_type=F32)


def group_rows(rows_of_group, n_groups, width, seq, by_slot):
    row = lax.broadcasted_iota(I32, (n_groups * rows_of_group, width), 0) // rows_of_group
    if by_slot:
        half = n_groups // 2
        row = jnp.where(row < half, row * 2, (row - half) * 2 + 1) ^ seq
    return row


def layout_kernel(n_parts, facts_ref, *refs):
    own_turned, *parts = refs[: n_parts + 1]
    k_all, v_all, k_turned, bias = refs[n_parts + 1 :]
    tok = facts_ref.shape[1]
    kv_width = v_all.shape[1]
    key_rows = v_all.shape[0]
    head = lax.axis_index("head")
    position = head * tok + lax.broadcasted_iota(I32, (1, tok), 1)
    key_position = (
        head * tok - (key_rows - tok) + lax.broadcasted_iota(I32, (key_rows, tok), 0)
    )
    allowed = (key_position >= facts_ref[0:1, :]) & (key_position <= position)
    bias[...] = jnp.where(allowed, 0.0, NEVER)
    for kv in range(KEY_VALUE_HEADS):
        start = 0
        at = slice(kv * HEAD_SIZE, (kv + 1) * HEAD_SIZE)
        for part in parts:
            rows = part.shape[0]
            k_all[start : start + rows, at] = part[:, at]
            v_all[start : start + rows, at] = part[:, kv_width + at.start : kv_width + at.stop]
            start += rows
        k_turned[at, : start - tok] = k_all[: start - tok, at].T
        k_turned[at, start - tok :] = own_turned[at, :]


def attention_kernel(by_slot, first_kv, n_kv, k_all, v_all, k_turned, bias, q_hbm, g_hbm, *refs):
    before, refs = (refs[:3], refs[3:]) if first_kv else ((), refs)
    dq_turned, *up_refs, q_ref, g_ref, q_sem, g_sem = refs
    tok = q_ref.shape[0]
    seq, head = lax.axis_index("seq"), lax.axis_index("head")
    per_kv = GROUP * HEAD_SIZE

    def fetch(kv):
        to = pl.ds(kv * per_kv, per_kv)
        at = pl.ds((first_kv + kv) * per_kv, per_kv)
        return (
            pltpu.make_async_copy(q_hbm.at[:, at], q_ref.at[:, to], q_sem.at[kv]),
            pltpu.make_async_copy(g_hbm.at[:, at], g_ref.at[:, to], g_sem.at[kv]),
        )

    for kv in range(n_kv):
        for copy in fetch(kv):
            copy.start()

    scale = 1.0 / HEAD_SIZE**0.5
    to_log2 = scale * math.log2(math.e)

    def one_group(kv, carry):
        for copy in fetch(kv):
            copy.wait()
        at_kv = pl.ds(pl.multiple_of((first_kv + kv) * HEAD_SIZE, HEAD_SIZE), HEAD_SIZE)
        k_g = k_all[:, at_kv]
        v_g = v_all[:, at_kv]
        kt_g = k_turned[at_kv, :]
        for i in range(0, GROUP, 2):
            first = (kv * GROUP + i) * HEAD_SIZE
            at = [
                pl.ds(pl.multiple_of(first + n * HEAD_SIZE, HEAD_SIZE), HEAD_SIZE) for n in range(2)
            ]
            q_two = jnp.concatenate([q_ref[:, at[0]], q_ref[:, at[1]]], axis=0)
            g_two = jnp.concatenate([g_ref[:, at[0]], g_ref[:, at[1]]], axis=0)
            s = dot(k_g, q_two, 1, 1) + jnp.concatenate([bias[...]] * 2, axis=1)
            d_prob = dot(v_g, g_two, 1, 1)
            weights = jnp.exp2((s - jnp.max(s, axis=0, keepdims=True)) * to_log2)
            inverse = 1.0 / jnp.sum(weights, axis=0, keepdims=True)
            delta = jnp.sum(weights * d_prob, axis=0, keepdims=True) * inverse
            dscore = (weights * (d_prob - delta)).astype(BF16)
            dq = dot(kt_g, dscore, 1, 0) * (inverse * scale)
            dq_turned[at[0], :] = dq[:, :tok].astype(BF16)
            dq_turned[at[1], :] = dq[:, tok:].astype(BF16)
        return carry

    lax.fori_loop(0, n_kv, one_group, 0)
    if not up_refs:
        return

    facts_ref, act_ref, dq_before = before
    rank = act_ref.shape[0]
    n_quarters, per, _, part = up_refs[0].shape
    n_groups = per * len(up_refs)
    own = group_rows(rank, n_groups, tok, seq, by_slot) == facts_ref[2:3, :]
    act = jnp.concatenate([act_ref[...].astype(F32)] * n_groups, axis=0)
    act_cols = jnp.where(own, act, 0.0).astype(BF16)
    n_before = dq_before.shape[0] // part
    for quarter in range(n_quarters):
        i, dq_ref = (quarter, dq_before) if quarter < n_before else (quarter - n_before, dq_turned)
        up = dot(act_cols, dq_ref[i * part : (i + 1) * part, :], 1, 1).astype(BF16)
        j = head ^ quarter if by_slot else quarter
        for n in range(n_groups):
            up_refs[n // per][j, n % per] = up[n * rank : (n + 1) * rank, :]


def rank_kernel(by_slot, n_w, facts_ref, *refs):
    w_refs, (dq_a, dq_b, out_ref) = refs[:n_w], refs[n_w:]
    tok = dq_a.shape[1]
    seq, head = lax.axis_index("seq"), lax.axis_index("head")
    n_adapters, n_quarters, rank, part = w_refs[0].shape
    adapter = facts_ref[1:2, :]
    total = jnp.zeros((rank, tok), F32)
    n_a = dq_a.shape[0] // part
    for c, w_ref in enumerate(w_refs):
        rows = None
        for quarter in range(n_quarters):
            j = lax.rem(head + n_quarters - quarter, n_quarters) if by_slot else quarter
            i, dq_ref = (quarter, dq_a) if quarter < n_a else (quarter - n_a, dq_b)
            dq = dq_ref[i * part : (i + 1) * part, :]
            new = dot(w_ref[:, j].reshape(n_adapters * rank, part), dq, 1, 0)
            rows = new if rows is None else rows + new
        for m in range(n_adapters):
            a = (2 * m + c) ^ seq if by_slot else m
            total = total + jnp.where(adapter == a, rows[m * rank : (m + 1) * rank, :], 0.0)
    out_ref[...] = total.astype(BF16)


def down_kernel(by_slot, facts_ref, x_ref, rank_ref, *out_refs):
    rank, tok = rank_ref.shape
    seq, head = lax.axis_index("seq"), lax.axis_index("head")
    per, n_quarters, _, x_part = out_refs[0].shape
    n_groups = per * len(out_refs)
    own = group_rows(rank, n_groups, tok, seq, by_slot) == facts_ref[2:3, :]
    low = jnp.concatenate([rank_ref[...].astype(F32)] * n_groups, axis=0)
    cols = jnp.where(own, low, 0.0).astype(BF16)
    step = min(512, x_part)
    for j in range(n_quarters):
        quarter = head ^ j if by_slot else j
        for start in range(0, x_part, step):
            at = pl.ds(pl.multiple_of(quarter * x_part + start, step), step)
            down = dot(cols, x_ref[:, at], 1, 0).astype(BF16)
            for n in range(n_groups):
                piece = down[n * rank : (n + 1) * rank, :]
                out_refs[n // per][n % per, j, :, start : start + step] = piece


def sum_kernel(a_ref, b_ref, *out_refs):
    for i, out_ref in enumerate(out_refs):
        out_ref[...] = (a_ref[i].astype(F32) + b_ref[i].astype(F32)).astype(BF16)


def token_facts(tok, lengths, adapters, owner, by_slot):
    n_seg = lengths.shape[0]
    order = jnp.arange(n_seg, dtype=I32)
    starts = jnp.sum(jnp.where(order[None, :] < order[:, None], lengths[None, :], 0), axis=1)
    if by_slot:
        hits = adapters[:, None] == jnp.arange(owner.shape[0], dtype=I32)[None, :]
        groups = jnp.sum(jnp.where(hits, owner[None, :], 0), axis=1)
    else:
        groups = order
    position = lax.axis_index("head") * tok + jnp.arange(tok, dtype=I32)
    inside = (position >= starts[:, None]) & (position < (starts + lengths)[:, None])
    told = jnp.stack([starts, adapters, groups] + [jnp.zeros_like(starts)] * 5)
    return jnp.sum(jnp.where(inside[None], told[:, :, None], 0), axis=1)


def shifted(x, n_head, j):
    return lax.ppermute(x, "head", [(i, (i + j) % n_head) for i in range(n_head)])


def across(x, n_head, j):
    return lax.ppermute(x, "head", [(i, i ^ j) for i in range(n_head)])


def partnered(x, n_seq, bits):
    return lax.ppermute(x, "seq", [(i, i ^ bits) for i in range(n_seq)])


def on_device(
    queries, keys, values, output_gradient, inputs, adapter_activation,
    adapter_up_weight, segment_length, segment_adapter, owner,
):
    n_head = lax.axis_size("head")
    n_seq = lax.axis_size("seq")
    tok, width = queries.shape
    pack = tok * n_head
    rank = adapter_up_weight.shape[1]
    n_adapters = owner.shape[0]
    n_seg = segment_length.shape[1]
    by_slot = n_adapters == n_seq == 8 and n_head == 4
    facts = token_facts(tok, segment_length[0], segment_adapter[0], owner, by_slot)

    reach = []
    while sum(reach) < pack * 3 // 8:
        reach.append(min(pack * 3 // 8 - sum(reach), tok))
    key_rows = tok + sum(reach)
    own = jnp.concatenate([keys, values], axis=1)
    parts = [own]
    for hop, rows in enumerate(reach, 1):
        shift = [(i, i + hop) for i in range(n_head - hop)]
        parts.insert(0, lax.ppermute(own[tok - rows :], "head", shift))

    if by_slot:
        w = [adapter_up_weight] + [shifted(adapter_up_weight, n_head, j) for j in range(1, n_head)]
        w = jnp.concatenate(w, axis=0)[None]
        w = [w] + [partnered(w, n_seq, 2 * m) for m in range(1, n_seq // 2)]
    else:
        w = lax.all_gather(adapter_up_weight, "seq", axis=0, tiled=True)
        up_weight = [lax.all_gather(w, "head", axis=1, tiled=False)]

    n_out = 2 if by_slot else 1
    n_groups = n_seq if by_slot else n_seg
    part = width // n_head
    x_part = inputs.shape[1] // n_head
    params = pltpu.CompilerParams(vmem_limit_bytes=32 * 2**20)

    laid_out = pl.pallas_call(
        functools.partial(layout_kernel, len(parts)),
        out_shape=[
            jax.ShapeDtypeStruct((key_rows, keys.shape[1]), BF16),
            jax.ShapeDtypeStruct((key_rows, keys.shape[1]), BF16),
            jax.ShapeDtypeStruct((keys.shape[1], key_rows), BF16),
            jax.ShapeDtypeStruct((key_rows, tok), F32),
        ],
        in_specs=[VMEM] * (2 + len(parts)),
        out_specs=[VMEM] * 4,
        compiler_params=params,
        cost_estimate=pl.CostEstimate(
            flops=0, bytes_accessed=LAYOUT_BYTES, transcendentals=0
        ),
        name="layout",
    )(facts, keys.T, *parts)
    halves = 2
    n_kv = KEY_VALUE_HEADS // halves
    half = width // halves

    def attention(h, before, up_shapes):
        return pl.pallas_call(
            functools.partial(attention_kernel, by_slot, h * n_kv, n_kv),
            out_shape=[jax.ShapeDtypeStruct((half, tok), BF16)] + up_shapes,
            in_specs=[VMEM] * 4 + [ANY] * 2 + [VMEM] * len(before),
            out_specs=[VMEM] * (1 + len(up_shapes)),
            scratch_shapes=[
                pltpu.VMEM((tok, half), BF16),
                pltpu.VMEM((tok, half), BF16),
                pltpu.SemaphoreType.DMA((n_kv,)),
                pltpu.SemaphoreType.DMA((n_kv,)),
            ],
            compiler_params=params,
            cost_estimate=pl.CostEstimate(
                flops=2 * tok * half * key_rows * 3,
                bytes_accessed=4 * tok * half * 2,
                transcendentals=tok * key_rows * QUERY_HEADS // halves,
            ),
            name="attention_%d" % h,
        )(*laid_out, queries, output_gradient, *before)

    (dq_a,) = attention(0, [], [])
    if by_slot:
        dq_a, w = lax.optimization_barrier((dq_a, w))
        w = jnp.concatenate(w, axis=0)
        up_weight = [w, partnered(w, n_seq, 1)]
    up_shape = jax.ShapeDtypeStruct((n_head, n_groups // n_out, rank, part), BF16)
    dq_b, *up = attention(1, [facts, adapter_activation.T, dq_a], [up_shape] * n_out)

    if by_slot:
        up, up_weight = lax.optimization_barrier((up, up_weight))
    rank_low = pl.pallas_call(
        functools.partial(rank_kernel, by_slot, len(up_weight)),
        out_shape=jax.ShapeDtypeStruct((rank, tok), BF16),
        in_specs=[VMEM] * (3 + len(up_weight)),
        out_specs=VMEM,
        compiler_params=params,
        name="rank_gradient",
    )(facts, *up_weight, dq_a, dq_b)

    down_shape = jax.ShapeDtypeStruct((n_groups // n_out, n_head, rank, x_part), BF16)
    down = pl.pallas_call(
        functools.partial(down_kernel, by_slot),
        out_shape=[down_shape] * n_out,
        in_specs=[VMEM] * 3,
        out_specs=[VMEM] * n_out,
        compiler_params=params,
        cost_estimate=pl.CostEstimate(
            flops=2 * n_groups * rank * tok * inputs.shape[1],
            bytes_accessed=4 * tok * inputs.shape[1] * 2,
            transcendentals=0,
        ),
        name="down_parts",
    )(facts, inputs, rank_low)

    if by_slot:
        down = pl.pallas_call(
            sum_kernel,
            out_shape=[jax.ShapeDtypeStruct(down[0].shape[1:], BF16)] * down[0].shape[0],
            in_specs=[VMEM] * 2,
            out_specs=[VMEM] * down[0].shape[0],
            compiler_params=params,
            cost_estimate=pl.CostEstimate(flops=0, bytes_accessed=SUM_BYTES, transcendentals=0),
            name="core_sum",
        )(down[0], partnered(down[1], n_seq, 1))
        up = over_chips(over_z(over_cores(up, n_seq), n_head, (1, 2, 3)).astype(BF16), n_seq)
        down = over_z(over_chips(down, n_seq).astype(BF16), n_head, (3, 1, 2))
    else:
        up = lax.all_to_all(up[0], "head", split_axis=0, concat_axis=0, tiled=True)
        up = spread(jnp.sum(up.astype(F32), axis=0), segment_adapter, owner, n_seq)
        down = lax.all_to_all(down[0], "head", split_axis=1, concat_axis=1, tiled=True)
        down = spread(jnp.sum(down.astype(F32), axis=1), segment_adapter, owner, n_seq)
    return down.T[None] * ADAPTER_SCALE, up[None] * ADAPTER_SCALE


def over_cores(parts, n_seq):
    keep, send = parts
    return (keep.astype(F32) + partnered(send, n_seq, 1).astype(F32)).astype(BF16)


def added(own, got):
    total = own.astype(F32)
    for piece in got:
        total = total + piece.astype(F32)
    return total


def over_chips(both, n_seq):
    return added(both[0], [partnered(both[m], n_seq, 2 * m) for m in range(1, n_seq // 2)])


def over_z(both, n_head, order):
    return added(both[0], [across(both[j], n_head, j) for j in order])


def spread(part, segment_adapter, owner, n_seq):
    goes_to = owner[segment_adapter[0]]
    slots = (goes_to[:, None] == jnp.arange(n_seq, dtype=I32)[None, :]).astype(F32)
    slotted = jnp.einsum("srw,so->orw", part, slots, precision=lax.Precision.HIGHEST)
    slotted = lax.all_to_all(slotted.astype(BF16), "seq", split_axis=0, concat_axis=0, tiled=True)
    return jnp.sum(slotted.astype(F32), axis=0)


def solution(mesh):
    return jax.shard_map(
        on_device,
        mesh=mesh,
        in_specs=(
            P(("seq", "head"), None),
            P(("seq", "head"), None),
            P(("seq", "head"), None),
            P(("seq", "head"), None),
            P(("seq", "head"), None),
            P(("seq", "head"), None),
            P("seq", None, "head"),
            P("seq", None),
            P("seq", None),
            P(),
        ),
        out_specs=(P("seq", "head", None), P("seq", None, "head")),
        check_vma=False,
    )
```

```python
import functools
import math

import jax
import jax.numpy as jnp
from jax import lax
from jax.experimental import pallas as pl
from jax.experimental.pallas import tpu as pltpu
from jax.sharding import PartitionSpec as P

QUERY_HEADS = 32
KEY_VALUE_HEADS = 4
HEAD_SIZE = 128
GROUP = QUERY_HEADS // KEY_VALUE_HEADS
ADAPTER_SCALE = 2.0
NEVER = -1e30
LAYOUT_BYTES = 16 * 2**20
SUM_BYTES = 16 * 2**20
BF16 = jnp.bfloat16
F32 = jnp.float32
I32 = jnp.int32
VMEM = pl.BlockSpec(memory_space=pltpu.VMEM)
ANY = pl.BlockSpec(memory_space=pl.ANY)


def dot(a, b, a_dim, b_dim):
    return lax.dot_general(a, b, (((a_dim,), (b_dim,)), ((), ())), preferred_element_type=F32)


def group_rows(rows_of_group, n_groups, width, seq, by_slot):
    row = lax.broadcasted_iota(I32, (n_groups * rows_of_group, width), 0) // rows_of_group
    if by_slot:
        half = n_groups // 2
        row = jnp.where(row < half, row * 2, (row - half) * 2 + 1) ^ seq
    return row


def layout_kernel(n_parts, facts_ref, *refs):
    own_turned, *parts = refs[: n_parts + 1]
    k_all, v_all, k_turned, bias = refs[n_parts + 1 :]
    tok = facts_ref.shape[1]
    kv_width = v_all.shape[1]
    key_rows = v_all.shape[0]
    head = lax.axis_index("head")
    position = head * tok + lax.broadcasted_iota(I32, (1, tok), 1)
    key_position = (
        head * tok - (key_rows - tok) + lax.broadcasted_iota(I32, (key_rows, tok), 0)
    )
    allowed = (key_position >= facts_ref[0:1, :]) & (key_position <= position)
    bias[...] = jnp.where(allowed, 0.0, NEVER)
    for kv in range(KEY_VALUE_HEADS):
        start = 0
        at = slice(kv * HEAD_SIZE, (kv + 1) * HEAD_SIZE)
        for part in parts:
            rows = part.shape[0]
            k_all[start : start + rows, at] = part[:, at]
            v_all[start : start + rows, at] = part[:, kv_width + at.start : kv_width + at.stop]
            start += rows
        k_turned[at, : start - tok] = k_all[: start - tok, at].T
        k_turned[at, start - tok :] = own_turned[at, :]


def attention_kernel(by_slot, first_kv, n_kv, k_all, v_all, k_turned, bias, q_hbm, g_hbm, *refs):
    before, refs = (refs[:3], refs[3:]) if first_kv else ((), refs)
    dq_turned, *up_refs, q_ref, g_ref, q_sem, g_sem = refs
    tok = q_ref.shape[0]
    seq, head = lax.axis_index("seq"), lax.axis_index("head")
    per_kv = GROUP * HEAD_SIZE

    def fetch(kv):
        to = pl.ds(kv * per_kv, per_kv)
        at = pl.ds((first_kv + kv) * per_kv, per_kv)
        return (
            pltpu.make_async_copy(q_hbm.at[:, at], q_ref.at[:, to], q_sem.at[kv]),
            pltpu.make_async_copy(g_hbm.at[:, at], g_ref.at[:, to], g_sem.at[kv]),
        )

    for kv in range(n_kv):
        for copy in fetch(kv):
            copy.start()

    scale = 1.0 / HEAD_SIZE**0.5
    to_log2 = scale * math.log2(math.e)

    def one_group(kv, carry):
        for copy in fetch(kv):
            copy.wait()
        at_kv = pl.ds(pl.multiple_of((first_kv + kv) * HEAD_SIZE, HEAD_SIZE), HEAD_SIZE)
        k_g = k_all[:, at_kv]
        v_g = v_all[:, at_kv]
        kt_g = k_turned[at_kv, :]
        for i in range(0, GROUP, 2):
            first = (kv * GROUP + i) * HEAD_SIZE
            at = [
                pl.ds(pl.multiple_of(first + n * HEAD_SIZE, HEAD_SIZE), HEAD_SIZE) for n in range(2)
            ]
            q_two = jnp.concatenate([q_ref[:, at[0]], q_ref[:, at[1]]], axis=0)
            g_two = jnp.concatenate([g_ref[:, at[0]], g_ref[:, at[1]]], axis=0)
            s = dot(k_g, q_two, 1, 1) + jnp.concatenate([bias[...]] * 2, axis=1)
            d_prob = dot(v_g, g_two, 1, 1)
            weights = jnp.exp2((s - jnp.max(s, axis=0, keepdims=True)) * to_log2)
            inverse = 1.0 / jnp.sum(weights, axis=0, keepdims=True)
            delta = jnp.sum(weights * d_prob, axis=0, keepdims=True) * inverse
            dscore = (weights * (d_prob - delta)).astype(BF16)
            dq = dot(kt_g, dscore, 1, 0) * (inverse * scale)
            dq_turned[at[0], :] = dq[:, :tok].astype(BF16)
            dq_turned[at[1], :] = dq[:, tok:].astype(BF16)
        return carry

    lax.fori_loop(0, n_kv, one_group, 0)
    if not up_refs:
        return

    facts_ref, act_ref, dq_before = before
    rank = act_ref.shape[0]
    n_quarters, per, _, part = up_refs[0].shape
    n_groups = per * len(up_refs)
    own = group_rows(rank, n_groups, tok, seq, by_slot) == facts_ref[2:3, :]
    act = jnp.concatenate([act_ref[...].astype(F32)] * n_groups, axis=0)
    act_cols = jnp.where(own, act, 0.0).astype(BF16)
    n_before = dq_before.shape[0] // part
    for quarter in range(n_quarters):
        i, dq_ref = (quarter, dq_before) if quarter < n_before else (quarter - n_before, dq_turned)
        up = dot(act_cols, dq_ref[i * part : (i + 1) * part, :], 1, 1).astype(BF16)
        j = head ^ quarter if by_slot else quarter
        for n in range(n_groups):
            up_refs[n // per][j, n % per] = up[n * rank : (n + 1) * rank, :]


def rank_kernel(by_slot, n_w, facts_ref, *refs):
    w_refs, (dq_a, dq_b, out_ref) = refs[:n_w], refs[n_w:]
    tok = dq_a.shape[1]
    seq, head = lax.axis_index("seq"), lax.axis_index("head")
    n_adapters, n_quarters, rank, part = w_refs[0].shape
    adapter = facts_ref[1:2, :]
    total = jnp.zeros((rank, tok), F32)
    n_a = dq_a.shape[0] // part
    for c, w_ref in enumerate(w_refs):
        rows = None
        for quarter in range(n_quarters):
            j = lax.rem(head + n_quarters - quarter, n_quarters) if by_slot else quarter
            i, dq_ref = (quarter, dq_a) if quarter < n_a else (quarter - n_a, dq_b)
            dq = dq_ref[i * part : (i + 1) * part, :]
            new = dot(w_ref[:, j].reshape(n_adapters * rank, part), dq, 1, 0)
            rows = new if rows is None else rows + new
        for m in range(n_adapters):
            a = (2 * m + c) ^ seq if by_slot else m
            total = total + jnp.where(adapter == a, rows[m * rank : (m + 1) * rank, :], 0.0)
    out_ref[...] = total.astype(BF16)


def down_kernel(by_slot, facts_ref, x_ref, rank_ref, *out_refs):
    rank, tok = rank_ref.shape
    seq, head = lax.axis_index("seq"), lax.axis_index("head")
    per, n_quarters, _, x_part = out_refs[0].shape
    n_groups = per * len(out_refs)
    own = group_rows(rank, n_groups, tok, seq, by_slot) == facts_ref[2:3, :]
    low = jnp.concatenate([rank_ref[...].astype(F32)] * n_groups, axis=0)
    cols = jnp.where(own, low, 0.0).astype(BF16)
    step = min(512, x_part)
    for j in range(n_quarters):
        quarter = head ^ j if by_slot else j
        for start in range(0, x_part, step):
            at = pl.ds(pl.multiple_of(quarter * x_part + start, step), step)
            down = dot(cols, x_ref[:, at], 1, 0).astype(BF16)
            for n in range(n_groups):
                piece = down[n * rank : (n + 1) * rank, :]
                out_refs[n // per][n % per, j, :, start : start + step] = piece


def sum_kernel(a_ref, b_ref, *out_refs):
    for i, out_ref in enumerate(out_refs):
        out_ref[...] = (a_ref[i].astype(F32) + b_ref[i].astype(F32)).astype(BF16)


def token_facts(tok, lengths, adapters, owner, by_slot):
    n_seg = lengths.shape[0]
    order = jnp.arange(n_seg, dtype=I32)
    starts = jnp.sum(jnp.where(order[None, :] < order[:, None], lengths[None, :], 0), axis=1)
    if by_slot:
        hits = adapters[:, None] == jnp.arange(owner.shape[0], dtype=I32)[None, :]
        groups = jnp.sum(jnp.where(hits, owner[None, :], 0), axis=1)
    else:
        groups = order
    position = lax.axis_index("head") * tok + jnp.arange(tok, dtype=I32)
    inside = (position >= starts[:, None]) & (position < (starts + lengths)[:, None])
    told = jnp.stack([starts, adapters, groups] + [jnp.zeros_like(starts)] * 5)
    return jnp.sum(jnp.where(inside[None], told[:, :, None], 0), axis=1)


def shifted(x, n_head, j):
    return lax.ppermute(x, "head", [(i, (i + j) % n_head) for i in range(n_head)])


def across(x, n_head, j):
    return lax.ppermute(x, "head", [(i, i ^ j) for i in range(n_head)])


def partnered(x, n_seq, bits):
    return lax.ppermute(x, "seq", [(i, i ^ bits) for i in range(n_seq)])


def on_device(
    queries, keys, values, output_gradient, inputs, adapter_activation,
    adapter_up_weight, segment_length, segment_adapter, owner,
):
    n_head = lax.axis_size("head")
    n_seq = lax.axis_size("seq")
    tok, width = queries.shape
    pack = tok * n_head
    rank = adapter_up_weight.shape[1]
    n_adapters = owner.shape[0]
    n_seg = segment_length.shape[1]
    by_slot = n_adapters == n_seq == 8 and n_head == 4
    facts = token_facts(tok, segment_length[0], segment_adapter[0], owner, by_slot)

    reach = []
    while sum(reach) < pack * 3 // 8:
        reach.append(min(pack * 3 // 8 - sum(reach), tok))
    key_rows = tok + sum(reach)
    own = jnp.concatenate([keys, values], axis=1)
    parts = [own]
    for hop, rows in enumerate(reach, 1):
        shift = [(i, i + hop) for i in range(n_head - hop)]
        parts.insert(0, lax.ppermute(own[tok - rows :], "head", shift))

    if by_slot:
        w = [adapter_up_weight] + [shifted(adapter_up_weight, n_head, j) for j in range(1, n_head)]
        w = jnp.concatenate(w, axis=0)[None]
        w = [w] + [partnered(w, n_seq, 2 * m) for m in range(1, n_seq // 2)]
    else:
        w = lax.all_gather(adapter_up_weight, "seq", axis=0, tiled=True)
        up_weight = [lax.all_gather(w, "head", axis=1, tiled=False)]

    n_out = 2 if by_slot else 1
    n_groups = n_seq if by_slot else n_seg
    part = width // n_head
    x_part = inputs.shape[1] // n_head
    params = pltpu.CompilerParams(vmem_limit_bytes=32 * 2**20)

    laid_out = pl.pallas_call(
        functools.partial(layout_kernel, len(parts)),
        out_shape=[
            jax.ShapeDtypeStruct((key_rows, keys.shape[1]), BF16),
            jax.ShapeDtypeStruct((key_rows, keys.shape[1]), BF16),
            jax.ShapeDtypeStruct((keys.shape[1], key_rows), BF16),
            jax.ShapeDtypeStruct((key_rows, tok), F32),
        ],
        in_specs=[VMEM] * (2 + len(parts)),
        out_specs=[VMEM] * 4,
        compiler_params=params,
        cost_estimate=pl.CostEstimate(
            flops=0, bytes_accessed=LAYOUT_BYTES, transcendentals=0
        ),
        name="layout",
    )(facts, keys.T, *parts)
    halves = 2
    n_kv = KEY_VALUE_HEADS // halves
    half = width // halves

    def attention(h, before, up_shapes):
        return pl.pallas_call(
            functools.partial(attention_kernel, by_slot, h * n_kv, n_kv),
            out_shape=[jax.ShapeDtypeStruct((half, tok), BF16)] + up_shapes,
            in_specs=[VMEM] * 4 + [ANY] * 2 + [VMEM] * len(before),
            out_specs=[VMEM] * (1 + len(up_shapes)),
            scratch_shapes=[
                pltpu.VMEM((tok, half), BF16),
                pltpu.VMEM((tok, half), BF16),
                pltpu.SemaphoreType.DMA((n_kv,)),
                pltpu.SemaphoreType.DMA((n_kv,)),
            ],
            compiler_params=params,
            cost_estimate=pl.CostEstimate(
                flops=2 * tok * half * key_rows * 3,
                bytes_accessed=4 * tok * half * 2,
                transcendentals=tok * key_rows * QUERY_HEADS // halves,
            ),
            name="attention_%d" % h,
        )(*laid_out, queries, output_gradient, *before)

    (dq_a,) = attention(0, [], [])
    if by_slot:
        dq_a, w = lax.optimization_barrier((dq_a, w))
        w = jnp.concatenate(w, axis=0)
        up_weight = [w, partnered(w, n_seq, 1)]
    up_shape = jax.ShapeDtypeStruct((n_head, n_groups // n_out, rank, part), BF16)
    dq_b, *up = attention(1, [facts, adapter_activation.T, dq_a], [up_shape] * n_out)

    if by_slot:
        up, up_weight = lax.optimization_barrier((up, up_weight))
    rank_low = pl.pallas_call(
        functools.partial(rank_kernel, by_slot, len(up_weight)),
        out_shape=jax.ShapeDtypeStruct((rank, tok), BF16),
        in_specs=[VMEM] * (3 + len(up_weight)),
        out_specs=VMEM,
        compiler_params=params,
        name="rank_gradient",
    )(facts, *up_weight, dq_a, dq_b)

    down_shape = jax.ShapeDtypeStruct((n_groups // n_out, n_head, rank, x_part), BF16)
    down = pl.pallas_call(
        functools.partial(down_kernel, by_slot),
        out_shape=[down_shape] * n_out,
        in_specs=[VMEM] * 3,
        out_specs=[VMEM] * n_out,
        compiler_params=params,
        cost_estimate=pl.CostEstimate(
            flops=2 * n_groups * rank * tok * inputs.shape[1],
            bytes_accessed=4 * tok * inputs.shape[1] * 2,
            transcendentals=0,
        ),
        name="down_parts",
    )(facts, inputs, rank_low)

    if by_slot:
        down = pl.pallas_call(
            sum_kernel,
            out_shape=[jax.ShapeDtypeStruct(down[0].shape[1:], BF16)] * down[0].shape[0],
            in_specs=[VMEM] * 2,
            out_specs=[VMEM] * down[0].shape[0],
            compiler_params=params,
            cost_estimate=pl.CostEstimate(flops=0, bytes_accessed=SUM_BYTES, transcendentals=0),
            name="core_sum",
        )(down[0], partnered(down[1], n_seq, 1))
        up = over_cores(up, n_seq)
        up = added(up[:2], [across(up[2:], n_head, 2)])
        up_got = across(up[1].astype(BF16), n_head, 1)
        down = over_chips(down, n_seq).astype(BF16)
        up_got, _ = lax.optimization_barrier((up_got, down))
        up = added(up[0], [up_got]).astype(BF16)
        down = over_z(down, n_head, (3, 1, 2))
        up_got = [partnered(up[m], n_seq, 2 * m) for m in range(1, n_seq // 2)]
        up_got, _ = lax.optimization_barrier((up_got, down))
        up = added(up[0], up_got)
    else:
        up = lax.all_to_all(up[0], "head", split_axis=0, concat_axis=0, tiled=True)
        up = spread(jnp.sum(up.astype(F32), axis=0), segment_adapter, owner, n_seq)
        down = lax.all_to_all(down[0], "head", split_axis=1, concat_axis=1, tiled=True)
        down = spread(jnp.sum(down.astype(F32), axis=1), segment_adapter, owner, n_seq)
    return down.T[None] * ADAPTER_SCALE, up[None] * ADAPTER_SCALE


def over_cores(parts, n_seq):
    keep, send = parts
    return (keep.astype(F32) + partnered(send, n_seq, 1).astype(F32)).astype(BF16)


def added(own, got):
    total = own.astype(F32)
    for piece in got:
        total = total + piece.astype(F32)
    return total


def over_chips(both, n_seq):
    return added(both[0], [partnered(both[m], n_seq, 2 * m) for m in range(1, n_seq // 2)])


def over_z(both, n_head, order):
    return added(both[0], [across(both[j], n_head, j) for j in order])


def spread(part, segment_adapter, owner, n_seq):
    goes_to = owner[segment_adapter[0]]
    slots = (goes_to[:, None] == jnp.arange(n_seq, dtype=I32)[None, :]).astype(F32)
    slotted = jnp.einsum("srw,so->orw", part, slots, precision=lax.Precision.HIGHEST)
    slotted = lax.all_to_all(slotted.astype(BF16), "seq", split_axis=0, concat_axis=0, tiled=True)
    return jnp.sum(slotted.astype(F32), axis=0)


def solution(mesh):
    return jax.shard_map(
        on_device,
        mesh=mesh,
        in_specs=(
            P(("seq", "head"), None),
            P(("seq", "head"), None),
            P(("seq", "head"), None),
            P(("seq", "head"), None),
            P(("seq", "head"), None),
            P(("seq", "head"), None),
            P("seq", None, "head"),
            P("seq", None),
            P("seq", None),
            P(),
        ),
        out_specs=(P("seq", "head", None), P("seq", None, "head")),
        check_vma=False,
    )
```

```python
import functools
import math

import jax
import jax.numpy as jnp
from jax import lax
from jax.experimental import pallas as pl
from jax.experimental.pallas import tpu as pltpu
from jax.sharding import PartitionSpec as P

QUERY_HEADS = 32
KEY_VALUE_HEADS = 4
HEAD_SIZE = 128
GROUP = QUERY_HEADS // KEY_VALUE_HEADS
ADAPTER_SCALE = 2.0
NEVER = -1e30
LAYOUT_BYTES = 16 * 2**20
SUM_BYTES = 16 * 2**20
BF16 = jnp.bfloat16
F32 = jnp.float32
I32 = jnp.int32
VMEM = pl.BlockSpec(memory_space=pltpu.VMEM)
ANY = pl.BlockSpec(memory_space=pl.ANY)


def dot(a, b, a_dim, b_dim):
    return lax.dot_general(a, b, (((a_dim,), (b_dim,)), ((), ())), preferred_element_type=F32)


def group_rows(rows_of_group, n_groups, width, seq, by_slot):
    row = lax.broadcasted_iota(I32, (n_groups * rows_of_group, width), 0) // rows_of_group
    if by_slot:
        half = n_groups // 2
        row = jnp.where(row < half, row * 2, (row - half) * 2 + 1) ^ seq
    return row


def layout_kernel(n_parts, facts_ref, *refs):
    own_turned, *parts = refs[: n_parts + 1]
    k_all, v_all, k_turned, bias = refs[n_parts + 1 :]
    tok = facts_ref.shape[1]
    kv_width = v_all.shape[1]
    key_rows = v_all.shape[0]
    head = lax.axis_index("head")
    position = head * tok + lax.broadcasted_iota(I32, (1, tok), 1)
    key_position = (
        head * tok - (key_rows - tok) + lax.broadcasted_iota(I32, (key_rows, tok), 0)
    )
    allowed = (key_position >= facts_ref[0:1, :]) & (key_position <= position)
    bias[...] = jnp.where(allowed, 0.0, NEVER)
    for kv in range(KEY_VALUE_HEADS):
        start = 0
        at = slice(kv * HEAD_SIZE, (kv + 1) * HEAD_SIZE)
        for part in parts:
            rows = part.shape[0]
            k_all[start : start + rows, at] = part[:, at]
            v_all[start : start + rows, at] = part[:, kv_width + at.start : kv_width + at.stop]
            start += rows
        k_turned[at, : start - tok] = k_all[: start - tok, at].T
        k_turned[at, start - tok :] = own_turned[at, :]


def attention_kernel(by_slot, first_kv, n_kv, k_all, v_all, k_turned, bias, q_hbm, g_hbm, *refs):
    before, refs = (refs[:3], refs[3:]) if first_kv else ((), refs)
    dq_turned, *up_refs, q_ref, g_ref, q_sem, g_sem = refs
    tok = q_ref.shape[0]
    seq, head = lax.axis_index("seq"), lax.axis_index("head")
    per_kv = GROUP * HEAD_SIZE

    def fetch(kv):
        to = pl.ds(kv * per_kv, per_kv)
        at = pl.ds((first_kv + kv) * per_kv, per_kv)
        return (
            pltpu.make_async_copy(q_hbm.at[:, at], q_ref.at[:, to], q_sem.at[kv]),
            pltpu.make_async_copy(g_hbm.at[:, at], g_ref.at[:, to], g_sem.at[kv]),
        )

    for kv in range(n_kv):
        for copy in fetch(kv):
            copy.start()

    scale = 1.0 / HEAD_SIZE**0.5
    to_log2 = scale * math.log2(math.e)

    def one_group(kv, carry):
        for copy in fetch(kv):
            copy.wait()
        at_kv = pl.ds(pl.multiple_of((first_kv + kv) * HEAD_SIZE, HEAD_SIZE), HEAD_SIZE)
        k_g = k_all[:, at_kv]
        v_g = v_all[:, at_kv]
        kt_g = k_turned[at_kv, :]
        def products(i):
            first = (kv * GROUP + i) * HEAD_SIZE
            at = [
                pl.ds(pl.multiple_of(first + n * HEAD_SIZE, HEAD_SIZE), HEAD_SIZE) for n in range(2)
            ]
            q_two = jnp.concatenate([q_ref[:, at[0]], q_ref[:, at[1]]], axis=0)
            g_two = jnp.concatenate([g_ref[:, at[0]], g_ref[:, at[1]]], axis=0)
            s = dot(k_g, q_two, 1, 1) + jnp.concatenate([bias[...]] * 2, axis=1)
            return at, s, dot(v_g, g_two, 1, 1)

        ahead = products(0)
        for i in range(0, GROUP, 2):
            at, s, d_prob = ahead
            if i + 2 < GROUP:
                ahead = products(i + 2)
            weights = jnp.exp2((s - jnp.max(s, axis=0, keepdims=True)) * to_log2)
            inverse = 1.0 / jnp.sum(weights, axis=0, keepdims=True)
            delta = jnp.sum(weights * d_prob, axis=0, keepdims=True) * inverse
            dscore = (weights * (d_prob - delta)).astype(BF16)
            dq = dot(kt_g, dscore, 1, 0) * (inverse * scale)
            dq_turned[at[0], :] = dq[:, :tok].astype(BF16)
            dq_turned[at[1], :] = dq[:, tok:].astype(BF16)
        return carry

    lax.fori_loop(0, n_kv, one_group, 0)
    if not up_refs:
        return

    facts_ref, act_ref, dq_before = before
    rank = act_ref.shape[0]
    n_quarters, per, _, part = up_refs[0].shape
    n_groups = per * len(up_refs)
    own = group_rows(rank, n_groups, tok, seq, by_slot) == facts_ref[2:3, :]
    act = jnp.concatenate([act_ref[...].astype(F32)] * n_groups, axis=0)
    act_cols = jnp.where(own, act, 0.0).astype(BF16)
    n_before = dq_before.shape[0] // part
    for quarter in range(n_quarters):
        i, dq_ref = (quarter, dq_before) if quarter < n_before else (quarter - n_before, dq_turned)
        up = dot(act_cols, dq_ref[i * part : (i + 1) * part, :], 1, 1).astype(BF16)
        j = head ^ quarter if by_slot else quarter
        for n in range(n_groups):
            up_refs[n // per][j, n % per] = up[n * rank : (n + 1) * rank, :]


def rank_kernel(by_slot, n_w, facts_ref, *refs):
    w_refs, (dq_a, dq_b, out_ref) = refs[:n_w], refs[n_w:]
    tok = dq_a.shape[1]
    seq, head = lax.axis_index("seq"), lax.axis_index("head")
    n_adapters, n_quarters, rank, part = w_refs[0].shape
    adapter = facts_ref[1:2, :]
    total = jnp.zeros((rank, tok), F32)
    n_a = dq_a.shape[0] // part
    for c, w_ref in enumerate(w_refs):
        rows = None
        for quarter in range(n_quarters):
            j = lax.rem(head + n_quarters - quarter, n_quarters) if by_slot else quarter
            i, dq_ref = (quarter, dq_a) if quarter < n_a else (quarter - n_a, dq_b)
            dq = dq_ref[i * part : (i + 1) * part, :]
            new = dot(w_ref[:, j].reshape(n_adapters * rank, part), dq, 1, 0)
            rows = new if rows is None else rows + new
        for m in range(n_adapters):
            a = (2 * m + c) ^ seq if by_slot else m
            total = total + jnp.where(adapter == a, rows[m * rank : (m + 1) * rank, :], 0.0)
    out_ref[...] = total.astype(BF16)


def down_kernel(by_slot, facts_ref, x_ref, rank_ref, *out_refs):
    rank, tok = rank_ref.shape
    seq, head = lax.axis_index("seq"), lax.axis_index("head")
    per, n_quarters, _, x_part = out_refs[0].shape
    n_groups = per * len(out_refs)
    own = group_rows(rank, n_groups, tok, seq, by_slot) == facts_ref[2:3, :]
    low = jnp.concatenate([rank_ref[...].astype(F32)] * n_groups, axis=0)
    cols = jnp.where(own, low, 0.0).astype(BF16)
    step = min(512, x_part)
    for j in range(n_quarters):
        quarter = head ^ j if by_slot else j
        for start in range(0, x_part, step):
            at = pl.ds(pl.multiple_of(quarter * x_part + start, step), step)
            down = dot(cols, x_ref[:, at], 1, 0).astype(BF16)
            for n in range(n_groups):
                piece = down[n * rank : (n + 1) * rank, :]
                out_refs[n // per][n % per, j, :, start : start + step] = piece


def sum_kernel(a_ref, b_ref, *out_refs):
    for i, out_ref in enumerate(out_refs):
        out_ref[...] = (a_ref[i].astype(F32) + b_ref[i].astype(F32)).astype(BF16)


def token_facts(tok, lengths, adapters, owner, by_slot):
    n_seg = lengths.shape[0]
    cube = (8, n_seg, n_seg)
    row, at, k = (lax.broadcasted_iota(I32, cube, d) for d in range(3))
    length = jnp.broadcast_to(lengths[None, None, :], cube)
    adapter = jnp.broadcast_to(adapters[None, None, :], cube)
    if by_slot:
        hit = jnp.broadcast_to(adapters[None, :, None], cube) == k
        group = jnp.where(hit, jnp.broadcast_to(owner[None, None, :], cube), 0)
    else:
        group = jnp.where(k == at, k, 0)
    terms = jnp.where(row == 2, group, 0)
    terms = jnp.where((row == 0) & (k < at), length, terms)
    terms = jnp.where((row == 1) & (k == at), adapter, terms)
    terms = jnp.where((row == 3) & (k <= at), length, terms)
    told = jnp.sum(terms, axis=2)
    position = lax.axis_index("head") * tok + jnp.arange(tok, dtype=I32)
    inside = (position >= told[0][:, None]) & (position < told[3][:, None])
    return jnp.sum(jnp.where(inside[None], told[:, :, None], 0), axis=1)


def shifted(x, n_head, j):
    return lax.ppermute(x, "head", [(i, (i + j) % n_head) for i in range(n_head)])


def across(x, n_head, j):
    return lax.ppermute(x, "head", [(i, i ^ j) for i in range(n_head)])


def partnered(x, n_seq, bits):
    return lax.ppermute(x, "seq", [(i, i ^ bits) for i in range(n_seq)])


def on_device(
    queries, keys, values, output_gradient, inputs, adapter_activation,
    adapter_up_weight, segment_length, segment_adapter, owner,
):
    n_head = lax.axis_size("head")
    n_seq = lax.axis_size("seq")
    tok, width = queries.shape
    pack = tok * n_head
    rank = adapter_up_weight.shape[1]
    n_adapters = owner.shape[0]
    n_seg = segment_length.shape[1]
    by_slot = n_adapters == n_seq == n_seg == 8 and n_head == 4
    facts = token_facts(tok, segment_length[0], segment_adapter[0], owner, by_slot)

    reach = []
    while sum(reach) < pack * 3 // 8:
        reach.append(min(pack * 3 // 8 - sum(reach), tok))
    key_rows = tok + sum(reach)
    own = jnp.concatenate([keys, values], axis=1)
    parts = [own]
    for hop, rows in enumerate(reach, 1):
        shift = [(i, i + hop) for i in range(n_head - hop)]
        parts.insert(0, lax.ppermute(own[tok - rows :], "head", shift))

    if by_slot:
        w = [adapter_up_weight] + [shifted(adapter_up_weight, n_head, j) for j in range(1, n_head)]
        w = jnp.concatenate(w, axis=0)[None]
        w = [w] + [partnered(w, n_seq, 2 * m) for m in range(1, n_seq // 2)]
    else:
        w = lax.all_gather(adapter_up_weight, "seq", axis=0, tiled=True)
        up_weight = [lax.all_gather(w, "head", axis=1, tiled=False)]

    n_out = 2 if by_slot else 1
    n_groups = n_seq if by_slot else n_seg
    part = width // n_head
    x_part = inputs.shape[1] // n_head
    params = pltpu.CompilerParams(vmem_limit_bytes=32 * 2**20)

    laid_out = pl.pallas_call(
        functools.partial(layout_kernel, len(parts)),
        out_shape=[
            jax.ShapeDtypeStruct((key_rows, keys.shape[1]), BF16),
            jax.ShapeDtypeStruct((key_rows, keys.shape[1]), BF16),
            jax.ShapeDtypeStruct((keys.shape[1], key_rows), BF16),
            jax.ShapeDtypeStruct((key_rows, tok), F32),
        ],
        in_specs=[VMEM] * (2 + len(parts)),
        out_specs=[VMEM] * 4,
        compiler_params=params,
        cost_estimate=pl.CostEstimate(
            flops=0, bytes_accessed=LAYOUT_BYTES, transcendentals=0
        ),
        name="layout",
    )(facts, keys.T, *parts)
    halves = 2
    n_kv = KEY_VALUE_HEADS // halves
    half = width // halves

    def attention(h, before, up_shapes):
        return pl.pallas_call(
            functools.partial(attention_kernel, by_slot, h * n_kv, n_kv),
            out_shape=[jax.ShapeDtypeStruct((half, tok), BF16)] + up_shapes,
            in_specs=[VMEM] * 4 + [ANY] * 2 + [VMEM] * len(before),
            out_specs=[VMEM] * (1 + len(up_shapes)),
            scratch_shapes=[
                pltpu.VMEM((tok, half), BF16),
                pltpu.VMEM((tok, half), BF16),
                pltpu.SemaphoreType.DMA((n_kv,)),
                pltpu.SemaphoreType.DMA((n_kv,)),
            ],
            compiler_params=params,
            cost_estimate=pl.CostEstimate(
                flops=2 * tok * half * key_rows * 3,
                bytes_accessed=4 * tok * half * 2,
                transcendentals=tok * key_rows * QUERY_HEADS // halves,
            ),
            name="attention_%d" % h,
        )(*laid_out, queries, output_gradient, *before)

    (dq_a,) = attention(0, [], [])
    if by_slot:
        dq_a, w = lax.optimization_barrier((dq_a, w))
        w = jnp.concatenate(w, axis=0)
        up_weight = [w, partnered(w, n_seq, 1)]
    up_shape = jax.ShapeDtypeStruct((n_head, n_groups // n_out, rank, part), BF16)
    dq_b, *up = attention(1, [facts, adapter_activation.T, dq_a], [up_shape] * n_out)

    if by_slot:
        up, up_weight = lax.optimization_barrier((up, up_weight))
    rank_low = pl.pallas_call(
        functools.partial(rank_kernel, by_slot, len(up_weight)),
        out_shape=jax.ShapeDtypeStruct((rank, tok), BF16),
        in_specs=[VMEM] * (3 + len(up_weight)),
        out_specs=VMEM,
        compiler_params=params,
        name="rank_gradient",
    )(facts, *up_weight, dq_a, dq_b)

    down_shape = jax.ShapeDtypeStruct((n_groups // n_out, n_head, rank, x_part), BF16)
    down = pl.pallas_call(
        functools.partial(down_kernel, by_slot),
        out_shape=[down_shape] * n_out,
        in_specs=[VMEM] * 3,
        out_specs=[VMEM] * n_out,
        compiler_params=params,
        cost_estimate=pl.CostEstimate(
            flops=2 * n_groups * rank * tok * inputs.shape[1],
            bytes_accessed=4 * tok * inputs.shape[1] * 2,
            transcendentals=0,
        ),
        name="down_parts",
    )(facts, inputs, rank_low)

    if by_slot:
        down = pl.pallas_call(
            sum_kernel,
            out_shape=[jax.ShapeDtypeStruct(down[0].shape[1:], BF16)] * down[0].shape[0],
            in_specs=[VMEM] * 2,
            out_specs=[VMEM] * down[0].shape[0],
            compiler_params=params,
            cost_estimate=pl.CostEstimate(flops=0, bytes_accessed=SUM_BYTES, transcendentals=0),
            name="core_sum",
        )(down[0], partnered(down[1], n_seq, 1))
        up = over_chips(over_z(over_cores(up, n_seq), n_head, (1, 2, 3)).astype(BF16), n_seq)
        down = over_z(over_chips(down, n_seq).astype(BF16), n_head, (3, 1, 2))
    else:
        up = lax.all_to_all(up[0], "head", split_axis=0, concat_axis=0, tiled=True)
        up = spread(jnp.sum(up.astype(F32), axis=0), segment_adapter, owner, n_seq)
        down = lax.all_to_all(down[0], "head", split_axis=1, concat_axis=1, tiled=True)
        down = spread(jnp.sum(down.astype(F32), axis=1), segment_adapter, owner, n_seq)
    return down.T[None] * ADAPTER_SCALE, up[None] * ADAPTER_SCALE


def over_cores(parts, n_seq):
    keep, send = parts
    return (keep.astype(F32) + partnered(send, n_seq, 1).astype(F32)).astype(BF16)


def added(own, got):
    total = own.astype(F32)
    for piece in got:
        total = total + piece.astype(F32)
    return total


def over_chips(both, n_seq):
    return added(both[0], [partnered(both[m], n_seq, 2 * m) for m in range(1, n_seq // 2)])


def over_z(both, n_head, order):
    return added(both[0], [across(both[j], n_head, j) for j in order])


def spread(part, segment_adapter, owner, n_seq):
    goes_to = owner[segment_adapter[0]]
    slots = (goes_to[:, None] == jnp.arange(n_seq, dtype=I32)[None, :]).astype(F32)
    slotted = jnp.einsum("srw,so->orw", part, slots, precision=lax.Precision.HIGHEST)
    slotted = lax.all_to_all(slotted.astype(BF16), "seq", split_axis=0, concat_axis=0, tiled=True)
    return jnp.sum(slotted.astype(F32), axis=0)


def solution(mesh):
    return jax.shard_map(
        on_device,
        mesh=mesh,
        in_specs=(
            P(("seq", "head"), None),
            P(("seq", "head"), None),
            P(("seq", "head"), None),
            P(("seq", "head"), None),
            P(("seq", "head"), None),
            P(("seq", "head"), None),
            P("seq", None, "head"),
            P("seq", None),
            P("seq", None),
            P(),
        ),
        out_specs=(P("seq", "head", None), P("seq", None, "head")),
        check_vma=False,
    )
```

```python
import functools
import math

import jax
import jax.numpy as jnp
from jax import lax
from jax.experimental import pallas as pl
from jax.experimental.pallas import tpu as pltpu
from jax.sharding import PartitionSpec as P

QUERY_HEADS = 32
KEY_VALUE_HEADS = 4
HEAD_SIZE = 128
GROUP = QUERY_HEADS // KEY_VALUE_HEADS
ADAPTER_SCALE = 2.0
NEVER = -1e30
LAYOUT_BYTES = 16 * 2**20
SUM_BYTES = 16 * 2**20
BF16 = jnp.bfloat16
F32 = jnp.float32
I32 = jnp.int32
VMEM = pl.BlockSpec(memory_space=pltpu.VMEM)
ANY = pl.BlockSpec(memory_space=pl.ANY)


def dot(a, b, a_dim, b_dim):
    return lax.dot_general(a, b, (((a_dim,), (b_dim,)), ((), ())), preferred_element_type=F32)


def group_rows(rows_of_group, n_groups, width, seq, by_slot):
    row = lax.broadcasted_iota(I32, (n_groups * rows_of_group, width), 0) // rows_of_group
    if by_slot:
        half = n_groups // 2
        row = jnp.where(row < half, row * 2, (row - half) * 2 + 1) ^ seq
    return row


def layout_kernel(n_parts, facts_ref, *refs):
    own_turned, *parts = refs[: n_parts + 1]
    k_all, v_all, k_turned, bias = refs[n_parts + 1 :]
    tok = facts_ref.shape[1]
    kv_width = v_all.shape[1]
    key_rows = v_all.shape[0]
    head = lax.axis_index("head")
    position = head * tok + lax.broadcasted_iota(I32, (1, tok), 1)
    key_position = (
        head * tok - (key_rows - tok) + lax.broadcasted_iota(I32, (key_rows, tok), 0)
    )
    allowed = (key_position >= facts_ref[0:1, :]) & (key_position <= position)
    bias[...] = jnp.where(allowed, 0.0, NEVER)
    for kv in range(KEY_VALUE_HEADS):
        start = 0
        at = slice(kv * HEAD_SIZE, (kv + 1) * HEAD_SIZE)
        for part in parts:
            rows = part.shape[0]
            k_all[start : start + rows, at] = part[:, at]
            v_all[start : start + rows, at] = part[:, kv_width + at.start : kv_width + at.stop]
            start += rows
        k_turned[at, : start - tok] = k_all[: start - tok, at].T
        k_turned[at, start - tok :] = own_turned[at, :]


def attention_kernel(by_slot, first_kv, n_kv, k_all, v_all, k_turned, bias, q_hbm, g_hbm, *refs):
    before, refs = (refs[:3], refs[3:]) if first_kv else ((), refs)
    dq_turned, *up_refs, q_ref, g_ref, q_sem, g_sem = refs
    tok = q_ref.shape[0]
    seq, head = lax.axis_index("seq"), lax.axis_index("head")
    per_kv = GROUP * HEAD_SIZE

    def fetch(kv):
        to = pl.ds(kv * per_kv, per_kv)
        at = pl.ds((first_kv + kv) * per_kv, per_kv)
        return (
            pltpu.make_async_copy(q_hbm.at[:, at], q_ref.at[:, to], q_sem.at[kv]),
            pltpu.make_async_copy(g_hbm.at[:, at], g_ref.at[:, to], g_sem.at[kv]),
        )

    for kv in range(n_kv):
        for copy in fetch(kv):
            copy.start()

    scale = 1.0 / HEAD_SIZE**0.5
    to_log2 = scale * math.log2(math.e)

    def products(kv, i):
        if i == 0:
            for copy in fetch(kv):
                copy.wait()
        at_kv = slice((first_kv + kv) * HEAD_SIZE, (first_kv + kv + 1) * HEAD_SIZE)
        first = (kv * GROUP + i) * HEAD_SIZE
        at = [slice(first + n * HEAD_SIZE, first + (n + 1) * HEAD_SIZE) for n in range(2)]
        q_two = jnp.concatenate([q_ref[:, at[0]], q_ref[:, at[1]]], axis=0)
        g_two = jnp.concatenate([g_ref[:, at[0]], g_ref[:, at[1]]], axis=0)
        s = dot(k_all[:, at_kv], q_two, 1, 1) + jnp.concatenate([bias[...]] * 2, axis=1)
        return at, at_kv, s, dot(v_all[:, at_kv], g_two, 1, 1)

    def softmax(at, at_kv, s, d_prob):
        weights = jnp.exp2((s - jnp.max(s, axis=0, keepdims=True)) * to_log2)
        inverse = 1.0 / jnp.sum(weights, axis=0, keepdims=True)
        delta = jnp.sum(weights * d_prob, axis=0, keepdims=True) * inverse
        return at, at_kv, (weights * (d_prob - delta)).astype(BF16), inverse * scale

    def finish(at, at_kv, dscore, factor):
        dq = dot(k_turned[at_kv, :], dscore, 1, 0) * factor
        dq_turned[at[0], :] = dq[:, :tok].astype(BF16)
        dq_turned[at[1], :] = dq[:, tok:].astype(BF16)

    pairs = [(kv, i) for kv in range(n_kv) for i in range(0, GROUP, 2)]
    ahead, behind = products(*pairs[0]), None
    for n in range(len(pairs)):
        now = ahead
        if n + 1 < len(pairs):
            ahead = products(*pairs[n + 1])
        if behind is not None:
            finish(*behind)
        behind = softmax(*now)
    finish(*behind)
    if not up_refs:
        return

    facts_ref, act_ref, dq_before = before
    rank = act_ref.shape[0]
    n_quarters, per, _, part = up_refs[0].shape
    n_groups = per * len(up_refs)
    own = group_rows(rank, n_groups, tok, seq, by_slot) == facts_ref[2:3, :]
    act = jnp.concatenate([act_ref[...].astype(F32)] * n_groups, axis=0)
    act_cols = jnp.where(own, act, 0.0).astype(BF16)
    n_before = dq_before.shape[0] // part
    for quarter in range(n_quarters):
        i, dq_ref = (quarter, dq_before) if quarter < n_before else (quarter - n_before, dq_turned)
        up = dot(act_cols, dq_ref[i * part : (i + 1) * part, :], 1, 1).astype(BF16)
        j = head ^ quarter if by_slot else quarter
        for n in range(n_groups):
            up_refs[n // per][j, n % per] = up[n * rank : (n + 1) * rank, :]


def rank_kernel(by_slot, n_w, facts_ref, *refs):
    w_refs, (dq_a, dq_b, out_ref) = refs[:n_w], refs[n_w:]
    tok = dq_a.shape[1]
    seq, head = lax.axis_index("seq"), lax.axis_index("head")
    n_adapters, n_quarters, rank, part = w_refs[0].shape
    adapter = facts_ref[1:2, :]
    total = jnp.zeros((rank, tok), F32)
    n_a = dq_a.shape[0] // part
    for c, w_ref in enumerate(w_refs):
        rows = None
        for quarter in range(n_quarters):
            j = lax.rem(head + n_quarters - quarter, n_quarters) if by_slot else quarter
            i, dq_ref = (quarter, dq_a) if quarter < n_a else (quarter - n_a, dq_b)
            dq = dq_ref[i * part : (i + 1) * part, :]
            new = dot(w_ref[:, j].reshape(n_adapters * rank, part), dq, 1, 0)
            rows = new if rows is None else rows + new
        for m in range(n_adapters):
            a = (2 * m + c) ^ seq if by_slot else m
            total = total + jnp.where(adapter == a, rows[m * rank : (m + 1) * rank, :], 0.0)
    out_ref[...] = total.astype(BF16)


def down_kernel(by_slot, facts_ref, x_ref, rank_ref, *out_refs):
    rank, tok = rank_ref.shape
    seq, head = lax.axis_index("seq"), lax.axis_index("head")
    per, n_quarters, _, x_part = out_refs[0].shape
    n_groups = per * len(out_refs)
    own = group_rows(rank, n_groups, tok, seq, by_slot) == facts_ref[2:3, :]
    low = jnp.concatenate([rank_ref[...].astype(F32)] * n_groups, axis=0)
    cols = jnp.where(own, low, 0.0).astype(BF16)
    step = min(512, x_part)
    for j in range(n_quarters):
        quarter = head ^ j if by_slot else j
        for start in range(0, x_part, step):
            at = pl.ds(pl.multiple_of(quarter * x_part + start, step), step)
            down = dot(cols, x_ref[:, at], 1, 0).astype(BF16)
            for n in range(n_groups):
                piece = down[n * rank : (n + 1) * rank, :]
                out_refs[n // per][n % per, j, :, start : start + step] = piece


def sum_kernel(a_ref, b_ref, *out_refs):
    for i, out_ref in enumerate(out_refs):
        out_ref[...] = (a_ref[i].astype(F32) + b_ref[i].astype(F32)).astype(BF16)


def token_facts(tok, lengths, adapters, owner, by_slot):
    n_seg = lengths.shape[0]
    cube = (8, n_seg, n_seg)
    row, at, k = (lax.broadcasted_iota(I32, cube, d) for d in range(3))
    length = jnp.broadcast_to(lengths[None, None, :], cube)
    adapter = jnp.broadcast_to(adapters[None, None, :], cube)
    if by_slot:
        hit = jnp.broadcast_to(adapters[None, :, None], cube) == k
        group = jnp.where(hit, jnp.broadcast_to(owner[None, None, :], cube), 0)
    else:
        group = jnp.where(k == at, k, 0)
    terms = jnp.where(row == 2, group, 0)
    terms = jnp.where((row == 0) & (k < at), length, terms)
    terms = jnp.where((row == 1) & (k == at), adapter, terms)
    terms = jnp.where((row == 3) & (k <= at), length, terms)
    told = jnp.sum(terms, axis=2)
    position = lax.axis_index("head") * tok + jnp.arange(tok, dtype=I32)
    inside = (position >= told[0][:, None]) & (position < told[3][:, None])
    return jnp.sum(jnp.where(inside[None], told[:, :, None], 0), axis=1)


def shifted(x, n_head, j):
    return lax.ppermute(x, "head", [(i, (i + j) % n_head) for i in range(n_head)])


def across(x, n_head, j):
    return lax.ppermute(x, "head", [(i, i ^ j) for i in range(n_head)])


def partnered(x, n_seq, bits):
    return lax.ppermute(x, "seq", [(i, i ^ bits) for i in range(n_seq)])


def on_device(
    queries, keys, values, output_gradient, inputs, adapter_activation,
    adapter_up_weight, segment_length, segment_adapter, owner,
):
    n_head = lax.axis_size("head")
    n_seq = lax.axis_size("seq")
    tok, width = queries.shape
    pack = tok * n_head
    rank = adapter_up_weight.shape[1]
    n_adapters = owner.shape[0]
    n_seg = segment_length.shape[1]
    by_slot = n_adapters == n_seq == n_seg == 8 and n_head == 4
    facts = token_facts(tok, segment_length[0], segment_adapter[0], owner, by_slot)

    reach = []
    while sum(reach) < pack * 3 // 8:
        reach.append(min(pack * 3 // 8 - sum(reach), tok))
    key_rows = tok + sum(reach)
    own = jnp.concatenate([keys, values], axis=1)
    parts = [own]
    for hop, rows in enumerate(reach, 1):
        shift = [(i, i + hop) for i in range(n_head - hop)]
        parts.insert(0, lax.ppermute(own[tok - rows :], "head", shift))

    if by_slot:
        w = [adapter_up_weight] + [shifted(adapter_up_weight, n_head, j) for j in range(1, n_head)]
        w = jnp.concatenate(w, axis=0)[None]
        w = [w] + [partnered(w, n_seq, 2 * m) for m in range(1, n_seq // 2)]
    else:
        w = lax.all_gather(adapter_up_weight, "seq", axis=0, tiled=True)
        up_weight = [lax.all_gather(w, "head", axis=1, tiled=False)]

    n_out = 2 if by_slot else 1
    n_groups = n_seq if by_slot else n_seg
    part = width // n_head
    x_part = inputs.shape[1] // n_head
    params = pltpu.CompilerParams(vmem_limit_bytes=32 * 2**20)

    laid_out = pl.pallas_call(
        functools.partial(layout_kernel, len(parts)),
        out_shape=[
            jax.ShapeDtypeStruct((key_rows, keys.shape[1]), BF16),
            jax.ShapeDtypeStruct((key_rows, keys.shape[1]), BF16),
            jax.ShapeDtypeStruct((keys.shape[1], key_rows), BF16),
            jax.ShapeDtypeStruct((key_rows, tok), F32),
        ],
        in_specs=[VMEM] * (2 + len(parts)),
        out_specs=[VMEM] * 4,
        compiler_params=params,
        cost_estimate=pl.CostEstimate(
            flops=0, bytes_accessed=LAYOUT_BYTES, transcendentals=0
        ),
        name="layout",
    )(facts, keys.T, *parts)
    halves = 2
    n_kv = KEY_VALUE_HEADS // halves
    half = width // halves

    def attention(h, before, up_shapes):
        return pl.pallas_call(
            functools.partial(attention_kernel, by_slot, h * n_kv, n_kv),
            out_shape=[jax.ShapeDtypeStruct((half, tok), BF16)] + up_shapes,
            in_specs=[VMEM] * 4 + [ANY] * 2 + [VMEM] * len(before),
            out_specs=[VMEM] * (1 + len(up_shapes)),
            scratch_shapes=[
                pltpu.VMEM((tok, half), BF16),
                pltpu.VMEM((tok, half), BF16),
                pltpu.SemaphoreType.DMA((n_kv,)),
                pltpu.SemaphoreType.DMA((n_kv,)),
            ],
            compiler_params=params,
            cost_estimate=pl.CostEstimate(
                flops=2 * tok * half * key_rows * 3,
                bytes_accessed=4 * tok * half * 2,
                transcendentals=tok * key_rows * QUERY_HEADS // halves,
            ),
            name="attention_%d" % h,
        )(*laid_out, queries, output_gradient, *before)

    (dq_a,) = attention(0, [], [])
    if by_slot:
        dq_a, w = lax.optimization_barrier((dq_a, w))
        w = jnp.concatenate(w, axis=0)
        up_weight = [w, partnered(w, n_seq, 1)]
    up_shape = jax.ShapeDtypeStruct((n_head, n_groups // n_out, rank, part), BF16)
    dq_b, *up = attention(1, [facts, adapter_activation.T, dq_a], [up_shape] * n_out)

    if by_slot:
        up, up_weight = lax.optimization_barrier((up, up_weight))
    rank_low = pl.pallas_call(
        functools.partial(rank_kernel, by_slot, len(up_weight)),
        out_shape=jax.ShapeDtypeStruct((rank, tok), BF16),
        in_specs=[VMEM] * (3 + len(up_weight)),
        out_specs=VMEM,
        compiler_params=params,
        name="rank_gradient",
    )(facts, *up_weight, dq_a, dq_b)

    down_shape = jax.ShapeDtypeStruct((n_groups // n_out, n_head, rank, x_part), BF16)
    down = pl.pallas_call(
        functools.partial(down_kernel, by_slot),
        out_shape=[down_shape] * n_out,
        in_specs=[VMEM] * 3,
        out_specs=[VMEM] * n_out,
        compiler_params=params,
        cost_estimate=pl.CostEstimate(
            flops=2 * n_groups * rank * tok * inputs.shape[1],
            bytes_accessed=4 * tok * inputs.shape[1] * 2,
            transcendentals=0,
        ),
        name="down_parts",
    )(facts, inputs, rank_low)

    if by_slot:
        down = pl.pallas_call(
            sum_kernel,
            out_shape=[jax.ShapeDtypeStruct(down[0].shape[1:], BF16)] * down[0].shape[0],
            in_specs=[VMEM] * 2,
            out_specs=[VMEM] * down[0].shape[0],
            compiler_params=params,
            cost_estimate=pl.CostEstimate(flops=0, bytes_accessed=SUM_BYTES, transcendentals=0),
            name="core_sum",
        )(down[0], partnered(down[1], n_seq, 1))
        up = over_chips(over_z(over_cores(up, n_seq), n_head, (1, 2, 3)).astype(BF16), n_seq)
        down = over_z(over_chips(down, n_seq).astype(BF16), n_head, (3, 1, 2))
    else:
        up = lax.all_to_all(up[0], "head", split_axis=0, concat_axis=0, tiled=True)
        up = spread(jnp.sum(up.astype(F32), axis=0), segment_adapter, owner, n_seq)
        down = lax.all_to_all(down[0], "head", split_axis=1, concat_axis=1, tiled=True)
        down = spread(jnp.sum(down.astype(F32), axis=1), segment_adapter, owner, n_seq)
    return down.T[None] * ADAPTER_SCALE, up[None] * ADAPTER_SCALE


def over_cores(parts, n_seq):
    keep, send = parts
    return (keep.astype(F32) + partnered(send, n_seq, 1).astype(F32)).astype(BF16)


def added(own, got):
    total = own.astype(F32)
    for piece in got:
        total = total + piece.astype(F32)
    return total


def over_chips(both, n_seq):
    return added(both[0], [partnered(both[m], n_seq, 2 * m) for m in range(1, n_seq // 2)])


def over_z(both, n_head, order):
    return added(both[0], [across(both[j], n_head, j) for j in order])


def spread(part, segment_adapter, owner, n_seq):
    goes_to = owner[segment_adapter[0]]
    slots = (goes_to[:, None] == jnp.arange(n_seq, dtype=I32)[None, :]).astype(F32)
    slotted = jnp.einsum("srw,so->orw", part, slots, precision=lax.Precision.HIGHEST)
    slotted = lax.all_to_all(slotted.astype(BF16), "seq", split_axis=0, concat_axis=0, tiled=True)
    return jnp.sum(slotted.astype(F32), axis=0)


def solution(mesh):
    return jax.shard_map(
        on_device,
        mesh=mesh,
        in_specs=(
            P(("seq", "head"), None),
            P(("seq", "head"), None),
            P(("seq", "head"), None),
            P(("seq", "head"), None),
            P(("seq", "head"), None),
            P(("seq", "head"), None),
            P("seq", None, "head"),
            P("seq", None),
            P("seq", None),
            P(),
        ),
        out_specs=(P("seq", "head", None), P("seq", None, "head")),
        check_vma=False,
    )
```

```python
import functools
import math

import jax
import jax.numpy as jnp
from jax import lax
from jax.experimental import pallas as pl
from jax.experimental.pallas import tpu as pltpu
from jax.sharding import PartitionSpec as P

QUERY_HEADS = 32
KEY_VALUE_HEADS = 4
HEAD_SIZE = 128
GROUP = QUERY_HEADS // KEY_VALUE_HEADS
ADAPTER_SCALE = 2.0
NEVER = -1e30
LAYOUT_BYTES = 16 * 2**20
SUM_BYTES = 16 * 2**20
BF16 = jnp.bfloat16
F32 = jnp.float32
I32 = jnp.int32
VMEM = pl.BlockSpec(memory_space=pltpu.VMEM)
ANY = pl.BlockSpec(memory_space=pl.ANY)


def dot(a, b, a_dim, b_dim):
    return lax.dot_general(a, b, (((a_dim,), (b_dim,)), ((), ())), preferred_element_type=F32)


def group_rows(rows_of_group, n_groups, width, seq, by_slot):
    row = lax.broadcasted_iota(I32, (n_groups * rows_of_group, width), 0) // rows_of_group
    if by_slot:
        half = n_groups // 2
        row = jnp.where(row < half, row * 2, (row - half) * 2 + 1) ^ seq
    return row


def layout_kernel(n_parts, facts_ref, *refs):
    own_turned, *parts = refs[: n_parts + 1]
    k_all, v_all, k_turned, bias = refs[n_parts + 1 :]
    tok = facts_ref.shape[1]
    kv_width = v_all.shape[1]
    key_rows = v_all.shape[0]
    head = lax.axis_index("head")
    position = head * tok + lax.broadcasted_iota(I32, (1, tok), 1)
    key_position = (
        head * tok - (key_rows - tok) + lax.broadcasted_iota(I32, (key_rows, tok), 0)
    )
    allowed = (key_position >= facts_ref[0:1, :]) & (key_position <= position)
    bias[...] = jnp.where(allowed, 0.0, NEVER)
    for kv in range(KEY_VALUE_HEADS):
        start = 0
        at = slice(kv * HEAD_SIZE, (kv + 1) * HEAD_SIZE)
        for part in parts:
            rows = part.shape[0]
            k_all[start : start + rows, at] = part[:, at]
            v_all[start : start + rows, at] = part[:, kv_width + at.start : kv_width + at.stop]
            start += rows
        k_turned[at, : start - tok] = k_all[: start - tok, at].T
        k_turned[at, start - tok :] = own_turned[at, :]


def attention_kernel(by_slot, first_kv, n_kv, k_all, v_all, k_turned, bias, q_hbm, g_hbm, *refs):
    before, refs = (refs[:3], refs[3:]) if first_kv else ((), refs)
    dq_turned, *up_refs, q_ref, g_ref, q_sem, g_sem = refs
    tok = q_ref.shape[0]
    seq, head = lax.axis_index("seq"), lax.axis_index("head")
    per_kv = GROUP * HEAD_SIZE

    def fetch(kv):
        to = pl.ds(kv * per_kv, per_kv)
        at = pl.ds((first_kv + kv) * per_kv, per_kv)
        return (
            pltpu.make_async_copy(q_hbm.at[:, at], q_ref.at[:, to], q_sem.at[kv]),
            pltpu.make_async_copy(g_hbm.at[:, at], g_ref.at[:, to], g_sem.at[kv]),
        )

    for kv in range(n_kv):
        for copy in fetch(kv):
            copy.start()

    scale = 1.0 / HEAD_SIZE**0.5
    to_log2 = scale * math.log2(math.e)

    def products(kv, i):
        if i == 0:
            for copy in fetch(kv):
                copy.wait()
        at_kv = slice((first_kv + kv) * HEAD_SIZE, (first_kv + kv + 1) * HEAD_SIZE)
        first = (kv * GROUP + i) * HEAD_SIZE
        at = [slice(first + n * HEAD_SIZE, first + (n + 1) * HEAD_SIZE) for n in range(2)]
        q_two = jnp.concatenate([q_ref[:, at[0]], q_ref[:, at[1]]], axis=0)
        g_two = jnp.concatenate([g_ref[:, at[0]], g_ref[:, at[1]]], axis=0)
        s = dot(k_all[:, at_kv], q_two, 1, 1) + jnp.concatenate([bias[...]] * 2, axis=1)
        return at, at_kv, s, dot(v_all[:, at_kv], g_two, 1, 1)

    def softmax(at, at_kv, s, d_prob):
        weights = jnp.exp2((s - jnp.max(s, axis=0, keepdims=True)) * to_log2)
        inverse = 1.0 / jnp.sum(weights, axis=0, keepdims=True)
        delta = jnp.sum(weights * d_prob, axis=0, keepdims=True) * inverse
        return at, at_kv, (weights * (d_prob - delta)).astype(BF16), inverse * scale

    def finish(at, at_kv, dscore, factor):
        dq = dot(k_turned[at_kv, :], dscore, 1, 0) * factor
        dq_turned[at[0], :] = dq[:, :tok].astype(BF16)
        dq_turned[at[1], :] = dq[:, tok:].astype(BF16)

    pairs = [(kv, i) for kv in range(n_kv) for i in range(0, GROUP, 2)]
    ahead, behind = products(*pairs[0]), None
    for n in range(len(pairs)):
        now = ahead
        if n + 1 < len(pairs):
            ahead = products(*pairs[n + 1])
        if behind is not None:
            finish(*behind)
        behind = softmax(*now)
    finish(*behind)
    if not up_refs:
        return

    facts_ref, act_ref, dq_before = before
    rank = act_ref.shape[0]
    n_quarters, per, _, part = up_refs[0].shape
    n_groups = per * len(up_refs)
    own = group_rows(rank, n_groups, tok, seq, by_slot) == facts_ref[2:3, :]
    act = jnp.concatenate([act_ref[...].astype(F32)] * n_groups, axis=0)
    act_cols = jnp.where(own, act, 0.0).astype(BF16)
    n_before = dq_before.shape[0] // part
    for quarter in range(n_quarters):
        i, dq_ref = (quarter, dq_before) if quarter < n_before else (quarter - n_before, dq_turned)
        up = dot(act_cols, dq_ref[i * part : (i + 1) * part, :], 1, 1).astype(BF16)
        j = head ^ quarter if by_slot else quarter
        for n in range(n_groups):
            up_refs[n // per][j, n % per] = up[n * rank : (n + 1) * rank, :]


def rank_kernel(by_slot, n_w, facts_ref, *refs):
    w_refs, (dq_a, dq_b, out_ref) = refs[:n_w], refs[n_w:]
    tok = dq_a.shape[1]
    seq, head = lax.axis_index("seq"), lax.axis_index("head")
    n_adapters, n_quarters, rank, part = w_refs[0].shape
    adapter = facts_ref[1:2, :]
    total = jnp.zeros((rank, tok), F32)
    n_a = dq_a.shape[0] // part
    for c, w_ref in enumerate(w_refs):
        rows = None
        for quarter in range(n_quarters):
            j = lax.rem(head + n_quarters - quarter, n_quarters) if by_slot else quarter
            i, dq_ref = (quarter, dq_a) if quarter < n_a else (quarter - n_a, dq_b)
            dq = dq_ref[i * part : (i + 1) * part, :]
            new = dot(w_ref[:, j].reshape(n_adapters * rank, part), dq, 1, 0)
            rows = new if rows is None else rows + new
        for m in range(n_adapters):
            a = (2 * m + c) ^ seq if by_slot else m
            total = total + jnp.where(adapter == a, rows[m * rank : (m + 1) * rank, :], 0.0)
    out_ref[...] = total.astype(BF16)


def down_kernel(by_slot, facts_ref, x_ref, rank_ref, *out_refs):
    rank, tok = rank_ref.shape
    seq, head = lax.axis_index("seq"), lax.axis_index("head")
    per, n_quarters, _, x_part = out_refs[0].shape
    n_groups = per * len(out_refs)
    own = group_rows(rank, n_groups, tok, seq, by_slot) == facts_ref[2:3, :]
    low = jnp.concatenate([rank_ref[...].astype(F32)] * n_groups, axis=0)
    cols = jnp.where(own, low, 0.0).astype(BF16)
    step = min(512, x_part)
    for j in range(n_quarters):
        quarter = head ^ j if by_slot else j
        for start in range(0, x_part, step):
            at = pl.ds(pl.multiple_of(quarter * x_part + start, step), step)
            down = dot(cols, x_ref[:, at], 1, 0).astype(BF16)
            for n in range(n_groups):
                piece = down[n * rank : (n + 1) * rank, :]
                out_refs[n // per][n % per, j, :, start : start + step] = piece


def sum_kernel(a_ref, b_ref, *out_refs):
    for i, out_ref in enumerate(out_refs):
        out_ref[...] = (a_ref[i].astype(F32) + b_ref[i].astype(F32)).astype(BF16)


def token_facts(tok, lengths, adapters, owner, by_slot):
    n_seg = lengths.shape[0]
    cube = (8, n_seg, n_seg)
    row, at, k = (lax.broadcasted_iota(I32, cube, d) for d in range(3))
    length = jnp.broadcast_to(lengths[None, None, :], cube)
    adapter = jnp.broadcast_to(adapters[None, None, :], cube)
    if by_slot:
        hit = jnp.broadcast_to(adapters[None, :, None], cube) == k
        group = jnp.where(hit, jnp.broadcast_to(owner[None, None, :], cube), 0)
    else:
        group = jnp.where(k == at, k, 0)
    terms = jnp.where(row == 2, group, 0)
    terms = jnp.where((row == 0) & (k < at), length, terms)
    terms = jnp.where((row == 1) & (k == at), adapter, terms)
    terms = jnp.where((row == 3) & (k <= at), length, terms)
    told = jnp.sum(terms, axis=2)
    position = lax.axis_index("head") * tok + jnp.arange(tok, dtype=I32)
    inside = (position >= told[0][:, None]) & (position < told[3][:, None])
    return jnp.sum(jnp.where(inside[None], told[:, :, None], 0), axis=1)


def shifted(x, n_head, j):
    return lax.ppermute(x, "head", [(i, (i + j) % n_head) for i in range(n_head)])


def across(x, n_head, j):
    return lax.ppermute(x, "head", [(i, i ^ j) for i in range(n_head)])


def partnered(x, n_seq, bits):
    return lax.ppermute(x, "seq", [(i, i ^ bits) for i in range(n_seq)])


def on_device(
    queries, keys, values, output_gradient, inputs, adapter_activation,
    adapter_up_weight, segment_length, segment_adapter, owner,
):
    n_head = lax.axis_size("head")
    n_seq = lax.axis_size("seq")
    tok, width = queries.shape
    pack = tok * n_head
    rank = adapter_up_weight.shape[1]
    n_adapters = owner.shape[0]
    n_seg = segment_length.shape[1]
    by_slot = n_adapters == n_seq == n_seg == 8 and n_head == 4

    reach = []
    while sum(reach) < pack * 3 // 8:
        reach.append(min(pack * 3 // 8 - sum(reach), tok))
    key_rows = tok + sum(reach)
    own = jnp.concatenate([keys, values], axis=1)
    parts = [own]
    for hop, rows in enumerate(reach, 1):
        shift = [(i, i + hop) for i in range(n_head - hop)]
        parts.insert(0, lax.ppermute(own[tok - rows :], "head", shift))

    if by_slot:
        w = [adapter_up_weight] + [shifted(adapter_up_weight, n_head, j) for j in range(1, n_head)]
        w = jnp.concatenate(w, axis=0)[None]
        lengths, own_keys, _ = lax.optimization_barrier((segment_length, keys, w))
        w = [w] + [partnered(w, n_seq, 2 * m) for m in range(1, n_seq // 2)]
    else:
        lengths, own_keys = segment_length, keys
        w = lax.all_gather(adapter_up_weight, "seq", axis=0, tiled=True)
        up_weight = [lax.all_gather(w, "head", axis=1, tiled=False)]

    facts = token_facts(tok, lengths[0], segment_adapter[0], owner, by_slot)
    n_out = 2 if by_slot else 1
    n_groups = n_seq if by_slot else n_seg
    part = width // n_head
    x_part = inputs.shape[1] // n_head
    params = pltpu.CompilerParams(vmem_limit_bytes=32 * 2**20)

    laid_out = pl.pallas_call(
        functools.partial(layout_kernel, len(parts)),
        out_shape=[
            jax.ShapeDtypeStruct((key_rows, keys.shape[1]), BF16),
            jax.ShapeDtypeStruct((key_rows, keys.shape[1]), BF16),
            jax.ShapeDtypeStruct((keys.shape[1], key_rows), BF16),
            jax.ShapeDtypeStruct((key_rows, tok), F32),
        ],
        in_specs=[VMEM] * (2 + len(parts)),
        out_specs=[VMEM] * 4,
        compiler_params=params,
        cost_estimate=pl.CostEstimate(
            flops=0, bytes_accessed=LAYOUT_BYTES, transcendentals=0
        ),
        name="layout",
    )(facts, own_keys.T, *parts)
    halves = 2
    n_kv = KEY_VALUE_HEADS // halves
    half = width // halves

    def attention(h, before, up_shapes):
        return pl.pallas_call(
            functools.partial(attention_kernel, by_slot, h * n_kv, n_kv),
            out_shape=[jax.ShapeDtypeStruct((half, tok), BF16)] + up_shapes,
            in_specs=[VMEM] * 4 + [ANY] * 2 + [VMEM] * len(before),
            out_specs=[VMEM] * (1 + len(up_shapes)),
            scratch_shapes=[
                pltpu.VMEM((tok, half), BF16),
                pltpu.VMEM((tok, half), BF16),
                pltpu.SemaphoreType.DMA((n_kv,)),
                pltpu.SemaphoreType.DMA((n_kv,)),
            ],
            compiler_params=params,
            cost_estimate=pl.CostEstimate(
                flops=2 * tok * half * key_rows * 3,
                bytes_accessed=4 * tok * half * 2,
                transcendentals=tok * key_rows * QUERY_HEADS // halves,
            ),
            name="attention_%d" % h,
        )(*laid_out, queries, output_gradient, *before)

    (dq_a,) = attention(0, [], [])
    if by_slot:
        dq_a, w = lax.optimization_barrier((dq_a, w))
        w = jnp.concatenate(w, axis=0)
        up_weight = [w, partnered(w, n_seq, 1)]
    up_shape = jax.ShapeDtypeStruct((n_head, n_groups // n_out, rank, part), BF16)
    dq_b, *up = attention(1, [facts, adapter_activation.T, dq_a], [up_shape] * n_out)

    if by_slot:
        up, up_weight = lax.optimization_barrier((up, up_weight))
    rank_low = pl.pallas_call(
        functools.partial(rank_kernel, by_slot, len(up_weight)),
        out_shape=jax.ShapeDtypeStruct((rank, tok), BF16),
        in_specs=[VMEM] * (3 + len(up_weight)),
        out_specs=VMEM,
        compiler_params=params,
        name="rank_gradient",
    )(facts, *up_weight, dq_a, dq_b)

    down_shape = jax.ShapeDtypeStruct((n_groups // n_out, n_head, rank, x_part), BF16)
    down = pl.pallas_call(
        functools.partial(down_kernel, by_slot),
        out_shape=[down_shape] * n_out,
        in_specs=[VMEM] * 3,
        out_specs=[VMEM] * n_out,
        compiler_params=params,
        cost_estimate=pl.CostEstimate(
            flops=2 * n_groups * rank * tok * inputs.shape[1],
            bytes_accessed=4 * tok * inputs.shape[1] * 2,
            transcendentals=0,
        ),
        name="down_parts",
    )(facts, inputs, rank_low)

    if by_slot:
        down = pl.pallas_call(
            sum_kernel,
            out_shape=[jax.ShapeDtypeStruct(down[0].shape[1:], BF16)] * down[0].shape[0],
            in_specs=[VMEM] * 2,
            out_specs=[VMEM] * down[0].shape[0],
            compiler_params=params,
            cost_estimate=pl.CostEstimate(flops=0, bytes_accessed=SUM_BYTES, transcendentals=0),
            name="core_sum",
        )(down[0], partnered(down[1], n_seq, 1))
        up = over_chips(over_z(over_cores(up, n_seq), n_head, (1, 2, 3)).astype(BF16), n_seq)
        down = over_z(over_chips(down, n_seq).astype(BF16), n_head, (3, 1, 2))
    else:
        up = lax.all_to_all(up[0], "head", split_axis=0, concat_axis=0, tiled=True)
        up = spread(jnp.sum(up.astype(F32), axis=0), segment_adapter, owner, n_seq)
        down = lax.all_to_all(down[0], "head", split_axis=1, concat_axis=1, tiled=True)
        down = spread(jnp.sum(down.astype(F32), axis=1), segment_adapter, owner, n_seq)
    return down.T[None] * ADAPTER_SCALE, up[None] * ADAPTER_SCALE


def over_cores(parts, n_seq):
    keep, send = parts
    return (keep.astype(F32) + partnered(send, n_seq, 1).astype(F32)).astype(BF16)


def added(own, got):
    total = own.astype(F32)
    for piece in got:
        total = total + piece.astype(F32)
    return total


def over_chips(both, n_seq):
    return added(both[0], [partnered(both[m], n_seq, 2 * m) for m in range(1, n_seq // 2)])


def over_z(both, n_head, order):
    return added(both[0], [across(both[j], n_head, j) for j in order])


def spread(part, segment_adapter, owner, n_seq):
    goes_to = owner[segment_adapter[0]]
    slots = (goes_to[:, None] == jnp.arange(n_seq, dtype=I32)[None, :]).astype(F32)
    slotted = jnp.einsum("srw,so->orw", part, slots, precision=lax.Precision.HIGHEST)
    slotted = lax.all_to_all(slotted.astype(BF16), "seq", split_axis=0, concat_axis=0, tiled=True)
    return jnp.sum(slotted.astype(F32), axis=0)


def solution(mesh):
    return jax.shard_map(
        on_device,
        mesh=mesh,
        in_specs=(
            P(("seq", "head"), None),
            P(("seq", "head"), None),
            P(("seq", "head"), None),
            P(("seq", "head"), None),
            P(("seq", "head"), None),
            P(("seq", "head"), None),
            P("seq", None, "head"),
            P("seq", None),
            P("seq", None),
            P(),
        ),
        out_specs=(P("seq", "head", None), P("seq", None, "head")),
        check_vma=False,
    )
```

```python
import functools
import math

import jax
import jax.numpy as jnp
from jax import lax
from jax.experimental import pallas as pl
from jax.experimental.pallas import tpu as pltpu
from jax.sharding import PartitionSpec as P

QUERY_HEADS = 32
KEY_VALUE_HEADS = 4
HEAD_SIZE = 128
GROUP = QUERY_HEADS // KEY_VALUE_HEADS
ADAPTER_SCALE = 2.0
NEVER = -1e30
LAYOUT_BYTES = 16 * 2**20
SUM_BYTES = 16 * 2**20
BF16 = jnp.bfloat16
F32 = jnp.float32
I32 = jnp.int32
VMEM = pl.BlockSpec(memory_space=pltpu.VMEM)
ANY = pl.BlockSpec(memory_space=pl.ANY)


def dot(a, b, a_dim, b_dim):
    return lax.dot_general(a, b, (((a_dim,), (b_dim,)), ((), ())), preferred_element_type=F32)


def group_rows(rows_of_group, n_groups, width, seq, by_slot):
    row = lax.broadcasted_iota(I32, (n_groups * rows_of_group, width), 0) // rows_of_group
    if by_slot:
        half = n_groups // 2
        row = jnp.where(row < half, row * 2, (row - half) * 2 + 1) ^ seq
    return row


def layout_kernel(n_parts, facts_ref, *refs):
    own_turned, *parts = refs[: n_parts + 1]
    k_all, v_all, k_turned, bias = refs[n_parts + 1 :]
    tok = facts_ref.shape[1]
    kv_width = v_all.shape[1]
    key_rows = v_all.shape[0]
    head = lax.axis_index("head")
    position = head * tok + lax.broadcasted_iota(I32, (1, tok), 1)
    key_position = (
        head * tok - (key_rows - tok) + lax.broadcasted_iota(I32, (key_rows, tok), 0)
    )
    allowed = (key_position >= facts_ref[0:1, :]) & (key_position <= position)
    bias[...] = jnp.where(allowed, 0.0, NEVER)
    for kv in range(KEY_VALUE_HEADS):
        start = 0
        at = slice(kv * HEAD_SIZE, (kv + 1) * HEAD_SIZE)
        for part in parts:
            rows = part.shape[0]
            k_all[start : start + rows, at] = part[:, at]
            v_all[start : start + rows, at] = part[:, kv_width + at.start : kv_width + at.stop]
            start += rows
        k_turned[at, : start - tok] = k_all[: start - tok, at].T
        k_turned[at, start - tok :] = own_turned[at, :]


def attention_kernel(by_slot, first_kv, n_kv, k_all, v_all, k_turned, bias, q_hbm, g_hbm, *refs):
    before, refs = (refs[:3], refs[3:]) if first_kv else ((), refs)
    dq_turned, *up_refs, q_ref, g_ref, q_sem, g_sem = refs
    tok = q_ref.shape[0]
    seq, head = lax.axis_index("seq"), lax.axis_index("head")
    per_kv = GROUP * HEAD_SIZE

    def fetch(kv):
        to = pl.ds(kv * per_kv, per_kv)
        at = pl.ds((first_kv + kv) * per_kv, per_kv)
        return (
            pltpu.make_async_copy(q_hbm.at[:, at], q_ref.at[:, to], q_sem.at[kv]),
            pltpu.make_async_copy(g_hbm.at[:, at], g_ref.at[:, to], g_sem.at[kv]),
        )

    for kv in range(n_kv):
        for copy in fetch(kv):
            copy.start()

    scale = 1.0 / HEAD_SIZE**0.5
    to_log2 = scale * math.log2(math.e)

    def products(kv, i):
        if i == 0:
            for copy in fetch(kv):
                copy.wait()
        at_kv = slice((first_kv + kv) * HEAD_SIZE, (first_kv + kv + 1) * HEAD_SIZE)
        first = (kv * GROUP + i) * HEAD_SIZE
        at = [slice(first + n * HEAD_SIZE, first + (n + 1) * HEAD_SIZE) for n in range(2)]
        q_two = jnp.concatenate([q_ref[:, at[0]], q_ref[:, at[1]]], axis=0)
        g_two = jnp.concatenate([g_ref[:, at[0]], g_ref[:, at[1]]], axis=0)
        s = dot(k_all[:, at_kv], q_two, 1, 1) + jnp.concatenate([bias[...]] * 2, axis=1)
        return at, at_kv, s, dot(v_all[:, at_kv], g_two, 1, 1)

    def softmax(at, at_kv, s, d_prob):
        weights = jnp.exp2((s - jnp.max(s, axis=0, keepdims=True)) * to_log2)
        inverse = 1.0 / jnp.sum(weights, axis=0, keepdims=True)
        delta = jnp.sum(weights * d_prob, axis=0, keepdims=True) * inverse
        return at, at_kv, (weights * (d_prob - delta)).astype(BF16), inverse * scale

    def finish(at, at_kv, dscore, factor):
        dq = dot(k_turned[at_kv, :], dscore, 1, 0) * factor
        dq_turned[at[0], :] = dq[:, :tok].astype(BF16)
        dq_turned[at[1], :] = dq[:, tok:].astype(BF16)

    pairs = [(kv, i) for kv in range(n_kv) for i in range(0, GROUP, 2)]
    ahead, behind = products(*pairs[0]), None
    for n in range(len(pairs)):
        now = ahead
        if n + 1 < len(pairs):
            ahead = products(*pairs[n + 1])
        if behind is not None:
            finish(*behind)
        behind = softmax(*now)
    finish(*behind)
    if not up_refs:
        return

    facts_ref, act_ref, dq_before = before
    rank = act_ref.shape[0]
    n_quarters, per, _, part = up_refs[0].shape
    n_groups = per * len(up_refs)
    own = group_rows(rank, n_groups, tok, seq, by_slot) == facts_ref[2:3, :]
    act = jnp.concatenate([act_ref[...].astype(F32)] * n_groups, axis=0)
    act_cols = jnp.where(own, act, 0.0).astype(BF16)
    n_before = dq_before.shape[0] // part
    for quarter in range(n_quarters):
        i, dq_ref = (quarter, dq_before) if quarter < n_before else (quarter - n_before, dq_turned)
        up = dot(act_cols, dq_ref[i * part : (i + 1) * part, :], 1, 1).astype(BF16)
        j = head ^ quarter if by_slot else quarter
        for n in range(n_groups):
            up_refs[n // per][j, n % per] = up[n * rank : (n + 1) * rank, :]


def rank_kernel(by_slot, n_w, facts_ref, *refs):
    w_refs, (dq_a, dq_b, out_ref) = refs[:n_w], refs[n_w:]
    tok = dq_a.shape[1]
    seq, head = lax.axis_index("seq"), lax.axis_index("head")
    n_adapters, n_quarters, rank, part = w_refs[0].shape
    adapter = facts_ref[1:2, :]
    total = jnp.zeros((rank, tok), F32)
    n_a = dq_a.shape[0] // part
    for c, w_ref in enumerate(w_refs):
        rows = None
        for quarter in range(n_quarters):
            j = lax.rem(head + n_quarters - quarter, n_quarters) if by_slot else quarter
            i, dq_ref = (quarter, dq_a) if quarter < n_a else (quarter - n_a, dq_b)
            dq = dq_ref[i * part : (i + 1) * part, :]
            new = dot(w_ref[:, j].reshape(n_adapters * rank, part), dq, 1, 0)
            rows = new if rows is None else rows + new
        for m in range(n_adapters):
            a = (2 * m + c) ^ seq if by_slot else m
            total = total + jnp.where(adapter == a, rows[m * rank : (m + 1) * rank, :], 0.0)
    out_ref[...] = total.astype(BF16)


def down_kernel(by_slot, facts_ref, x_ref, rank_ref, *out_refs):
    rank, tok = rank_ref.shape
    seq, head = lax.axis_index("seq"), lax.axis_index("head")
    per, n_quarters, _, x_part = out_refs[0].shape
    n_groups = per * len(out_refs)
    own = group_rows(rank, n_groups, tok, seq, by_slot) == facts_ref[2:3, :]
    low = jnp.concatenate([rank_ref[...].astype(F32)] * n_groups, axis=0)
    cols = jnp.where(own, low, 0.0).astype(BF16)
    step = min(512, x_part)
    for j in range(n_quarters):
        quarter = head ^ j if by_slot else j
        for start in range(0, x_part, step):
            at = pl.ds(pl.multiple_of(quarter * x_part + start, step), step)
            down = dot(cols, x_ref[:, at], 1, 0).astype(BF16)
            for n in range(n_groups):
                piece = down[n * rank : (n + 1) * rank, :]
                out_refs[n // per][n % per, j, :, start : start + step] = piece


def sum_kernel(a_ref, b_ref, *out_refs):
    for i, out_ref in enumerate(out_refs):
        out_ref[...] = (a_ref[i].astype(F32) + b_ref[i].astype(F32)).astype(BF16)


def token_facts(tok, lengths, adapters, owner, by_slot):
    n_seg = lengths.shape[0]
    cube = (8, n_seg, n_seg)
    row, at, k = (lax.broadcasted_iota(I32, cube, d) for d in range(3))
    length = jnp.broadcast_to(lengths[None, None, :], cube)
    adapter = jnp.broadcast_to(adapters[None, None, :], cube)
    if by_slot:
        hit = jnp.broadcast_to(adapters[None, :, None], cube) == k
        group = jnp.where(hit, jnp.broadcast_to(owner[None, None, :], cube), 0)
    else:
        group = jnp.where(k == at, k, 0)
    terms = jnp.where(row == 2, group, 0)
    terms = jnp.where((row == 0) & (k < at), length, terms)
    terms = jnp.where((row == 1) & (k == at), adapter, terms)
    terms = jnp.where((row == 3) & (k <= at), length, terms)
    told = jnp.sum(terms, axis=2)
    position = lax.axis_index("head") * tok + jnp.arange(tok, dtype=I32)
    inside = (position >= told[0][:, None]) & (position < told[3][:, None])
    return jnp.sum(jnp.where(inside[None], told[:, :, None], 0), axis=1)


def shifted(x, n_head, j):
    return lax.ppermute(x, "head", [(i, (i + j) % n_head) for i in range(n_head)])


def across(x, n_head, j):
    return lax.ppermute(x, "head", [(i, i ^ j) for i in range(n_head)])


def partnered(x, n_seq, bits):
    return lax.ppermute(x, "seq", [(i, i ^ bits) for i in range(n_seq)])


def on_device(
    queries, keys, values, output_gradient, inputs, adapter_activation,
    adapter_up_weight, segment_length, segment_adapter, owner,
):
    n_head = lax.axis_size("head")
    n_seq = lax.axis_size("seq")
    tok, width = queries.shape
    pack = tok * n_head
    rank = adapter_up_weight.shape[1]
    n_adapters = owner.shape[0]
    n_seg = segment_length.shape[1]
    by_slot = n_adapters == n_seq == n_seg == 8 and n_head == 4

    reach = []
    while sum(reach) < pack * 3 // 8:
        reach.append(min(pack * 3 // 8 - sum(reach), tok))
    key_rows = tok + sum(reach)
    own = jnp.concatenate([keys, values], axis=1)
    parts = [own]
    for hop, rows in enumerate(reach, 1):
        shift = [(i, i + hop) for i in range(n_head - hop)]
        parts.insert(0, lax.ppermute(own[tok - rows :], "head", shift))

    if by_slot:
        w = [adapter_up_weight] + [shifted(adapter_up_weight, n_head, j) for j in range(1, n_head)]
        w = jnp.concatenate(w, axis=0)[None]
        lengths, own_keys, _ = lax.optimization_barrier((segment_length, keys, w))
        w = [w] + [partnered(w, n_seq, 2 * m) for m in range(1, n_seq // 2)]
    else:
        lengths, own_keys = segment_length, keys
        w = lax.all_gather(adapter_up_weight, "seq", axis=0, tiled=True)
        up_weight = [lax.all_gather(w, "head", axis=1, tiled=False)]

    facts = token_facts(tok, lengths[0], segment_adapter[0], owner, by_slot)
    n_out = 2 if by_slot else 1
    n_groups = n_seq if by_slot else n_seg
    part = width // n_head
    x_part = inputs.shape[1] // n_head
    params = pltpu.CompilerParams(vmem_limit_bytes=32 * 2**20)

    laid_out = pl.pallas_call(
        functools.partial(layout_kernel, len(parts)),
        out_shape=[
            jax.ShapeDtypeStruct((key_rows, keys.shape[1]), BF16),
            jax.ShapeDtypeStruct((key_rows, keys.shape[1]), BF16),
            jax.ShapeDtypeStruct((keys.shape[1], key_rows), BF16),
            jax.ShapeDtypeStruct((key_rows, tok), F32),
        ],
        in_specs=[VMEM] * (2 + len(parts)),
        out_specs=[VMEM] * 4,
        compiler_params=params,
        cost_estimate=pl.CostEstimate(
            flops=0, bytes_accessed=LAYOUT_BYTES, transcendentals=0
        ),
        name="layout",
    )(facts, own_keys.T, *parts)
    halves = 2
    n_kv = KEY_VALUE_HEADS // halves
    half = width // halves

    def attention(h, before, up_shapes):
        return pl.pallas_call(
            functools.partial(attention_kernel, by_slot, h * n_kv, n_kv),
            out_shape=[jax.ShapeDtypeStruct((half, tok), BF16)] + up_shapes,
            in_specs=[VMEM] * 4 + [ANY] * 2 + [VMEM] * len(before),
            out_specs=[VMEM] * (1 + len(up_shapes)),
            scratch_shapes=[
                pltpu.VMEM((tok, half), BF16),
                pltpu.VMEM((tok, half), BF16),
                pltpu.SemaphoreType.DMA((n_kv,)),
                pltpu.SemaphoreType.DMA((n_kv,)),
            ],
            compiler_params=params,
            cost_estimate=pl.CostEstimate(
                flops=2 * tok * half * key_rows * 3,
                bytes_accessed=4 * tok * half * 2,
                transcendentals=tok * key_rows * QUERY_HEADS // halves,
            ),
            name="attention_%d" % h,
        )(*laid_out, queries, output_gradient, *before)

    (dq_a,) = attention(0, [], [])
    if by_slot:
        dq_a, w = lax.optimization_barrier((dq_a, w))
        w = jnp.concatenate(w, axis=0)
        up_weight = [w, partnered(w, n_seq, 1)]
    up_shape = jax.ShapeDtypeStruct((n_head, n_groups // n_out, rank, part), BF16)
    dq_b, *up = attention(1, [facts, adapter_activation.T, dq_a], [up_shape] * n_out)

    if by_slot:
        up, up_weight = lax.optimization_barrier((up, up_weight))
    rank_low = pl.pallas_call(
        functools.partial(rank_kernel, by_slot, len(up_weight)),
        out_shape=jax.ShapeDtypeStruct((rank, tok), BF16),
        in_specs=[VMEM] * (3 + len(up_weight)),
        out_specs=VMEM,
        compiler_params=params,
        name="rank_gradient",
    )(facts, *up_weight, dq_a, dq_b)

    down_shape = jax.ShapeDtypeStruct((n_groups // n_out, n_head, rank, x_part), BF16)
    down = pl.pallas_call(
        functools.partial(down_kernel, by_slot),
        out_shape=[down_shape] * n_out,
        in_specs=[VMEM] * 3,
        out_specs=[VMEM] * n_out,
        compiler_params=params,
        cost_estimate=pl.CostEstimate(
            flops=2 * n_groups * rank * tok * inputs.shape[1],
            bytes_accessed=4 * tok * inputs.shape[1] * 2,
            transcendentals=0,
        ),
        name="down_parts",
    )(facts, inputs, rank_low)

    if by_slot:
        down = pl.pallas_call(
            sum_kernel,
            out_shape=[jax.ShapeDtypeStruct(down[0].shape[1:], BF16)] * down[0].shape[0],
            in_specs=[VMEM] * 2,
            out_specs=[VMEM] * down[0].shape[0],
            compiler_params=params,
            cost_estimate=pl.CostEstimate(flops=0, bytes_accessed=SUM_BYTES, transcendentals=0),
            name="core_sum",
        )(down[0], partnered(down[1], n_seq, 1))
        up = over_z(over_cores(up, n_seq), n_head, (1, 2, 3)).astype(BF16)
        up = over_chips(up, n_seq, (1, 2, 3))
        down = over_chips(down, n_seq, (1, 3, 2)).astype(BF16)
        down = over_z(down, n_head, (3, 1, 2))
    else:
        up = lax.all_to_all(up[0], "head", split_axis=0, concat_axis=0, tiled=True)
        up = spread(jnp.sum(up.astype(F32), axis=0), segment_adapter, owner, n_seq)
        down = lax.all_to_all(down[0], "head", split_axis=1, concat_axis=1, tiled=True)
        down = spread(jnp.sum(down.astype(F32), axis=1), segment_adapter, owner, n_seq)
    return down.T[None] * ADAPTER_SCALE, up[None] * ADAPTER_SCALE


def over_cores(parts, n_seq):
    keep, send = parts
    return (keep.astype(F32) + partnered(send, n_seq, 1).astype(F32)).astype(BF16)


def added(own, got):
    total = own.astype(F32)
    for piece in got:
        total = total + piece.astype(F32)
    return total


def over_chips(both, n_seq, order):
    return added(both[0], [partnered(both[m], n_seq, 2 * m) for m in order])


def over_z(both, n_head, order):
    return added(both[0], [across(both[j], n_head, j) for j in order])


def spread(part, segment_adapter, owner, n_seq):
    goes_to = owner[segment_adapter[0]]
    slots = (goes_to[:, None] == jnp.arange(n_seq, dtype=I32)[None, :]).astype(F32)
    slotted = jnp.einsum("srw,so->orw", part, slots, precision=lax.Precision.HIGHEST)
    slotted = lax.all_to_all(slotted.astype(BF16), "seq", split_axis=0, concat_axis=0, tiled=True)
    return jnp.sum(slotted.astype(F32), axis=0)


def solution(mesh):
    return jax.shard_map(
        on_device,
        mesh=mesh,
        in_specs=(
            P(("seq", "head"), None),
            P(("seq", "head"), None),
            P(("seq", "head"), None),
            P(("seq", "head"), None),
            P(("seq", "head"), None),
            P(("seq", "head"), None),
            P("seq", None, "head"),
            P("seq", None),
            P("seq", None),
            P(),
        ),
        out_specs=(P("seq", "head", None), P("seq", None, "head")),
        check_vma=False,
    )
```

```python
import functools
import math

import jax
import jax.numpy as jnp
from jax import lax
from jax.experimental import pallas as pl
from jax.experimental.pallas import tpu as pltpu
from jax.sharding import PartitionSpec as P

QUERY_HEADS = 32
KEY_VALUE_HEADS = 4
HEAD_SIZE = 128
GROUP = QUERY_HEADS // KEY_VALUE_HEADS
ADAPTER_SCALE = 2.0
NEVER = -1e30
LAYOUT_BYTES = 16 * 2**20
SUM_BYTES = 16 * 2**20
BF16 = jnp.bfloat16
F32 = jnp.float32
I32 = jnp.int32
VMEM = pl.BlockSpec(memory_space=pltpu.VMEM)
ANY = pl.BlockSpec(memory_space=pl.ANY)


def dot(a, b, a_dim, b_dim):
    return lax.dot_general(a, b, (((a_dim,), (b_dim,)), ((), ())), preferred_element_type=F32)


def group_rows(rows_of_group, n_groups, width, seq, by_slot):
    row = lax.broadcasted_iota(I32, (n_groups * rows_of_group, width), 0) // rows_of_group
    if by_slot:
        half = n_groups // 2
        row = jnp.where(row < half, row * 2, (row - half) * 2 + 1) ^ seq
    return row


def layout_kernel(n_parts, facts_ref, *refs):
    own_turned, *parts = refs[: n_parts + 1]
    k_all, v_all, k_turned, bias = refs[n_parts + 1 :]
    tok = facts_ref.shape[1]
    kv_width = v_all.shape[1]
    key_rows = v_all.shape[0]
    head = lax.axis_index("head")
    position = head * tok + lax.broadcasted_iota(I32, (1, tok), 1)
    key_position = (
        head * tok - (key_rows - tok) + lax.broadcasted_iota(I32, (key_rows, tok), 0)
    )
    allowed = (key_position >= facts_ref[0:1, :]) & (key_position <= position)
    bias[...] = jnp.where(allowed, 0.0, NEVER)
    for kv in range(KEY_VALUE_HEADS):
        start = 0
        at = slice(kv * HEAD_SIZE, (kv + 1) * HEAD_SIZE)
        for part in parts:
            rows = part.shape[0]
            k_all[start : start + rows, at] = part[:, at]
            v_all[start : start + rows, at] = part[:, kv_width + at.start : kv_width + at.stop]
            start += rows
        k_turned[at, : start - tok] = k_all[: start - tok, at].T
        k_turned[at, start - tok :] = own_turned[at, :]


def attention_kernel(by_slot, first_kv, n_kv, k_all, v_all, k_turned, bias, q_hbm, g_hbm, *refs):
    before, refs = (refs[:3], refs[3:]) if first_kv else ((), refs)
    dq_turned, *up_refs, q_ref, g_ref, q_sem, g_sem = refs
    tok = q_ref.shape[0]
    seq, head = lax.axis_index("seq"), lax.axis_index("head")
    per_kv = GROUP * HEAD_SIZE

    def fetch(kv):
        to = pl.ds(kv * per_kv, per_kv)
        at = pl.ds((first_kv + kv) * per_kv, per_kv)
        return (
            pltpu.make_async_copy(q_hbm.at[:, at], q_ref.at[:, to], q_sem.at[kv]),
            pltpu.make_async_copy(g_hbm.at[:, at], g_ref.at[:, to], g_sem.at[kv]),
        )

    for kv in range(n_kv):
        for copy in fetch(kv):
            copy.start()

    scale = 1.0 / HEAD_SIZE**0.5
    to_log2 = scale * math.log2(math.e)

    def products(kv, i):
        if i == 0:
            for copy in fetch(kv):
                copy.wait()
        at_kv = slice((first_kv + kv) * HEAD_SIZE, (first_kv + kv + 1) * HEAD_SIZE)
        first = (kv * GROUP + i) * HEAD_SIZE
        at = [slice(first + n * HEAD_SIZE, first + (n + 1) * HEAD_SIZE) for n in range(2)]
        q_two = jnp.concatenate([q_ref[:, at[0]], q_ref[:, at[1]]], axis=0)
        g_two = jnp.concatenate([g_ref[:, at[0]], g_ref[:, at[1]]], axis=0)
        s = dot(k_all[:, at_kv], q_two, 1, 1) + jnp.concatenate([bias[...]] * 2, axis=1)
        return at, at_kv, s, dot(v_all[:, at_kv], g_two, 1, 1)

    def softmax(at, at_kv, s, d_prob):
        weights = jnp.exp2((s - jnp.max(s, axis=0, keepdims=True)) * to_log2)
        inverse = 1.0 / jnp.sum(weights, axis=0, keepdims=True)
        delta = jnp.sum(weights * d_prob, axis=0, keepdims=True) * inverse
        return at, at_kv, (weights * (d_prob - delta)).astype(BF16), inverse * scale

    def finish(at, at_kv, dscore, factor):
        dq = dot(k_turned[at_kv, :], dscore, 1, 0) * factor
        dq_turned[at[0], :] = dq[:, :tok].astype(BF16)
        dq_turned[at[1], :] = dq[:, tok:].astype(BF16)

    pairs = [(kv, i) for kv in range(n_kv) for i in range(0, GROUP, 2)]
    ahead, behind = products(*pairs[0]), None
    for n in range(len(pairs)):
        now = ahead
        if n + 1 < len(pairs):
            ahead = products(*pairs[n + 1])
        if behind is not None:
            finish(*behind)
        behind = softmax(*now)
    finish(*behind)
    if not up_refs:
        return

    facts_ref, act_ref, dq_before = before
    rank = act_ref.shape[0]
    n_quarters, per, _, part = up_refs[0].shape
    n_groups = per * len(up_refs)
    own = group_rows(rank, n_groups, tok, seq, by_slot) == facts_ref[2:3, :]
    act = jnp.concatenate([act_ref[...].astype(F32)] * n_groups, axis=0)
    act_cols = jnp.where(own, act, 0.0).astype(BF16)
    n_before = dq_before.shape[0] // part
    for quarter in range(n_quarters):
        i, dq_ref = (quarter, dq_before) if quarter < n_before else (quarter - n_before, dq_turned)
        up = dot(act_cols, dq_ref[i * part : (i + 1) * part, :], 1, 1).astype(BF16)
        j = head ^ quarter if by_slot else quarter
        for n in range(n_groups):
            up_refs[n // per][j, n % per] = up[n * rank : (n + 1) * rank, :]


def rank_kernel(by_slot, n_w, facts_ref, *refs):
    w_refs, (dq_a, dq_b, out_ref) = refs[:n_w], refs[n_w:]
    tok = dq_a.shape[1]
    seq, head = lax.axis_index("seq"), lax.axis_index("head")
    n_adapters, n_quarters, rank, part = w_refs[0].shape
    adapter = facts_ref[1:2, :]
    total = jnp.zeros((rank, tok), F32)
    n_a = dq_a.shape[0] // part
    for c, w_ref in enumerate(w_refs):
        rows = None
        for quarter in range(n_quarters):
            j = lax.rem(head + n_quarters - quarter, n_quarters) if by_slot else quarter
            i, dq_ref = (quarter, dq_a) if quarter < n_a else (quarter - n_a, dq_b)
            dq = dq_ref[i * part : (i + 1) * part, :]
            new = dot(w_ref[:, j].reshape(n_adapters * rank, part), dq, 1, 0)
            rows = new if rows is None else rows + new
        for m in range(n_adapters):
            a = (2 * m + c) ^ seq if by_slot else m
            total = total + jnp.where(adapter == a, rows[m * rank : (m + 1) * rank, :], 0.0)
    out_ref[...] = total.astype(BF16)


def down_kernel(by_slot, facts_ref, x_ref, rank_ref, *out_refs):
    rank, tok = rank_ref.shape
    seq, head = lax.axis_index("seq"), lax.axis_index("head")
    per, n_quarters, _, x_part = out_refs[0].shape
    n_groups = per * len(out_refs)
    own = group_rows(rank, n_groups, tok, seq, by_slot) == facts_ref[2:3, :]
    low = jnp.concatenate([rank_ref[...].astype(F32)] * n_groups, axis=0)
    cols = jnp.where(own, low, 0.0).astype(BF16)
    step = min(512, x_part)
    for j in range(n_quarters):
        quarter = head ^ j if by_slot else j
        for start in range(0, x_part, step):
            at = pl.ds(pl.multiple_of(quarter * x_part + start, step), step)
            down = dot(cols, x_ref[:, at], 1, 0).astype(BF16)
            for n in range(n_groups):
                piece = down[n * rank : (n + 1) * rank, :]
                out_refs[n // per][n % per, j, :, start : start + step] = piece


def sum_kernel(a_ref, b_ref, *out_refs):
    for i, out_ref in enumerate(out_refs):
        out_ref[...] = (a_ref[i].astype(F32) + b_ref[i].astype(F32)).astype(BF16)


def token_facts(tok, lengths, adapters, owner, by_slot):
    n_seg = lengths.shape[0]
    cube = (8, n_seg, n_seg)
    row, at, k = (lax.broadcasted_iota(I32, cube, d) for d in range(3))
    length = jnp.broadcast_to(lengths[None, None, :], cube)
    adapter = jnp.broadcast_to(adapters[None, None, :], cube)
    if by_slot:
        hit = jnp.broadcast_to(adapters[None, :, None], cube) == k
        group = jnp.where(hit, jnp.broadcast_to(owner[None, None, :], cube), 0)
    else:
        group = jnp.where(k == at, k, 0)
    terms = jnp.where(row == 2, group, 0)
    terms = jnp.where((row == 0) & (k < at), length, terms)
    terms = jnp.where((row == 1) & (k == at), adapter, terms)
    terms = jnp.where((row == 3) & (k <= at), length, terms)
    told = jnp.sum(terms, axis=2)
    position = lax.axis_index("head") * tok + jnp.arange(tok, dtype=I32)
    inside = (position >= told[0][:, None]) & (position < told[3][:, None])
    return jnp.sum(jnp.where(inside[None], told[:, :, None], 0), axis=1)


def shifted(x, n_head, j):
    return lax.ppermute(x, "head", [(i, (i + j) % n_head) for i in range(n_head)])


def across(x, n_head, j):
    return lax.ppermute(x, "head", [(i, i ^ j) for i in range(n_head)])


def partnered(x, n_seq, bits):
    return lax.ppermute(x, "seq", [(i, i ^ bits) for i in range(n_seq)])


def on_device(
    queries, keys, values, output_gradient, inputs, adapter_activation,
    adapter_up_weight, segment_length, segment_adapter, owner,
):
    n_head = lax.axis_size("head")
    n_seq = lax.axis_size("seq")
    tok, width = queries.shape
    pack = tok * n_head
    rank = adapter_up_weight.shape[1]
    n_adapters = owner.shape[0]
    n_seg = segment_length.shape[1]
    by_slot = n_adapters == n_seq == n_seg == 8 and n_head == 4

    reach = []
    while sum(reach) < pack * 3 // 8:
        reach.append(min(pack * 3 // 8 - sum(reach), tok))
    key_rows = tok + sum(reach)
    own = jnp.concatenate([keys, values], axis=1)
    parts = [own]
    for hop, rows in enumerate(reach, 1):
        shift = [(i, i + hop) for i in range(n_head - hop)]
        parts.insert(0, lax.ppermute(own[tok - rows :], "head", shift))

    if by_slot:
        w = [adapter_up_weight] + [shifted(adapter_up_weight, n_head, j) for j in range(1, n_head)]
        w = jnp.concatenate(w, axis=0)[None]
        lengths, own_keys, _ = lax.optimization_barrier((segment_length, keys, w))
        w = [w] + [partnered(w, n_seq, 2 * m) for m in range(1, n_seq // 2)]
    else:
        lengths, own_keys = segment_length, keys
        w = lax.all_gather(adapter_up_weight, "seq", axis=0, tiled=True)
        up_weight = [lax.all_gather(w, "head", axis=1, tiled=False)]

    facts = token_facts(tok, lengths[0], segment_adapter[0], owner, by_slot)
    n_out = 2 if by_slot else 1
    n_groups = n_seq if by_slot else n_seg
    part = width // n_head
    x_part = inputs.shape[1] // n_head
    params = pltpu.CompilerParams(vmem_limit_bytes=32 * 2**20)

    laid_out = pl.pallas_call(
        functools.partial(layout_kernel, len(parts)),
        out_shape=[
            jax.ShapeDtypeStruct((key_rows, keys.shape[1]), BF16),
            jax.ShapeDtypeStruct((key_rows, keys.shape[1]), BF16),
            jax.ShapeDtypeStruct((keys.shape[1], key_rows), BF16),
            jax.ShapeDtypeStruct((key_rows, tok), F32),
        ],
        in_specs=[VMEM] * (2 + len(parts)),
        out_specs=[VMEM] * 4,
        compiler_params=params,
        cost_estimate=pl.CostEstimate(
            flops=0, bytes_accessed=LAYOUT_BYTES, transcendentals=0
        ),
        name="layout",
    )(facts, own_keys.T, *parts)
    halves = 2
    n_kv = KEY_VALUE_HEADS // halves
    half = width // halves

    def attention(h, before, up_shapes):
        return pl.pallas_call(
            functools.partial(attention_kernel, by_slot, h * n_kv, n_kv),
            out_shape=[jax.ShapeDtypeStruct((half, tok), BF16)] + up_shapes,
            in_specs=[VMEM] * 4 + [ANY] * 2 + [VMEM] * len(before),
            out_specs=[VMEM] * (1 + len(up_shapes)),
            scratch_shapes=[
                pltpu.VMEM((tok, half), BF16),
                pltpu.VMEM((tok, half), BF16),
                pltpu.SemaphoreType.DMA((n_kv,)),
                pltpu.SemaphoreType.DMA((n_kv,)),
            ],
            compiler_params=params,
            cost_estimate=pl.CostEstimate(
                flops=2 * tok * half * key_rows * 3,
                bytes_accessed=4 * tok * half * 2,
                transcendentals=tok * key_rows * QUERY_HEADS // halves,
            ),
            name="attention_%d" % h,
        )(*laid_out, queries, output_gradient, *before)

    (dq_a,) = attention(0, [], [])
    if by_slot:
        dq_a, w = lax.optimization_barrier((dq_a, w))
        w = jnp.concatenate(w, axis=0)
        up_weight = [w, partnered(w, n_seq, 1)]
    up_shape = jax.ShapeDtypeStruct((n_head, n_groups // n_out, rank, part), BF16)
    dq_b, *up = attention(1, [facts, adapter_activation.T, dq_a], [up_shape] * n_out)

    if by_slot:
        up, up_weight = lax.optimization_barrier((up, up_weight))
    rank_low = pl.pallas_call(
        functools.partial(rank_kernel, by_slot, len(up_weight)),
        out_shape=jax.ShapeDtypeStruct((rank, tok), BF16),
        in_specs=[VMEM] * (3 + len(up_weight)),
        out_specs=VMEM,
        compiler_params=params,
        name="rank_gradient",
    )(facts, *up_weight, dq_a, dq_b)

    down_shape = jax.ShapeDtypeStruct((n_groups // n_out, n_head, rank, x_part), BF16)
    down = pl.pallas_call(
        functools.partial(down_kernel, by_slot),
        out_shape=[down_shape] * n_out,
        in_specs=[VMEM] * 3,
        out_specs=[VMEM] * n_out,
        compiler_params=params,
        cost_estimate=pl.CostEstimate(
            flops=2 * n_groups * rank * tok * inputs.shape[1],
            bytes_accessed=4 * tok * inputs.shape[1] * 2,
            transcendentals=0,
        ),
        name="down_parts",
    )(facts, inputs, rank_low)

    if by_slot:
        down = pl.pallas_call(
            sum_kernel,
            out_shape=[jax.ShapeDtypeStruct(down[0].shape[1:], BF16)] * down[0].shape[0],
            in_specs=[VMEM] * 2,
            out_specs=[VMEM] * down[0].shape[0],
            compiler_params=params,
            cost_estimate=pl.CostEstimate(flops=0, bytes_accessed=SUM_BYTES, transcendentals=0),
            name="core_sum",
        )(down[0], partnered(down[1], n_seq, 1))
        up = over_z(over_cores(up, n_seq), n_head, (1, 2, 3)).astype(BF16)
        down = over_z(over_chips(down, n_seq).astype(BF16), n_head, (3, 1, 2))
        up_got = [partnered(up[m], n_seq, 2 * m) for m in range(1, n_seq // 2)]
        up_got, _ = lax.optimization_barrier((up_got, down))
        up = added(up[0], up_got)
    else:
        up = lax.all_to_all(up[0], "head", split_axis=0, concat_axis=0, tiled=True)
        up = spread(jnp.sum(up.astype(F32), axis=0), segment_adapter, owner, n_seq)
        down = lax.all_to_all(down[0], "head", split_axis=1, concat_axis=1, tiled=True)
        down = spread(jnp.sum(down.astype(F32), axis=1), segment_adapter, owner, n_seq)
    return down.T[None] * ADAPTER_SCALE, up[None] * ADAPTER_SCALE


def over_cores(parts, n_seq):
    keep, send = parts
    return (keep.astype(F32) + partnered(send, n_seq, 1).astype(F32)).astype(BF16)


def added(own, got):
    total = own.astype(F32)
    for piece in got:
        total = total + piece.astype(F32)
    return total


def over_chips(both, n_seq):
    return added(both[0], [partnered(both[m], n_seq, 2 * m) for m in range(1, n_seq // 2)])


def over_z(both, n_head, order):
    return added(both[0], [across(both[j], n_head, j) for j in order])


def spread(part, segment_adapter, owner, n_seq):
    goes_to = owner[segment_adapter[0]]
    slots = (goes_to[:, None] == jnp.arange(n_seq, dtype=I32)[None, :]).astype(F32)
    slotted = jnp.einsum("srw,so->orw", part, slots, precision=lax.Precision.HIGHEST)
    slotted = lax.all_to_all(slotted.astype(BF16), "seq", split_axis=0, concat_axis=0, tiled=True)
    return jnp.sum(slotted.astype(F32), axis=0)


def solution(mesh):
    return jax.shard_map(
        on_device,
        mesh=mesh,
        in_specs=(
            P(("seq", "head"), None),
            P(("seq", "head"), None),
            P(("seq", "head"), None),
            P(("seq", "head"), None),
            P(("seq", "head"), None),
            P(("seq", "head"), None),
            P("seq", None, "head"),
            P("seq", None),
            P("seq", None),
            P(),
        ),
        out_specs=(P("seq", "head", None), P("seq", None, "head")),
        check_vma=False,
    )
```

```python
import functools
import math

import jax
import jax.numpy as jnp
from jax import lax
from jax.experimental import pallas as pl
from jax.experimental.pallas import tpu as pltpu
from jax.sharding import PartitionSpec as P

QUERY_HEADS = 32
KEY_VALUE_HEADS = 4
HEAD_SIZE = 128
GROUP = QUERY_HEADS // KEY_VALUE_HEADS
ADAPTER_SCALE = 2.0
NEVER = -1e30
LAYOUT_BYTES = 16 * 2**20
SUM_BYTES = 16 * 2**20
BF16 = jnp.bfloat16
F32 = jnp.float32
I32 = jnp.int32
VMEM = pl.BlockSpec(memory_space=pltpu.VMEM)


def dot(a, b, a_dim, b_dim):
    return lax.dot_general(a, b, (((a_dim,), (b_dim,)), ((), ())), preferred_element_type=F32)


def group_rows(rows_of_group, n_groups, width, seq, by_slot):
    row = lax.broadcasted_iota(I32, (n_groups * rows_of_group, width), 0) // rows_of_group
    if by_slot:
        half = n_groups // 2
        row = jnp.where(row < half, row * 2, (row - half) * 2 + 1) ^ seq
    return row


def layout_kernel(n_parts, facts_ref, *refs):
    own_turned, *parts = refs[: n_parts + 1]
    k_all, v_all, k_turned, bias = refs[n_parts + 1 :]
    tok = facts_ref.shape[1]
    kv_width = v_all.shape[1]
    key_rows = v_all.shape[0]
    head = lax.axis_index("head")
    position = head * tok + lax.broadcasted_iota(I32, (1, tok), 1)
    key_position = (
        head * tok - (key_rows - tok) + lax.broadcasted_iota(I32, (key_rows, tok), 0)
    )
    allowed = (key_position >= facts_ref[0:1, :]) & (key_position <= position)
    bias[...] = jnp.where(allowed, 0.0, NEVER)
    for kv in range(KEY_VALUE_HEADS):
        start = 0
        at = slice(kv * HEAD_SIZE, (kv + 1) * HEAD_SIZE)
        for part in parts:
            rows = part.shape[0]
            k_all[start : start + rows, at] = part[:, at]
            v_all[start : start + rows, at] = part[:, kv_width + at.start : kv_width + at.stop]
            start += rows
        k_turned[at, : start - tok] = k_all[: start - tok, at].T
        k_turned[at, start - tok :] = own_turned[at, :]


def attention_kernel(by_slot, first_kv, n_kv, k_all, v_all, k_turned, bias, q_ref, g_ref, *refs):
    before, refs = (refs[:3], refs[3:]) if first_kv else ((), refs)
    dq_turned, *up_refs = refs
    tok = q_ref.shape[0]
    seq, head = lax.axis_index("seq"), lax.axis_index("head")

    scale = 1.0 / HEAD_SIZE**0.5
    to_log2 = scale * math.log2(math.e)

    def products(kv, i):
        at_kv = slice((first_kv + kv) * HEAD_SIZE, (first_kv + kv + 1) * HEAD_SIZE)
        first = (kv * GROUP + i) * HEAD_SIZE
        at = [slice(first + n * HEAD_SIZE, first + (n + 1) * HEAD_SIZE) for n in range(2)]
        skip = first_kv * GROUP * HEAD_SIZE
        wide = [slice(skip + a.start, skip + a.stop) for a in at]
        q_two = jnp.concatenate([q_ref[:, wide[0]], q_ref[:, wide[1]]], axis=0)
        g_two = jnp.concatenate([g_ref[:, wide[0]], g_ref[:, wide[1]]], axis=0)
        s = dot(k_all[:, at_kv], q_two, 1, 1) + jnp.concatenate([bias[...]] * 2, axis=1)
        return at, at_kv, s, dot(v_all[:, at_kv], g_two, 1, 1)

    def softmax(at, at_kv, s, d_prob):
        weights = jnp.exp2((s - jnp.max(s, axis=0, keepdims=True)) * to_log2)
        inverse = 1.0 / jnp.sum(weights, axis=0, keepdims=True)
        delta = jnp.sum(weights * d_prob, axis=0, keepdims=True) * inverse
        return at, at_kv, (weights * (d_prob - delta)).astype(BF16), inverse * scale

    def finish(at, at_kv, dscore, factor):
        dq = dot(k_turned[at_kv, :], dscore, 1, 0) * factor
        dq_turned[at[0], :] = dq[:, :tok].astype(BF16)
        dq_turned[at[1], :] = dq[:, tok:].astype(BF16)

    pairs = [(kv, i) for kv in range(n_kv) for i in range(0, GROUP, 2)]
    ahead, behind = products(*pairs[0]), None
    for n in range(len(pairs)):
        now = ahead
        if n + 1 < len(pairs):
            ahead = products(*pairs[n + 1])
        if behind is not None:
            finish(*behind)
        behind = softmax(*now)
    finish(*behind)
    if not up_refs:
        return

    facts_ref, act_ref, dq_before = before
    rank = act_ref.shape[0]
    n_quarters, per, _, part = up_refs[0].shape
    n_groups = per * len(up_refs)
    own = group_rows(rank, n_groups, tok, seq, by_slot) == facts_ref[2:3, :]
    act = jnp.concatenate([act_ref[...].astype(F32)] * n_groups, axis=0)
    act_cols = jnp.where(own, act, 0.0).astype(BF16)
    n_before = dq_before.shape[0] // part
    for quarter in range(n_quarters):
        i, dq_ref = (quarter, dq_before) if quarter < n_before else (quarter - n_before, dq_turned)
        up = dot(act_cols, dq_ref[i * part : (i + 1) * part, :], 1, 1).astype(BF16)
        j = head ^ quarter if by_slot else quarter
        for n in range(n_groups):
            up_refs[n // per][j, n % per] = up[n * rank : (n + 1) * rank, :]


def rank_kernel(by_slot, n_w, facts_ref, *refs):
    w_refs, (dq_a, dq_b, out_ref) = refs[:n_w], refs[n_w:]
    tok = dq_a.shape[1]
    seq, head = lax.axis_index("seq"), lax.axis_index("head")
    n_adapters, n_quarters, rank, part = w_refs[0].shape
    adapter = facts_ref[1:2, :]
    total = jnp.zeros((rank, tok), F32)
    n_a = dq_a.shape[0] // part
    for c, w_ref in enumerate(w_refs):
        rows = None
        for quarter in range(n_quarters):
            j = lax.rem(head + n_quarters - quarter, n_quarters) if by_slot else quarter
            i, dq_ref = (quarter, dq_a) if quarter < n_a else (quarter - n_a, dq_b)
            dq = dq_ref[i * part : (i + 1) * part, :]
            new = dot(w_ref[:, j].reshape(n_adapters * rank, part), dq, 1, 0)
            rows = new if rows is None else rows + new
        for m in range(n_adapters):
            a = (2 * m + c) ^ seq if by_slot else m
            total = total + jnp.where(adapter == a, rows[m * rank : (m + 1) * rank, :], 0.0)
    out_ref[...] = total.astype(BF16)


def down_kernel(by_slot, facts_ref, x_ref, rank_ref, *out_refs):
    rank, tok = rank_ref.shape
    seq, head = lax.axis_index("seq"), lax.axis_index("head")
    per, n_quarters, _, x_part = out_refs[0].shape
    n_groups = per * len(out_refs)
    own = group_rows(rank, n_groups, tok, seq, by_slot) == facts_ref[2:3, :]
    low = jnp.concatenate([rank_ref[...].astype(F32)] * n_groups, axis=0)
    cols = jnp.where(own, low, 0.0).astype(BF16)
    step = min(512, x_part)
    for j in range(n_quarters):
        quarter = head ^ j if by_slot else j
        for start in range(0, x_part, step):
            at = pl.ds(pl.multiple_of(quarter * x_part + start, step), step)
            down = dot(cols, x_ref[:, at], 1, 0).astype(BF16)
            for n in range(n_groups):
                piece = down[n * rank : (n + 1) * rank, :]
                out_refs[n // per][n % per, j, :, start : start + step] = piece


def sum_kernel(a_ref, b_ref, *out_refs):
    for i, out_ref in enumerate(out_refs):
        out_ref[...] = (a_ref[i].astype(F32) + b_ref[i].astype(F32)).astype(BF16)


def token_facts(tok, lengths, adapters, owner, by_slot):
    n_seg = lengths.shape[0]
    cube = (8, n_seg, n_seg)
    row, at, k = (lax.broadcasted_iota(I32, cube, d) for d in range(3))
    length = jnp.broadcast_to(lengths[None, None, :], cube)
    adapter = jnp.broadcast_to(adapters[None, None, :], cube)
    if by_slot:
        hit = jnp.broadcast_to(adapters[None, :, None], cube) == k
        group = jnp.where(hit, jnp.broadcast_to(owner[None, None, :], cube), 0)
    else:
        group = jnp.where(k == at, k, 0)
    terms = jnp.where(row == 2, group, 0)
    terms = jnp.where((row == 0) & (k < at), length, terms)
    terms = jnp.where((row == 1) & (k == at), adapter, terms)
    terms = jnp.where((row == 3) & (k <= at), length, terms)
    told = jnp.sum(terms, axis=2)
    position = lax.axis_index("head") * tok + jnp.arange(tok, dtype=I32)
    inside = (position >= told[0][:, None]) & (position < told[3][:, None])
    return jnp.sum(jnp.where(inside[None], told[:, :, None], 0), axis=1)


def shifted(x, n_head, j):
    return lax.ppermute(x, "head", [(i, (i + j) % n_head) for i in range(n_head)])


def across(x, n_head, j):
    return lax.ppermute(x, "head", [(i, i ^ j) for i in range(n_head)])


def partnered(x, n_seq, bits):
    return lax.ppermute(x, "seq", [(i, i ^ bits) for i in range(n_seq)])


def on_device(
    queries, keys, values, output_gradient, inputs, adapter_activation,
    adapter_up_weight, segment_length, segment_adapter, owner,
):
    n_head = lax.axis_size("head")
    n_seq = lax.axis_size("seq")
    tok, width = queries.shape
    pack = tok * n_head
    rank = adapter_up_weight.shape[1]
    n_adapters = owner.shape[0]
    n_seg = segment_length.shape[1]
    by_slot = n_adapters == n_seq == n_seg == 8 and n_head == 4

    reach = []
    while sum(reach) < pack * 3 // 8:
        reach.append(min(pack * 3 // 8 - sum(reach), tok))
    key_rows = tok + sum(reach)
    own = jnp.concatenate([keys, values], axis=1)
    parts = [own]
    for hop, rows in enumerate(reach, 1):
        shift = [(i, i + hop) for i in range(n_head - hop)]
        parts.insert(0, lax.ppermute(own[tok - rows :], "head", shift))

    if by_slot:
        w = [adapter_up_weight] + [shifted(adapter_up_weight, n_head, j) for j in range(1, n_head)]
        w = jnp.concatenate(w, axis=0)[None]
        lengths, own_keys, _ = lax.optimization_barrier((segment_length, keys, w))
        w = [w] + [partnered(w, n_seq, 2 * m) for m in range(1, n_seq // 2)]
    else:
        lengths, own_keys = segment_length, keys
        w = lax.all_gather(adapter_up_weight, "seq", axis=0, tiled=True)
        up_weight = [lax.all_gather(w, "head", axis=1, tiled=False)]

    facts = token_facts(tok, lengths[0], segment_adapter[0], owner, by_slot)
    n_out = 2 if by_slot else 1
    n_groups = n_seq if by_slot else n_seg
    part = width // n_head
    x_part = inputs.shape[1] // n_head
    params = pltpu.CompilerParams(vmem_limit_bytes=32 * 2**20)

    laid_out = pl.pallas_call(
        functools.partial(layout_kernel, len(parts)),
        out_shape=[
            jax.ShapeDtypeStruct((key_rows, keys.shape[1]), BF16),
            jax.ShapeDtypeStruct((key_rows, keys.shape[1]), BF16),
            jax.ShapeDtypeStruct((keys.shape[1], key_rows), BF16),
            jax.ShapeDtypeStruct((key_rows, tok), F32),
        ],
        in_specs=[VMEM] * (2 + len(parts)),
        out_specs=[VMEM] * 4,
        compiler_params=params,
        cost_estimate=pl.CostEstimate(
            flops=0, bytes_accessed=LAYOUT_BYTES, transcendentals=0
        ),
        name="layout",
    )(facts, own_keys.T, *parts)
    halves = 2
    n_kv = KEY_VALUE_HEADS // halves
    half = width // halves

    def attention(h, before, up_shapes):
        return pl.pallas_call(
            functools.partial(attention_kernel, by_slot, h * n_kv, n_kv),
            out_shape=[jax.ShapeDtypeStruct((half, tok), BF16)] + up_shapes,
            in_specs=[VMEM] * (6 + len(before)),
            out_specs=[VMEM] * (1 + len(up_shapes)),
            compiler_params=params,
            cost_estimate=pl.CostEstimate(
                flops=2 * tok * half * key_rows * 3,
                bytes_accessed=4 * tok * half * 2,
                transcendentals=tok * key_rows * QUERY_HEADS // halves,
            ),
            name="attention_%d" % h,
        )(*laid_out, queries, output_gradient, *before)

    (dq_a,) = attention(0, [], [])
    if by_slot:
        dq_a, w = lax.optimization_barrier((dq_a, w))
        w = jnp.concatenate(w, axis=0)
        up_weight = [w, partnered(w, n_seq, 1)]
    up_shape = jax.ShapeDtypeStruct((n_head, n_groups // n_out, rank, part), BF16)
    dq_b, *up = attention(1, [facts, adapter_activation.T, dq_a], [up_shape] * n_out)

    if by_slot:
        up, up_weight = lax.optimization_barrier((up, up_weight))
    rank_low = pl.pallas_call(
        functools.partial(rank_kernel, by_slot, len(up_weight)),
        out_shape=jax.ShapeDtypeStruct((rank, tok), BF16),
        in_specs=[VMEM] * (3 + len(up_weight)),
        out_specs=VMEM,
        compiler_params=params,
        name="rank_gradient",
    )(facts, *up_weight, dq_a, dq_b)

    down_shape = jax.ShapeDtypeStruct((n_groups // n_out, n_head, rank, x_part), BF16)
    down = pl.pallas_call(
        functools.partial(down_kernel, by_slot),
        out_shape=[down_shape] * n_out,
        in_specs=[VMEM] * 3,
        out_specs=[VMEM] * n_out,
        compiler_params=params,
        cost_estimate=pl.CostEstimate(
            flops=2 * n_groups * rank * tok * inputs.shape[1],
            bytes_accessed=4 * tok * inputs.shape[1] * 2,
            transcendentals=0,
        ),
        name="down_parts",
    )(facts, inputs, rank_low)

    if by_slot:
        down = pl.pallas_call(
            sum_kernel,
            out_shape=[jax.ShapeDtypeStruct(down[0].shape[1:], BF16)] * down[0].shape[0],
            in_specs=[VMEM] * 2,
            out_specs=[VMEM] * down[0].shape[0],
            compiler_params=params,
            cost_estimate=pl.CostEstimate(flops=0, bytes_accessed=SUM_BYTES, transcendentals=0),
            name="core_sum",
        )(down[0], partnered(down[1], n_seq, 1))
        up = over_chips(over_z(over_cores(up, n_seq), n_head, (1, 2, 3)).astype(BF16), n_seq)
        down = over_z(over_chips(down, n_seq).astype(BF16), n_head, (3, 1, 2))
    else:
        up = lax.all_to_all(up[0], "head", split_axis=0, concat_axis=0, tiled=True)
        up = spread(jnp.sum(up.astype(F32), axis=0), segment_adapter, owner, n_seq)
        down = lax.all_to_all(down[0], "head", split_axis=1, concat_axis=1, tiled=True)
        down = spread(jnp.sum(down.astype(F32), axis=1), segment_adapter, owner, n_seq)
    return down.T[None] * ADAPTER_SCALE, up[None] * ADAPTER_SCALE


def over_cores(parts, n_seq):
    keep, send = parts
    return (keep.astype(F32) + partnered(send, n_seq, 1).astype(F32)).astype(BF16)


def added(own, got):
    total = own.astype(F32)
    for piece in got:
        total = total + piece.astype(F32)
    return total


def over_chips(both, n_seq):
    return added(both[0], [partnered(both[m], n_seq, 2 * m) for m in range(1, n_seq // 2)])


def over_z(both, n_head, order):
    return added(both[0], [across(both[j], n_head, j) for j in order])


def spread(part, segment_adapter, owner, n_seq):
    goes_to = owner[segment_adapter[0]]
    slots = (goes_to[:, None] == jnp.arange(n_seq, dtype=I32)[None, :]).astype(F32)
    slotted = jnp.einsum("srw,so->orw", part, slots, precision=lax.Precision.HIGHEST)
    slotted = lax.all_to_all(slotted.astype(BF16), "seq", split_axis=0, concat_axis=0, tiled=True)
    return jnp.sum(slotted.astype(F32), axis=0)


def solution(mesh):
    return jax.shard_map(
        on_device,
        mesh=mesh,
        in_specs=(
            P(("seq", "head"), None),
            P(("seq", "head"), None),
            P(("seq", "head"), None),
            P(("seq", "head"), None),
            P(("seq", "head"), None),
            P(("seq", "head"), None),
            P("seq", None, "head"),
            P("seq", None),
            P("seq", None),
            P(),
        ),
        out_specs=(P("seq", "head", None), P("seq", None, "head")),
        check_vma=False,
    )
```
